512 devices in a mesh: node: 32 (over z, x_lo), local: 16 (over y, x_hi, core).
Axes of the slice: x: 4 (x_hi: 2, x_lo: 2; x = x_hi * 2 + x_lo), y: 4, z: 16, core: 2. Of those that a mesh axis runs over, the one named last changes fastest.
Arguments:
- tokens: bfloat16 [131072, 4096], P(('node', 'local')), may hold values from -6 to 6
- gain: float32 [4096], replicated, may hold values from 0.1 to 1.9
- w_codes: bfloat16 [4, 4096, 128], P(None, ('node', 'local')), may hold values from -1 to 1
- w_scales: bfloat16 [4, 4096], P(None, ('node', 'local')), may hold values from 0.0099487305 to 0.049804688
- seq_counts: int32 [512], P(('node', 'local')), may hold values from 1 to 4, as said below
- key_grad: bfloat16 [131072, 512], P(('node', 'local')), may hold values from -6 to 6
Outputs:
- keys: bfloat16 [131072, 512], P(('node', 'local'))
- token_input_grad: bfloat16 [131072, 4096], P(('node', 'local'))
- weight_grad: float32 [4096, 512], P(('node', 'local'))
- gain_grad: float32 [4096], replicated
The draws below stay inside these ranges and needn't reach their ends.
Inputs may be any that keep to these rules, and one draw needn't show every extreme that they name: `seq_counts`: some device has exactly 4 live sequences.
All inputs are finite; a program needn't handle non-finite values. Where the reference program divides by a largest or mean magnitude, that divisor is 1e-20 or more.
Results may differ from the reference program's by a relative error of at most 0.012.
Values may be sent and summed in bfloat16 or wider, within the bound.
A program may use at most 192 MiB of HBM per device.

```python
import math
import jax
import jax.numpy as jnp
from jax import lax

D = 4096
BLOCK = 128
SEQ_LEN = 64
SEQ_CAP = 4
KV = 512
ROWS = 256
DEVICES_ALL = 512
TOKENS = 131072


def draw_seq_counts(key, part):
    key = jax.random.fold_in(key, 11)
    first, second = jax.random.split(key)
    counts = jax.random.randint(first, (DEVICES_ALL,), 1, 3).astype(jnp.int32)
    chosen = jax.random.randint(second, (), 0, DEVICES_ALL)
    places = jnp.arange(DEVICES_ALL, dtype=jnp.int32)
    return jnp.where(places == chosen, jnp.int32(SEQ_CAP), counts).astype(jnp.int32)


def level_of(rng, shape, cuts, least, high):
    def one(position, parts):
        heights = jax.random.uniform(jax.random.fold_in(jax.random.fold_in(rng, 6), position), (parts,), jnp.float32, least / len(cuts), high / len(cuts))
        return jnp.repeat(jnp.exp(heights), shape[position] // parts).reshape((-1,) + (1,) * (len(shape) - position - 1))

    loudness = one(*cuts[0])
    for cut in cuts[1:]:
        loudness = loudness * one(*cut)
    return loudness


def scatter_about(own_key, extent, width, bound, cuts=(), kind=jnp.bfloat16):
    level = level_of(own_key, extent, cuts, -0.22, 0.18) if cuts else 1.0
    array = jax.random.normal(own_key, extent, jnp.float32) * width * level
    return jnp.minimum(jnp.maximum(array, -bound), bound).astype(kind)


def setup_inputs(seed: int = 0) -> dict:
    splits = jax.random.split(jax.random.key(seed), 7)
    return {
        "tokens": scatter_about(splits[0], (TOKENS, D), 1.0, 6.0, ((0, 512),)),
        "gain": jnp.clip(1.0 + 0.18 * jax.random.normal(splits[1], (D,), jnp.float32), 0.1, 1.9),
        "w_codes": jnp.clip(jax.random.uniform(splits[2], (KV // BLOCK, D, BLOCK), jnp.float32, -1.0, 1.0) * level_of(splits[2], (KV // BLOCK, D, BLOCK), ((1, 512),), -0.4, 0.0), -1.0, 1.0).astype(jnp.bfloat16),
        "w_scales": jnp.clip(jnp.exp(math.log(0.049804688) - 1.61066415 * jax.random.uniform(splits[3], (KV // BLOCK, D), jnp.float32) ** level_of(splits[3], (KV // BLOCK, D), ((1, 512),), -0.2, 0.2)), 0.0099487305, 0.049804688).astype(jnp.bfloat16),
        "seq_counts": draw_seq_counts(jax.random.fold_in(splits[6], 71), 0),
        "key_grad": scatter_about(splits[5], (TOKENS, KV), 1.0, 6.0, ((0, 512),)),
    }


def build_weight(codes, scales):
    pieces = [(codes[c].astype(jnp.float32) * scales[c].astype(jnp.float32)[:, None]).astype(jnp.bfloat16) for c in range(codes.shape[0])]
    return jnp.concatenate(pieces, axis=1)

def restore_grad(part):
    pieces = []
    for c in range(KV // BLOCK):
        block_part = part[:, c * BLOCK:(c + 1) * BLOCK]
        scale_row = (lax.optimization_barrier(jnp.max(jnp.abs(block_part), axis=1)) + 1e-06).astype(jnp.bfloat16)
        code_part = (block_part / scale_row.astype(jnp.float32)[:, None]).astype(jnp.bfloat16)
        code_part = lax.optimization_barrier(code_part)
        pieces.append(code_part.astype(jnp.float32) * scale_row.astype(jnp.float32)[:, None])
    return jnp.concatenate(pieces, axis=1)

def reference(tokens, gain, w_codes, w_scales, seq_counts, key_grad):
    weight = build_weight(w_codes, w_scales)
    devices = seq_counts.shape[0]
    token_blocks = tokens.reshape(devices, ROWS, D)
    grad_blocks = key_grad.reshape(devices, ROWS, KV)
    inverse = 1.0 / math.sqrt(TOKENS)

    def one_device(carry, item):
        block, upstream, count = item
        slots = (jnp.arange(ROWS, dtype=jnp.int32) // SEQ_LEN).astype(jnp.int32)
        live = (slots < count)[:, None]
        input_float = block.astype(jnp.float32)
        inverse_root_mean = lax.rsqrt(lax.optimization_barrier(jnp.mean(input_float * input_float, axis=-1, keepdims=True)) + 1e-05)
        input_normalized = input_float * inverse_root_mean
        normalized_rows = (input_normalized * gain).astype(jnp.bfloat16)
        keys = jnp.where(live, jnp.dot(normalized_rows, weight, preferred_element_type=jnp.float32), 0.0).astype(jnp.bfloat16)
        masked = jnp.where(live, upstream, jnp.zeros_like(upstream))
        normalized_grad = jnp.dot(masked, weight.T, preferred_element_type=jnp.float32)
        scaled_grad = normalized_grad * gain
        input_grad_rows = inverse_root_mean * (scaled_grad - input_normalized * lax.optimization_barrier(jnp.mean(scaled_grad * input_normalized, axis=-1, keepdims=True)))
        gain_partial_sum = lax.optimization_barrier(jnp.sum(normalized_grad * input_normalized, axis=0))
        part = jnp.dot(normalized_rows.T, masked, preferred_element_type=jnp.float32)
        restored = restore_grad(part)
        return ((carry[0] + restored, carry[1] + gain_partial_sum), (keys, input_grad_rows.astype(jnp.bfloat16)))
    start = (jnp.zeros((D, KV), jnp.float32), jnp.zeros((D,), jnp.float32))
    (total, gain_grad_total), (keys, grads) = lax.scan(one_device, start, (token_blocks, grad_blocks, seq_counts))
    return (keys.reshape(TOKENS, KV), grads.reshape(TOKENS, D), total * inverse, gain_grad_total * inverse)
```

```python
import functools
import math

import jax
import jax.numpy as jnp
from jax import lax
from jax.experimental import pallas as pl
from jax.experimental.pallas import tpu as pltpu
from jax.sharding import PartitionSpec as P

SEQ_LEN = 64
HALF = 256
TILE = 512
MESH = pl.DeviceIdType.MESH
F32 = jnp.float32
BF16 = jnp.bfloat16


def kernel(
    Z, inverse,
    cnt, tok, kg, wsh, g16,
    keys, tig, wg, gg,
    W, M, G, GR, W16, wrecv,
    yA, yB, yL, yR, S2, xA, xB, xL, xR, S3, zr, S4, wgr,
    qs, qz, qy, qyr, qx, qxr, qc, qcr,
    ag_s, ag_r, gz_s, gz_r, rz_s, rz_r, qz_s, qz_r, cr_s, cr_r, ms_s, ms_r,
):
    D = tok.shape[1]
    tiles = D // TILE
    zt = Z // tiles
    hz = Z // 2
    node = lax.axis_index("node")
    loc = lax.axis_index("local")
    z, xlo = node // 2, node % 2
    y, xhi, c = loc // 4, (loc // 2) % 2, loc % 2
    x = 2 * xhi + xlo
    sib = 1 - c

    def at_z(o):
        return (((z + o) % Z) * 2 + xlo, loc)

    def at_y(o):
        return (node, ((y + o) % 4) * 4 + xhi * 2 + c)

    def at_x(o):
        xx = (x + o) % 4
        return (z * 2 + xx % 2, y * 4 + (xx // 2) * 2 + c)

    at_core = (node, y * 4 + xhi * 2 + sib)

    def copy(src, dst, ss, rs_, dev):
        return pltpu.make_async_remote_copy(
            src_ref=src, dst_ref=dst, send_sem=ss, recv_sem=rs_,
            device_id=dev, device_id_type=MESH,
        )

    yp, ym, yo = (y + 1) % 4, (y + 3) % 4, (y + 2) % 4
    xs = [((x + o) % 4) % 2 for o in range(4)]
    xh = [((x + o) % 4) // 2 for o in range(4)]
    zA, zB = pl.ds(0, hz), pl.ds(hz, hz)

    barrier = pltpu.get_barrier_semaphore()

    def hello(o, carry):
        pl.semaphore_signal(barrier, inc=1, device_id=at_z(o), device_id_type=MESH)
        return carry

    lax.fori_loop(1, Z, hello, 0)
    for o in (1, 2, 3):
        pl.semaphore_signal(barrier, inc=1, device_id=at_y(o), device_id_type=MESH)
        pl.semaphore_signal(barrier, inc=1, device_id=at_x(o), device_id_type=MESH)
    pl.semaphore_signal(barrier, inc=1, device_id=at_core, device_id_type=MESH)

    def square(k, acc):
        t = tok[:, pl.ds(pl.multiple_of(k * TILE, TILE), TILE)].astype(F32)
        return acc + jnp.sum(t * t, axis=1, keepdims=True)

    total = lax.fori_loop(0, tiles, square, jnp.zeros((tok.shape[0], 1), F32))
    rs = lax.rsqrt(total / D + 1e-05)
    live = lax.broadcasted_iota(jnp.int32, (tok.shape[0], 1), 0) // SEQ_LEN < cnt[0]
    for h in range(2):
        m = jnp.where(live, kg[:, h * HALF:(h + 1) * HALF].astype(F32), 0.0)
        M[h] = (m * rs).astype(BF16)

    pl.semaphore_wait(barrier, Z - 1 + 7)

    wx = copy(wsh.at[sib], wrecv, ms_s.at[0], ms_r.at[0], at_core)
    wx.start()
    wx.wait()
    own, other = wsh[c], wrecv[...]
    W16[0:8, :] = jnp.where(c == 0, own, other)
    W16[8:16, :] = jnp.where(c == 0, other, own)
    W[c, z, xlo, y, xhi] = (W16[...] * g16[...]).astype(BF16)

    def agz(o, src_z):
        blk = W.at[c, src_z, xlo, y, xhi]
        return copy(blk, blk, gz_s.at[o], gz_r.at[o], at_z(o))

    def agz_start(o, carry):
        agz(o, z).start()
        return carry

    lax.fori_loop(1, Z, agz_start, 0)

    def core_copy(k):
        part = pl.ds(k * zt, zt)
        return copy(G.at[sib, part], GR.at[part], cr_s.at[k], cr_r.at[k], at_core)

    def grad(k, carry):
        t = tok[:, pl.ds(pl.multiple_of(k * TILE, TILE), TILE)]
        for h in range(2):
            g = lax.dot_general(t, M[h], (((0,), (0,)), ((), ())), preferred_element_type=F32)
            G[h, pl.ds(k * zt, zt)] = g.astype(BF16).reshape(zt, 2, 4, 2, 16, HALF)
        core_copy(k).start()
        return carry

    lax.fori_loop(0, tiles, grad, 0)

    def core_add(k, carry):
        core_copy(k).wait_recv()
        part = pl.ds(k * zt, zt)
        G[c, part] = (G[c, part].astype(F32) + GR[part].astype(F32)).astype(BF16)
        return carry

    y_a = copy(G.at[c, zA, :, yo], yA, ms_s.at[1], ms_r.at[1], at_y(1))
    y_b = copy(G.at[c, zB, :, yo], yB, ms_s.at[2], ms_r.at[2], at_y(3))
    y_l0 = copy(G.at[c, zA, :, yp], yL.at[zA], ms_s.at[3], ms_r.at[3], at_y(1))
    y_l1 = copy(G.at[c, zB, :, yp], yL.at[zB], ms_s.at[4], ms_r.at[4], at_y(1))
    y_r0 = copy(G.at[c, zA, :, ym], yR.at[zA], ms_s.at[5], ms_r.at[5], at_y(3))
    y_r1 = copy(G.at[c, zB, :, ym], yR.at[zB], ms_s.at[6], ms_r.at[6], at_y(3))
    lax.fori_loop(0, tiles // 2, core_add, 0)
    y_a.start()
    y_r0.start()
    lax.fori_loop(tiles // 2, tiles, core_add, 0)
    y_b.start()
    y_l1.start()

    def agz_wait(o, carry):
        agz(o, (z + Z - o) % Z).wait_recv()
        return carry

    lax.fori_loop(1, Z, agz_wait, 0)

    def agy(i, yy, o, half=None):
        blk = W.at[c, pl.ds(0, Z) if half is None else half, xlo, yy, xhi]
        return copy(blk, blk, ag_s.at[i], ag_r.at[i], at_y(o))

    agy(0, y, 1).start()
    agy(1, y, 3).start()

    def add_ya(k, carry):
        G[c, k, :, yp] = (G[c, k, :, yp].astype(F32) + yA[k].astype(F32)).astype(BF16)
        return carry

    def add_yb(k, carry):
        G[c, hz + k, :, ym] = (G[c, hz + k, :, ym].astype(F32) + yB[k].astype(F32)).astype(BF16)
        return carry

    y_a.wait_recv()
    lax.fori_loop(0, hz, add_ya, 0)
    y_l0.start()
    y_b.wait_recv()
    lax.fori_loop(0, hz, add_yb, 0)
    y_r1.start()

    agy(0, ym, 1).wait_recv()
    agy(2, ym, 1, zA).start()
    agy(1, yp, 3).wait_recv()
    agy(3, yp, 3, zB).start()
    agy(2, yo, 1, zA).wait_recv()
    agy(3, yo, 3, zB).wait_recv()

    def agx(i, o_src, o, half=None):
        blk = W.at[c, pl.ds(0, Z) if half is None else half, xs[o_src], :, xh[o_src]]
        return copy(blk, blk, ag_s.at[i], ag_r.at[i], at_x(o))

    def agc(i, o_src, h):
        blk = W.at[h, :, xs[o_src], :, xh[o_src]]
        return copy(blk, blk, ag_s.at[i], ag_r.at[i], at_core)

    agx(4, 0, 1).start()
    agx(5, 0, 3).start()
    agc(8, 0, c).start()

    y_r0.wait_recv()
    y_l1.wait_recv()
    y_l0.wait_recv()
    y_r1.wait_recv()

    def add_y(k, carry):
        S2[k] = (G[c, k, :, y].astype(F32) + yL[k].astype(F32) + yR[k].astype(F32)).astype(BF16)
        return carry

    lax.fori_loop(0, Z, add_y, 0)

    x_a = copy(S2.at[zA, xs[2], xh[2]], xA, ms_s.at[7], ms_r.at[7], at_x(1))
    x_b = copy(S2.at[zB, xs[2], xh[2]], xB, ms_s.at[8], ms_r.at[8], at_x(3))
    x_l0 = copy(S2.at[zA, xs[1], xh[1]], xL.at[zA], ms_s.at[9], ms_r.at[9], at_x(1))
    x_l1 = copy(S2.at[zB, xs[1], xh[1]], xL.at[zB], ms_s.at[10], ms_r.at[10], at_x(1))
    x_r0 = copy(S2.at[zA, xs[3], xh[3]], xR.at[zA], ms_s.at[11], ms_r.at[11], at_x(3))
    x_r1 = copy(S2.at[zB, xs[3], xh[3]], xR.at[zB], ms_s.at[12], ms_r.at[12], at_x(3))
    x_a.start()
    x_b.start()
    x_l1.start()
    x_r0.start()

    agx(4, 3, 1).wait_recv()
    agx(6, 3, 1, zA).start()
    agc(9, 3, c).start()
    agx(5, 1, 3).wait_recv()
    agx(7, 1, 3, zB).start()
    agc(10, 1, c).start()

    def add_xa(k, carry):
        S2[k, xs[1], xh[1]] = (S2[k, xs[1], xh[1]].astype(F32) + xA[k].astype(F32)).astype(BF16)
        return carry

    def add_xb(k, carry):
        S2[hz + k, xs[3], xh[3]] = (S2[hz + k, xs[3], xh[3]].astype(F32) + xB[k].astype(F32)).astype(BF16)
        return carry

    x_a.wait_recv()
    lax.fori_loop(0, hz, add_xa, 0)
    x_l0.start()
    x_b.wait_recv()
    lax.fori_loop(0, hz, add_xb, 0)
    x_r1.start()
    x_r0.wait_recv()
    x_l1.wait_recv()
    x_l0.wait_recv()
    x_r1.wait_recv()

    def add_x(k, carry):
        S3[k] = (S2[k, xlo, xhi].astype(F32) + xL[k].astype(F32) + xR[k].astype(F32)).astype(BF16)
        return carry

    lax.fori_loop(0, Z, add_x, 0)

    def rsz(o, dst_z, src_z):
        return copy(S3.at[dst_z], zr.at[src_z], rz_s.at[o], rz_r.at[o], at_z(o))

    def rsz_start(o, carry):
        rsz(o, (z + o) % Z, z).start()
        return carry

    lax.fori_loop(1, Z, rsz_start, 0)

    agx(6, 2, 1, zA).wait_recv()
    agx(7, 2, 3, zB).wait_recv()
    agc(11, 2, c).start()

    def rsz_add(o, acc):
        src = (z + Z - o) % Z
        rsz(o, z, src).wait_recv()
        return acc + zr[src].astype(F32)

    s4 = lax.fori_loop(1, Z, rsz_add, S3[z].astype(F32))

    q = jnp.sum(W16[...] * s4, axis=1, keepdims=True) * inverse
    s4 = s4 * (g16[...] * inverse)
    S4[0] = s4[0:8]
    S4[1] = s4[8:16]
    gx = copy(S4.at[sib], wgr, ms_s.at[13], ms_r.at[13], at_core)
    gx.start()
    lane = lax.broadcasted_iota(jnp.int32, (16, 128), 1)
    sub = lax.broadcasted_iota(jnp.int32, (16, 128), 0)
    row = jnp.sum(jnp.where(lane == (y * 2 + xhi) * 16 + sub, q, 0.0), axis=0, keepdims=True)
    sub8 = lax.broadcasted_iota(jnp.int32, (8, 128), 0)
    qs[...] = jnp.where(sub8 == (z * 2 + xlo) % 8, row, 0.0)
    qz[z] = qs[...]

    def gqz(o, src_z):
        return copy(qs, qz.at[src_z], qz_s.at[o], qz_r.at[o], at_z(o))

    def gqz_start(o, carry):
        gqz(o, z).start()
        return carry

    lax.fori_loop(1, Z, gqz_start, 0)

    for o in range(4):
        agc(8 + (0, 2, 3, 1)[o], o, sib).wait_recv()

    def project(k, acc):
        t = tok[:, pl.ds(pl.multiple_of(k * TILE, TILE), TILE)]
        return tuple(
            acc[h] + jnp.dot(t, W[h, pl.ds(k * zt, zt)].reshape(TILE, HALF), preferred_element_type=F32)
            for h in range(2)
        )

    zero = jnp.zeros((tok.shape[0], HALF), F32)
    prods = lax.fori_loop(0, tiles, project, (zero, zero))
    mean = jnp.zeros((tok.shape[0], 1), F32)
    for h in range(2):
        kf = jnp.where(live, prods[h] * rs, 0.0)
        keys[:, h * HALF:(h + 1) * HALF] = kf.astype(BF16)
        mean += jnp.sum(kf * kg[:, h * HALF:(h + 1) * HALF].astype(F32), axis=1, keepdims=True)
    coef = rs * rs * (mean / D)

    def back(k, carry):
        cols = pl.ds(pl.multiple_of(k * TILE, TILE), TILE)
        d = -(tok[:, cols].astype(F32) * coef)
        for h in range(2):
            d += lax.dot_general(
                M[h], W[h, pl.ds(k * zt, zt)].reshape(TILE, HALF),
                (((1,), (1,)), ((), ())), preferred_element_type=F32,
            )
        tig[:, cols] = d.astype(BF16)
        return carry

    def gqz_wait(o, carry):
        gqz(o, (z + Z - o) % Z).wait_recv()
        return carry

    lax.fori_loop(1, Z, gqz_wait, 0)
    for b in range(Z // 4):
        qy[b * 8:(b + 1) * 8, :] = qz[4 * b] + qz[4 * b + 1] + qz[4 * b + 2] + qz[4 * b + 3]
    qys = [copy(qy, qyr.at[o], ms_s.at[13 + o], ms_r.at[13 + o], at_y(o)) for o in (1, 2, 3)]
    for d in qys:
        d.start()
    lax.fori_loop(0, tiles // 2, back, 0)
    for d in qys:
        d.wait_recv()
    qx[...] = qy[...] + qyr[1] + qyr[2] + qyr[3]
    qxs = [copy(qx, qxr.at[o], ms_s.at[16 + o], ms_r.at[16 + o], at_x(o)) for o in (1, 2, 3)]
    for d in qxs:
        d.start()
    lax.fori_loop(tiles // 2, tiles, back, 0)
    for d in qxs:
        d.wait_recv()
    qc[...] = qx[...] + qxr[1] + qxr[2] + qxr[3]
    qcs = copy(qc, qcr, ms_s.at[20], ms_r.at[20], at_core)
    qcs.start()

    gx.wait_recv()
    own, other = S4[c], wgr[...]
    wg[:, 0:HALF] = jnp.where(c == 0, own, other)
    wg[:, HALF:2 * HALF] = jnp.where(c == 0, other, own)
    qcs.wait_recv()
    gg[...] = qc[...] + qcr[...]

    def sent_z(o, carry):
        agz(o, z).wait_send()
        rsz(o, (z + o) % Z, z).wait_send()
        gqz(o, z).wait_send()
        return carry

    lax.fori_loop(1, Z, sent_z, 0)

    def sent_core(k, carry):
        core_copy(k).wait_send()
        return carry

    lax.fori_loop(0, tiles, sent_core, 0)
    for d in (
        y_a, y_b, y_l0, y_l1, y_r0, y_r1, x_a, x_b, x_l0, x_l1, x_r0, x_r1, gx, qcs, *qys, *qxs,
        agy(0, y, 1), agy(1, y, 3), agy(2, ym, 1, zA), agy(3, yp, 3, zB),
        agx(4, 0, 1), agx(5, 0, 3), agx(6, 3, 1, zA), agx(7, 1, 3, zB),
        agc(8, 0, c), agc(9, 3, c), agc(10, 1, c), agc(11, 2, c),
    ):
        d.wait_send()


def local(tokens, gain, w_codes, w_scales, seq_counts, key_grad):
    rows, D = tokens.shape
    node_count = lax.axis_size("node")
    local_count = lax.axis_size("local")
    Z = node_count // 2
    inverse = 1.0 / math.sqrt(rows * node_count * local_count)
    chip = (lax.axis_index("node") * local_count + lax.axis_index("local")) // 2
    g16 = lax.dynamic_slice_in_dim(gain, chip * 16, 16, 0).reshape(16, 1)
    wsh = w_codes.astype(F32) * w_scales.astype(F32)[:, :, None]
    wsh = wsh.reshape(2, 2, 8, 128).transpose(0, 2, 1, 3).reshape(2, 8, HALF)
    vmem = pl.BlockSpec(memory_space=pltpu.VMEM)
    dma = pltpu.SemaphoreType.DMA
    hz = Z // 2
    keys, tig, wg, gg = pl.pallas_call(
        functools.partial(kernel, Z, inverse),
        out_shape=(
            jax.ShapeDtypeStruct((rows, 2 * HALF), BF16),
            jax.ShapeDtypeStruct((rows, D), BF16),
            jax.ShapeDtypeStruct((8, 2 * HALF), F32),
            jax.ShapeDtypeStruct((2 * Z, 128), F32),
        ),
        in_specs=[pl.BlockSpec(memory_space=pltpu.SMEM)] + [vmem] * 4,
        out_specs=(vmem,) * 4,
        scratch_shapes=[
            pltpu.VMEM((2, Z, 2, 4, 2, 16, HALF), BF16),
            pltpu.VMEM((2, rows, HALF), BF16),
            pltpu.VMEM((2, Z, 2, 4, 2, 16, HALF), BF16),
            pltpu.VMEM((Z, 2, 4, 2, 16, HALF), BF16),
            pltpu.VMEM((16, HALF), F32),
            pltpu.VMEM((8, HALF), F32),
            pltpu.VMEM((hz, 2, 2, 16, HALF), BF16),
            pltpu.VMEM((hz, 2, 2, 16, HALF), BF16),
            pltpu.VMEM((Z, 2, 2, 16, HALF), BF16),
            pltpu.VMEM((Z, 2, 2, 16, HALF), BF16),
            pltpu.VMEM((Z, 2, 2, 16, HALF), BF16),
            pltpu.VMEM((hz, 16, HALF), BF16),
            pltpu.VMEM((hz, 16, HALF), BF16),
            pltpu.VMEM((Z, 16, HALF), BF16),
            pltpu.VMEM((Z, 16, HALF), BF16),
            pltpu.VMEM((Z, 16, HALF), BF16),
            pltpu.VMEM((Z, 16, HALF), BF16),
            pltpu.VMEM((2, 8, HALF), F32),
            pltpu.VMEM((8, HALF), F32),
            pltpu.VMEM((8, 128), F32),
            pltpu.VMEM((Z, 8, 128), F32),
            pltpu.VMEM((2 * Z, 128), F32),
            pltpu.VMEM((4, 2 * Z, 128), F32),
            pltpu.VMEM((2 * Z, 128), F32),
            pltpu.VMEM((4, 2 * Z, 128), F32),
            pltpu.VMEM((2 * Z, 128), F32),
            pltpu.VMEM((2 * Z, 128), F32),
            dma((12,)), dma((12,)),
            dma((Z,)), dma((Z,)),
            dma((Z,)), dma((Z,)),
            dma((Z,)), dma((Z,)),
            dma((D // TILE,)), dma((D // TILE,)),
            dma((21,)), dma((21,)),
        ],
        compiler_params=pltpu.CompilerParams(
            collective_id=0, has_side_effects=True, vmem_limit_bytes=48 << 20
        ),
    )(seq_counts, tokens, key_grad, wsh, g16)
    return keys, tig, wg, gg.reshape(D)


def solution(mesh):
    return jax.shard_map(
        local,
        mesh=mesh,
        in_specs=(
            P(("node", "local"), None),
            P(),
            P(None, ("node", "local"), None),
            P(None, ("node", "local")),
            P(("node", "local")),
            P(("node", "local"), None),
        ),
        out_specs=(
            P(("node", "local"), None),
            P(("node", "local"), None),
            P(("node", "local"), None),
            P(),
        ),
        check_vma=False,
    )
```

```python
import functools
import math

import jax
import jax.numpy as jnp
from jax import lax
from jax.experimental import pallas as pl
from jax.experimental.pallas import tpu as pltpu
from jax.sharding import PartitionSpec as P

SEQ_LEN = 64
HALF = 256
TILE = 512
MESH = pl.DeviceIdType.MESH
F32 = jnp.float32
BF16 = jnp.bfloat16
ALL = slice(None)


def copy(src, dst, send, recv, dev):
    return pltpu.make_async_remote_copy(
        src_ref=src, dst_ref=dst, send_sem=send, recv_sem=recv, device_id=dev, device_id_type=MESH
    )


class RingSum:
    def __init__(self, ref, at, first, n, bufs, sems, plus, minus):
        self.ref, self.at, self.first, self.n, self.h = ref, at, first, n, n // 2
        self.a, self.b, self.l, self.r = bufs
        h = self.h
        near, far = pl.ds(0, h), pl.ds(h, h)

        def one(i, o, part, dst, dev):
            src = ref.at[at(o, pl.ds(first + part.start, h))]
            return copy(src, dst, sems[0].at[i], sems[1].at[i], dev)

        self.to_a = one(0, 2, near, self.a, plus)
        self.to_b = one(1, 2, far, self.b, minus)
        self.l0 = one(2, 1, near, self.l.at[near], plus)
        self.l1 = one(3, 1, far, self.l.at[far], plus)
        self.r0 = one(4, 3, near, self.r.at[near], minus)
        self.r1 = one(5, 3, far, self.r.at[far], minus)
        self.copies = (self.to_a, self.to_b, self.l0, self.l1, self.r0, self.r1)

    def start(self):
        for d in (self.to_a, self.to_b, self.l1, self.r0):
            d.start()

    def add(self, o, base, buf):
        def body(k, carry):
            i = self.at(o, self.first + base + k)
            self.ref[i] = (self.ref[i].astype(F32) + buf[k].astype(F32)).astype(BF16)
            return carry

        lax.fori_loop(0, self.h, body, 0)

    def forward(self):
        self.to_a.wait_recv()
        self.add(1, 0, self.a)
        self.l0.start()
        self.to_b.wait_recv()
        self.add(3, self.h, self.b)
        self.r1.start()

    def finish(self, dst, dst_first):
        for d in (self.l1, self.r0, self.l0, self.r1):
            d.wait_recv()

        def body(k, carry):
            own = self.ref[self.at(0, self.first + k)].astype(F32)
            dst[dst_first + k] = (own + self.l[k].astype(F32) + self.r[k].astype(F32)).astype(BF16)
            return carry

        lax.fori_loop(0, self.n, body, 0)


class RingGather:
    def __init__(self, ref, at, first, n, sems, plus, minus):
        h = n // 2
        whole, near, far = pl.ds(first, n), pl.ds(first, h), pl.ds(first + h, h)

        def one(i, o, part, dev):
            block = ref.at[at(o, part)]
            return copy(block, block, sems[0].at[i], sems[1].at[i], dev)

        self.sends = (one(0, 0, whole, plus), one(1, 0, whole, minus), one(2, 3, near, plus), one(3, 1, far, minus))
        self.recvs = (one(0, 3, whole, plus), one(1, 1, whole, minus), one(2, 2, near, plus), one(3, 2, far, minus))

    def start(self):
        self.sends[0].start()
        self.sends[1].start()

    def pass_on(self, i):
        self.recvs[i].wait_recv()
        self.sends[2 + i].start()

    def finish(self):
        self.recvs[2].wait_recv()
        self.recvs[3].wait_recv()


def kernel(
    Z, inverse,
    cnt, tok_hbm, kg_hbm, codes, scales, gain,
    keys, tig, wg, gg,
    tok, kg, wsh, W, M, G, GR, W16, wrecv,
    ya, yb, yl, yr, xa, xb, xl, xr, Sy, Sx,
    ya2, yb2, yl2, yr2, xa2, xb2, xl2, xr2, S3, zr, S4, wgr,
    qs, qz, qy, qyr, qx, qxr,
    in_s, ag_s, ag_r, agc_s, agc_r, rs_s, rs_r, gz_s, gz_r, rz_s, rz_r, qz_s, qz_r, cr_s, cr_r, ms_s, ms_r,
):
    rows, D = tok.shape
    tiles = D // TILE
    zt = Z // tiles
    hz = Z // 2
    node = lax.axis_index("node")
    loc = lax.axis_index("local")
    z, xlo = node // 2, node % 2
    y, xhi, c = loc // 4, (loc // 2) % 2, loc % 2
    x = 2 * xhi + xlo
    sib = 1 - c

    def at_z(o):
        return (((z + o) % Z) * 2 + xlo, loc)

    def at_y(o):
        return (node, ((y + o) % 4) * 4 + xhi * 2 + c)

    def at_x(o, core):
        xx = (x + o) % 4
        return (z * 2 + xx % 2, y * 4 + (xx // 2) * 2 + core)

    at_core = (node, y * 4 + xhi * 2 + sib)
    ys = [(y + o) % 4 for o in range(4)]
    xs = [((x + o) % 4) % 2 for o in range(4)]
    xh = [((x + o) % 4) // 2 for o in range(4)]

    loads = [pltpu.make_async_copy(kg_hbm, kg, in_s.at[0])]
    for i in range(2):
        part = pl.ds(i * (D // 2), D // 2)
        loads.append(pltpu.make_async_copy(tok_hbm.at[:, part], tok.at[:, part], in_s.at[1 + i]))
    for d in loads:
        d.start()

    barrier = pltpu.get_barrier_semaphore()

    def greet(dev):
        pl.semaphore_signal(barrier, inc=1, device_id=dev, device_id_type=MESH)

    def hello(o, carry):
        greet(at_z(o))
        return carry

    greet(at_core)
    lax.fori_loop(1, Z, hello, 0)
    for o in (1, 2, 3):
        greet(at_y(o))
        greet(at_x(o, c))
        greet(at_x(o, sib))

    chip = (node * 16 + loc) // 2
    lane = lax.broadcasted_iota(jnp.int32, (16, 128), 1)
    sub = lax.broadcasted_iota(jnp.int32, (16, 128), 0)
    grow = gain[pl.ds(chip // 8, 1), :]
    g16 = jnp.sum(jnp.where(lane == (chip % 8) * 16 + sub, grow, 0.0), axis=1, keepdims=True)
    eye = lax.broadcasted_iota(jnp.int32, (8, 8), 0) == lax.broadcasted_iota(jnp.int32, (8, 8), 1)
    sc = scales[...].astype(F32)
    for b in range(4):
        col = jnp.sum(jnp.where(eye, sc[b:b + 1, :], 0.0), axis=1, keepdims=True)
        wsh[b // 2, :, (b % 2) * 128:(b % 2 + 1) * 128] = codes[b].astype(F32) * col

    pl.semaphore_wait(barrier, Z - 1 + 10)
    wx = copy(wsh.at[sib], wrecv, ms_s.at[0], ms_r.at[0], at_core)
    wx.start()

    def square(k, acc):
        t = tok[:, pl.ds(pl.multiple_of(k * TILE, TILE), TILE)].astype(F32)
        return acc + jnp.sum(t * t, axis=1, keepdims=True)

    loads[1].wait()
    total = lax.fori_loop(0, tiles // 2, square, jnp.zeros((rows, 1), F32))
    loads[2].wait()
    total = lax.fori_loop(tiles // 2, tiles, square, total)
    rs = lax.rsqrt(total / D + 1e-05)
    live = lax.broadcasted_iota(jnp.int32, (rows, 1), 0) // SEQ_LEN < cnt[0]
    loads[0].wait()
    for h in range(2):
        m = jnp.where(live, kg[:, h * HALF:(h + 1) * HALF].astype(F32), 0.0)
        M[h] = (m * rs).astype(BF16)

    wx.wait()
    own, other = wsh[c], wrecv[...]
    W16[0:8, :] = jnp.where(c == 0, own, other)
    W16[8:16, :] = jnp.where(c == 0, other, own)
    W[c, z, xlo, y, xhi] = (W16[...] * g16).astype(BF16)

    def agz(o, src_z):
        block = W.at[c, src_z, xlo, y, xhi]
        return copy(block, block, gz_s.at[o], gz_r.at[o], at_z(o))

    def agz_start(o, carry):
        agz(o, z).start()
        return carry

    lax.fori_loop(1, Z, agz_start, 0)

    def core_copy(k):
        part = pl.ds(k * zt, zt)
        return copy(G.at[sib, part], GR.at[part], cr_s.at[k], cr_r.at[k], at_core)

    def grad(k, carry):
        t = tok[:, pl.ds(pl.multiple_of(k * TILE, TILE), TILE)]
        for h in range(2):
            g = lax.dot_general(t, M[h], (((0,), (0,)), ((), ())), preferred_element_type=F32)
            G[h, pl.ds(k * zt, zt)] = g.astype(BF16).reshape(zt, 2, 4, 2, 16, HALF)
        core_copy(k).start()
        return carry

    lax.fori_loop(0, tiles, grad, 0)

    def core_add(k, carry):
        core_copy(k).wait_recv()
        part = pl.ds(k * zt, zt)
        G[c, part] = (G[c, part].astype(F32) + GR[part].astype(F32)).astype(BF16)
        return carry

    def sems(pair, i, n):
        return pair[0].at[pl.ds(i, n)], pair[1].at[pl.ds(i, n)]

    rsem = (rs_s, rs_r)
    sum_y = RingSum(
        G, lambda o, p: (c, p, ALL, ys[o]), 0, hz, (ya, yb, yl, yr), sems(rsem, 0, 6), at_y(1), at_y(3)
    )
    sum_x = RingSum(
        G, lambda o, p: (c, p, xs[o], ALL, xh[o]), hz, hz, (xa, xb, xl, xr), sems(rsem, 6, 6), at_x(1, c), at_x(3, c)
    )
    sum_yx = RingSum(
        Sy, lambda o, p: (p, xs[o], xh[o]), 0, hz, (xa2, xb2, xl2, xr2), sems(rsem, 12, 6), at_x(1, c), at_x(3, c)
    )
    sum_xy = RingSum(
        Sx, lambda o, p: (p, ys[o]), 0, hz, (ya2, yb2, yl2, yr2), sems(rsem, 18, 6), at_y(1), at_y(3)
    )
    asem = (ag_s, ag_r)
    get_y = RingGather(W, lambda o, p: (c, p, xlo, ys[o], xhi), 0, hz, sems(asem, 0, 4), at_y(1), at_y(3))
    get_x = RingGather(W, lambda o, p: (c, p, xs[o], y, xh[o]), hz, hz, sems(asem, 4, 4), at_x(1, c), at_x(3, c))
    get_yx = RingGather(W, lambda o, p: (c, p, xs[o], ALL, xh[o]), 0, hz, sems(asem, 8, 4), at_x(1, c), at_x(3, c))
    get_xy = RingGather(W, lambda o, p: (c, p, ALL, ys[o]), hz, hz, sems(asem, 12, 4), at_y(1), at_y(3))

    def hand_yx(o, half):
        block = W.at[half, pl.ds(0, hz), xs[o], :, xh[o]]
        return copy(block, block, agc_s.at[o], agc_r.at[o], at_core)

    def hand_xy(o, half):
        block = W.at[half, pl.ds(hz, hz), :, ys[o]]
        return copy(block, block, agc_s.at[4 + o], agc_r.at[4 + o], at_core)

    lax.fori_loop(0, tiles // 2, core_add, 0)
    sum_y.start()
    lax.fori_loop(tiles // 2, tiles, core_add, 0)
    sum_x.start()
    sum_y.forward()
    sum_x.forward()

    def agz_wait(o, carry):
        agz(o, (z + Z - o) % Z).wait_recv()
        return carry

    lax.fori_loop(1, Z, agz_wait, 0)
    get_y.start()
    get_x.start()
    sum_y.finish(Sy, 0)
    sum_yx.start()
    sum_x.finish(Sx, 0)
    sum_xy.start()
    for i in range(2):
        get_y.pass_on(i)
        get_x.pass_on(i)
    sum_yx.forward()
    sum_xy.forward()
    get_y.finish()
    get_yx.start()
    hand_yx(0, c).start()
    get_x.finish()
    get_xy.start()
    hand_xy(0, c).start()
    sum_yx.finish(S3, 0)
    sum_xy.finish(S3, hz)

    def rsz(o, dst_z, src_z):
        return copy(S3.at[dst_z], zr.at[src_z], rz_s.at[o], rz_r.at[o], at_z(o))

    def rsz_start(o, carry):
        rsz(o, (z + o) % Z, z).start()
        return carry

    lax.fori_loop(1, Z, rsz_start, 0)

    for i, o in ((0, 3), (1, 1)):
        get_yx.pass_on(i)
        hand_yx(o, c).start()
        get_xy.pass_on(i)
        hand_xy(o, c).start()

    def rsz_add(o, acc):
        src = (z + Z - o) % Z
        rsz(o, z, src).wait_recv()
        return acc + zr[src].astype(F32)

    s4 = lax.fori_loop(1, Z, rsz_add, S3[z].astype(F32))

    q = jnp.sum(W16[...] * s4, axis=1, keepdims=True) * inverse
    s4 = s4 * (g16 * inverse)
    S4[0] = s4[0:8]
    S4[1] = s4[8:16]
    gx = copy(S4.at[sib], wgr, ms_s.at[1], ms_r.at[1], at_core)
    gx.start()
    qs[...] = jnp.sum(jnp.where(lane == (y * 2 + xhi) * 16 + sub, q, 0.0), axis=0, keepdims=True)

    def gqz(o, src_z):
        return copy(qs, qz.at[src_z], qz_s.at[o], qz_r.at[o], at_z(o))

    def gqz_start(o, carry):
        gqz(o, z).start()
        return carry

    lax.fori_loop(1, Z, gqz_start, 0)

    get_yx.finish()
    hand_yx(2, c).start()
    get_xy.finish()
    hand_xy(2, c).start()

    zrow = lax.broadcasted_iota(jnp.int32, (Z, 128), 0)

    def gqz_add(o, acc):
        src = (z + Z - o) % Z
        gqz(o, src).wait_recv()
        return jnp.where(zrow == src, qz[src], acc)

    qy[...] = lax.fori_loop(1, Z, gqz_add, jnp.where(zrow == z, qs[...], 0.0))
    qys = [copy(qy, qyr.at[o], ms_s.at[1 + o], ms_r.at[1 + o], at_y(o)) for o in (1, 2, 3)]
    for d in qys:
        d.start()

    for o in range(4):
        hand_yx(o, sib).wait_recv()
        hand_xy(o, sib).wait_recv()
    span = D // 2

    def project(k, acc):
        t = tok[:, pl.ds(pl.multiple_of(k * span, span), span)]
        return tuple(
            acc[h] + jnp.dot(t, W[h, pl.ds(k * hz, hz)].reshape(span, HALF), preferred_element_type=F32)
            for h in range(2)
        )

    zero = jnp.zeros((rows, HALF), F32)
    prods = lax.fori_loop(0, 2, project, (zero, zero))
    mean = jnp.zeros((rows, 1), F32)
    for h in range(2):
        kf = jnp.where(live, prods[h] * rs, 0.0)
        keys[:, h * HALF:(h + 1) * HALF] = kf.astype(BF16)
        mean += jnp.sum(kf * kg[:, h * HALF:(h + 1) * HALF].astype(F32), axis=1, keepdims=True)
    coef = rs * rs * (mean / D)

    for d in qys:
        d.wait_recv()
    qx[...] = qy[...] + qyr[1] + qyr[2] + qyr[3]
    qxs = [
        copy(qx, qxr.at[o, r], ms_s.at[5 + 2 * o + r], ms_r.at[5 + 2 * o + r], at_x(o, sib if r else c))
        for o in range(4) for r in range(2) if o or r
    ]
    for d in qxs:
        d.start()

    def back(k, carry):
        cols = pl.ds(pl.multiple_of(k * TILE, TILE), TILE)
        d = -(tok[:, cols].astype(F32) * coef)
        for h in range(2):
            d += lax.dot_general(
                M[h], W[h, pl.ds(k * zt, zt)].reshape(TILE, HALF),
                (((1,), (1,)), ((), ())), preferred_element_type=F32,
            )
        tig[:, cols] = d.astype(BF16)
        return carry

    lax.fori_loop(0, tiles, back, 0)

    gx.wait_recv()
    own, other = S4[c], wgr[...]
    wg[:, 0:HALF] = jnp.where(c == 0, own, other)
    wg[:, HALF:2 * HALF] = jnp.where(c == 0, other, own)
    for d in qxs:
        d.wait_recv()
    gg[xlo] = qx[...] + qxr[0, 1] + qxr[2, 0] + qxr[2, 1]
    gg[1 - xlo] = (qxr[1, 0] + qxr[1, 1]) + (qxr[3, 0] + qxr[3, 1])

    def sent_z(o, carry):
        agz(o, z).wait_send()
        rsz(o, (z + o) % Z, z).wait_send()
        gqz(o, z).wait_send()
        return carry

    lax.fori_loop(1, Z, sent_z, 0)

    def sent_core(k, carry):
        core_copy(k).wait_send()
        return carry

    lax.fori_loop(0, tiles, sent_core, 0)
    for s in (sum_y, sum_x, sum_yx, sum_xy):
        for d in s.copies:
            d.wait_send()
    for s in (get_y, get_x, get_yx, get_xy):
        for d in s.sends:
            d.wait_send()
    for o in range(4):
        hand_yx(o, c).wait_send()
        hand_xy(o, c).wait_send()
    for d in (gx, *qys, *qxs):
        d.wait_send()


def local(tokens, gain, w_codes, w_scales, seq_counts, key_grad):
    rows, D = tokens.shape
    node_count = lax.axis_size("node")
    local_count = lax.axis_size("local")
    Z = node_count // 2
    inverse = 1.0 / math.sqrt(rows * node_count * local_count)
    vmem = pl.BlockSpec(memory_space=pltpu.VMEM)
    hbm = pl.BlockSpec(memory_space=pl.ANY)
    dma = pltpu.SemaphoreType.DMA
    hz = Z // 2

    def ring(n, *inner):
        return [pltpu.VMEM((m, *inner, 16, HALF), BF16) for m in (n // 2, n // 2, n, n)]

    keys, tig, wg, gg = pl.pallas_call(
        functools.partial(kernel, Z, inverse),
        out_shape=(
            jax.ShapeDtypeStruct((rows, 2 * HALF), BF16),
            jax.ShapeDtypeStruct((rows, D), BF16),
            jax.ShapeDtypeStruct((8, 2 * HALF), F32),
            jax.ShapeDtypeStruct((2, Z, 128), F32),
        ),
        in_specs=[pl.BlockSpec(memory_space=pltpu.SMEM), hbm, hbm, vmem, vmem, vmem],
        out_specs=(vmem,) * 4,
        scratch_shapes=[
            pltpu.VMEM((rows, D), BF16),
            pltpu.VMEM((rows, 2 * HALF), BF16),
            pltpu.VMEM((2, 8, HALF), F32),
            pltpu.VMEM((2, Z, 2, 4, 2, 16, HALF), BF16),
            pltpu.VMEM((2, rows, HALF), BF16),
            pltpu.VMEM((2, Z, 2, 4, 2, 16, HALF), BF16),
            pltpu.VMEM((Z, 2, 4, 2, 16, HALF), BF16),
            pltpu.VMEM((16, HALF), F32),
            pltpu.VMEM((8, HALF), F32),
            *ring(hz, 2, 2),
            *ring(hz, 4),
            pltpu.VMEM((hz, 2, 2, 16, HALF), BF16),
            pltpu.VMEM((hz, 4, 16, HALF), BF16),
            *ring(hz),
            *ring(hz),
            pltpu.VMEM((Z, 16, HALF), BF16),
            pltpu.VMEM((Z, 16, HALF), BF16),
            pltpu.VMEM((2, 8, HALF), F32),
            pltpu.VMEM((8, HALF), F32),
            pltpu.VMEM((1, 128), F32),
            pltpu.VMEM((Z, 1, 128), F32),
            pltpu.VMEM((Z, 128), F32),
            pltpu.VMEM((4, Z, 128), F32),
            pltpu.VMEM((Z, 128), F32),
            pltpu.VMEM((4, 2, Z, 128), F32),
            dma((3,)),
            dma((16,)), dma((16,)),
            dma((8,)), dma((8,)),
            dma((24,)), dma((24,)),
            dma((Z,)), dma((Z,)),
            dma((Z,)), dma((Z,)),
            dma((Z,)), dma((Z,)),
            dma((D // TILE,)), dma((D // TILE,)),
            dma((13,)), dma((13,)),
        ],
        compiler_params=pltpu.CompilerParams(
            collective_id=0, has_side_effects=True, vmem_limit_bytes=48 << 20
        ),
    )(seq_counts, tokens, key_grad, w_codes, w_scales, gain.reshape(D // 128, 128))
    return keys, tig, wg, gg.transpose(1, 0, 2).reshape(D)


def solution(mesh):
    return jax.shard_map(
        local,
        mesh=mesh,
        in_specs=(
            P(("node", "local"), None),
            P(),
            P(None, ("node", "local"), None),
            P(None, ("node", "local")),
            P(("node", "local")),
            P(("node", "local"), None),
        ),
        out_specs=(
            P(("node", "local"), None),
            P(("node", "local"), None),
            P(("node", "local"), None),
            P(),
        ),
        check_vma=False,
    )
```

```python
import functools
import math

import jax
import jax.numpy as jnp
from jax import lax
from jax.experimental import pallas as pl
from jax.experimental.pallas import tpu as pltpu
from jax.sharding import PartitionSpec as P

SEQ_LEN = 64
HALF = 256
TILE = 512
WIDE = 1024
MESH = pl.DeviceIdType.MESH
F32 = jnp.float32
BF16 = jnp.bfloat16
ALL = slice(None)
VMEM_BYTES = 63 << 20


def copy(src, dst, send, recv, dev):
    return pltpu.make_async_remote_copy(
        src_ref=src, dst_ref=dst, send_sem=send, recv_sem=recv, device_id=dev, device_id_type=MESH
    )


def settle(ref, send=None, recv=None, dev=None):
    d = copy(ref, ref, send if recv is None else recv, recv if send is None else send, dev)
    if recv is None:
        d.wait_send()
    else:
        d.wait_recv()


class RingSum:
    def __init__(self, ref, at, first, n, bufs, sems, plus, minus):
        self.ref, self.at, self.first, self.n, self.h = ref, at, first, n, n // 2
        self.a, self.b, self.lr = bufs
        self.send, self.recv, self.dev = *sems, plus
        h = self.h
        near, far = pl.ds(0, h), pl.ds(h, h)

        def one(i, o, part, dst, dev):
            src = ref.at[at(o, pl.ds(first + part.start, h))]
            return copy(src, dst, self.send, self.recv.at[i], dev)

        self.to_a = one(0, 2, near, self.a, plus)
        self.to_b = one(1, 2, far, self.b, minus)
        self.l0 = one(2, 1, near, self.lr.at[0, near], plus)
        self.l1 = one(2, 1, far, self.lr.at[0, far], plus)
        self.r0 = one(2, 3, near, self.lr.at[1, near], minus)
        self.r1 = one(2, 3, far, self.lr.at[1, far], minus)

    def start(self):
        for d in (self.to_a, self.to_b, self.l1, self.r0):
            d.start()

    def add(self, o, base, buf):
        def body(k, carry):
            i = self.at(o, self.first + base + k)
            self.ref[i] = (self.ref[i].astype(F32) + buf[k].astype(F32)).astype(BF16)
            return carry

        lax.fori_loop(0, self.h, body, 0)

    def forward(self):
        self.to_a.wait_recv()
        self.add(1, 0, self.a)
        self.l0.start()
        self.to_b.wait_recv()
        self.add(3, self.h, self.b)
        self.r1.start()

    def finish(self, dst, dst_first):
        settle(self.lr, recv=self.recv.at[2], dev=self.dev)

        def body(k, carry):
            own = self.ref[self.at(0, self.first + k)].astype(F32)
            total = own + self.lr[0, k].astype(F32) + self.lr[1, k].astype(F32)
            dst[dst_first + k] = total.astype(BF16)
            return carry

        lax.fori_loop(0, self.n, body, 0)

    def sent(self, like):
        settle(like, send=self.send, dev=self.dev)


class RingGather:
    def __init__(self, ref, at, first, n, sems, plus, minus):
        h = n // 2
        whole, near, far = pl.ds(first, n), pl.ds(first, h), pl.ds(first + h, h)
        self.send, self.recv, self.dev = *sems, plus
        self.opposite = ref.at[at(2, whole)]

        def one(i, o, part, dev):
            block = ref.at[at(o, part)]
            return copy(block, block, self.send, self.recv.at[i], dev)

        self.sends = (one(0, 0, whole, plus), one(1, 0, whole, minus), one(2, 3, near, plus), one(2, 1, far, minus))
        self.recvs = (one(0, 3, whole, plus), one(1, 1, whole, minus))

    def start(self):
        self.sends[0].start()
        self.sends[1].start()

    def pass_on(self, i):
        self.recvs[i].wait_recv()
        self.sends[2 + i].start()

    def finish(self):
        settle(self.opposite, recv=self.recv.at[2], dev=self.dev)

    def sent(self, like):
        settle(like, send=self.send, dev=self.dev)


def kernel(
    Z, inverse,
    cnt, tok_hbm, kg_hbm, codes_hbm, scales_hbm, gain_hbm,
    keys_hbm, tig_hbm, wg_hbm, gg_hbm,
    tok, kg, codes, scales, gain, keys, tig, wg, gg, wsh, W, M, G, GR, W16, wrecv,
    ya, yb, ylr, xa, xb, xlr, Sy, Sx,
    ya2, yb2, ylr2, xa2, xb2, xlr2, S3, zr, S4, wgr,
    qs, qz, qy, qyr, qx, qxr,
    in_s, out_s, ag_r, rs_r, cr_r, ms_s, ms_r,
):
    rows, D = tok.shape
    tiles = D // TILE
    zt = Z // tiles
    gtiles = D // WIDE
    gt = Z // gtiles
    hz = Z // 2
    node = lax.axis_index("node")
    loc = lax.axis_index("local")
    z, xlo = node // 2, node % 2
    y, xhi, c = loc // 4, (loc // 2) % 2, loc % 2
    x = 2 * xhi + xlo
    sib = 1 - c

    def at_z(o):
        return (((z + o) % Z) * 2 + xlo, loc)

    def at_y(o):
        return (node, ((y + o) % 4) * 4 + xhi * 2 + c)

    def at_x(o, core):
        xx = (x + o) % 4
        return (z * 2 + xx % 2, y * 4 + (xx // 2) * 2 + core)

    at_core = (node, y * 4 + xhi * 2 + sib)
    ys = [(y + o) % 4 for o in range(4)]
    xs = [((x + o) % 4) % 2 for o in range(4)]
    xh = [((x + o) % 4) // 2 for o in range(4)]

    loads = []
    for i in range(2):
        part = pl.ds(i * (D // 2), D // 2)
        loads.append(pltpu.make_async_copy(tok_hbm.at[:, part], tok.at[:, part], in_s.at[i]))
    for i, (a, b) in enumerate(((kg_hbm, kg), (codes_hbm, codes), (scales_hbm, scales), (gain_hbm, gain))):
        loads.append(pltpu.make_async_copy(a, b, in_s.at[2 + i]))
    for d in loads:
        d.start()

    barrier = pltpu.get_barrier_semaphore()

    def greet(dev):
        pl.semaphore_signal(barrier, inc=1, device_id=dev, device_id_type=MESH)

    def hello(o, carry):
        greet(at_z(o))
        return carry

    greet(at_core)
    lax.fori_loop(1, Z, hello, 0)
    for o in (1, 2, 3):
        greet(at_y(o))
        greet(at_x(o, c))
        greet(at_x(o, sib))

    for d in loads[3:]:
        d.wait()
    chip = (node * 16 + loc) // 2
    lane = lax.broadcasted_iota(jnp.int32, (16, 128), 1)
    sub = lax.broadcasted_iota(jnp.int32, (16, 128), 0)
    grow = gain[pl.ds(chip // 8, 1), :]
    g16 = jnp.sum(jnp.where(lane == (chip % 8) * 16 + sub, grow, 0.0), axis=1, keepdims=True)
    eye = lax.broadcasted_iota(jnp.int32, (8, 8), 0) == lax.broadcasted_iota(jnp.int32, (8, 8), 1)
    sc = scales[...].astype(F32)
    for b in range(4):
        col = jnp.sum(jnp.where(eye, sc[b:b + 1, :], 0.0), axis=1, keepdims=True)
        wsh[b // 2, :, (b % 2) * 128:(b % 2 + 1) * 128] = codes[b].astype(F32) * col

    def square(k, acc):
        for i in range(TILE // 128):
            t = tok[:, pl.ds(pl.multiple_of(k * TILE + i * 128, 128), 128)].astype(F32)
            acc += t * t
        return acc

    loads[0].wait()
    total = lax.fori_loop(0, tiles // 2, square, jnp.zeros((rows, 128), F32))
    loads[1].wait()
    total = lax.fori_loop(tiles // 2, tiles, square, total)
    pl.semaphore_wait(barrier, Z - 1 + 10)
    wx = copy(wsh.at[sib], wrecv, ms_s.at[1], ms_r.at[0], at_core)
    wx.start()

    rs = lax.rsqrt(jnp.sum(total, axis=1, keepdims=True) / D + 1e-05)
    live = lax.broadcasted_iota(jnp.int32, (rows, 1), 0) // SEQ_LEN < cnt[0]
    loads[2].wait()
    M[...] = (jnp.where(live, kg[...].astype(F32), 0.0) * rs).astype(BF16)

    def core_copy(k):
        part = pl.ds(k * gt, gt)
        return copy(G.at[sib, part], GR.at[part], ms_s.at[0], cr_r.at[k], at_core)

    def grad(k, carry):
        t = tok[:, pl.ds(pl.multiple_of(k * WIDE, WIDE), WIDE)]
        g = lax.dot_general(t, M[...], (((0,), (0,)), ((), ())), preferred_element_type=F32).astype(BF16)
        for h in range(2):
            G[h, pl.ds(k * gt, gt)] = g[:, h * HALF:(h + 1) * HALF].reshape(gt, 2, 4, 2, 16, HALF)
        core_copy(k).start()
        return carry

    lax.fori_loop(0, gtiles // 2, grad, 0)

    wx.wait_recv()
    own, other = wsh[c], wrecv[...]
    W16[0:8, :] = jnp.where(c == 0, own, other)
    W16[8:16, :] = jnp.where(c == 0, other, own)
    W[c, z, xlo, y, xhi] = (W16[...] * g16).astype(BF16)

    def agz(o, src_z):
        block = W.at[c, src_z, xlo, y, xhi]
        return copy(block, block, ms_s.at[2], ms_r.at[1], at_z(o))

    def agz_start(o, carry):
        agz(o, z).start()
        return carry

    lax.fori_loop(1, Z, agz_start, 0)

    lax.fori_loop(gtiles // 2, gtiles, grad, 0)

    def core_add(k, carry):
        core_copy(k).wait_recv()
        part = pl.ds(k * gt, gt)
        G[c, part] = (G[c, part].astype(F32) + GR[part].astype(F32)).astype(BF16)
        return carry

    def sems(i, pair, j, n):
        return ms_s.at[i], pair.at[pl.ds(j, n)]

    sum_y = RingSum(G, lambda o, p: (c, p, ALL, ys[o]), 0, hz, (ya, yb, ylr), sems(8, rs_r, 0, 3), at_y(1), at_y(3))
    sum_x = RingSum(
        G, lambda o, p: (c, p, xs[o], ALL, xh[o]), hz, hz, (xa, xb, xlr), sems(9, rs_r, 3, 3), at_x(1, c), at_x(3, c)
    )
    sum_yx = RingSum(
        Sy, lambda o, p: (p, xs[o], xh[o]), 0, hz, (xa2, xb2, xlr2), sems(10, rs_r, 6, 3), at_x(1, c), at_x(3, c)
    )
    sum_xy = RingSum(Sx, lambda o, p: (p, ys[o]), 0, hz, (ya2, yb2, ylr2), sems(11, rs_r, 9, 3), at_y(1), at_y(3))
    get_y = RingGather(W, lambda o, p: (c, p, xlo, ys[o], xhi), 0, hz, sems(12, ag_r, 0, 3), at_y(1), at_y(3))
    get_x = RingGather(W, lambda o, p: (c, p, xs[o], y, xh[o]), hz, hz, sems(13, ag_r, 3, 3), at_x(1, c), at_x(3, c))
    get_yx = RingGather(
        W, lambda o, p: (c, p, xs[o], ALL, xh[o]), 0, hz, sems(14, ag_r, 6, 3), at_x(1, c), at_x(3, c)
    )
    get_xy = RingGather(W, lambda o, p: (c, p, ALL, ys[o]), hz, hz, sems(15, ag_r, 9, 3), at_y(1), at_y(3))

    def hand_yx(o, half):
        block = W.at[half, pl.ds(0, hz), xs[o], :, xh[o]]
        return copy(block, block, ms_s.at[3], ms_r.at[2], at_core)

    def hand_xy(o, half):
        block = W.at[half, pl.ds(hz, hz), :, ys[o]]
        return copy(block, block, ms_s.at[3], ms_r.at[2], at_core)

    lax.fori_loop(0, gtiles // 2, core_add, 0)
    sum_y.start()
    lax.fori_loop(gtiles // 2, gtiles, core_add, 0)
    sum_x.start()

    sum_y.forward()
    sum_x.forward()

    settle(W.at[c, pl.ds(0, Z - 1), xlo, y, xhi], recv=ms_r.at[1], dev=at_core)
    get_y.start()
    get_x.start()
    sum_y.finish(Sy, 0)
    sum_yx.start()
    sum_x.finish(Sx, 0)
    sum_xy.start()
    for i in range(2):
        get_y.pass_on(i)
        get_x.pass_on(i)
    sum_yx.forward()
    sum_xy.forward()
    get_y.finish()
    get_yx.start()
    hand_yx(0, c).start()
    get_x.finish()
    get_xy.start()
    hand_xy(0, c).start()
    sum_yx.finish(S3, 0)
    sum_xy.finish(S3, hz)

    q = jnp.sum(W[c, :, xlo, y, xhi].astype(F32) * S3[...].astype(F32), axis=2, keepdims=True).reshape(Z * 16, 1)
    diag = lax.broadcasted_iota(jnp.int32, (Z * 16, Z * 16), 0) == lax.broadcasted_iota(jnp.int32, (Z * 16, Z * 16), 1)
    qs[...] = jnp.sum(jnp.where(diag, q, 0.0), axis=0, keepdims=True)

    def gqz(o, src_z):
        return copy(qs, qz.at[src_z], ms_s.at[5], ms_r.at[4], at_z(o))

    def gqz_start(o, carry):
        gqz(o, z).start()
        return carry

    lax.fori_loop(1, Z, gqz_start, 0)

    def rsz(o, dst_z, src_z):
        return copy(S3.at[dst_z], zr.at[src_z], ms_s.at[4], ms_r.at[3], at_z(o))

    def rsz_start(o, carry):
        rsz(o, (z + o) % Z, z).start()
        return carry

    lax.fori_loop(1, Z, rsz_start, 0)

    for i, o in ((0, 3), (1, 1)):
        get_yx.pass_on(i)
        hand_yx(o, c).start()
        get_xy.pass_on(i)
        hand_xy(o, c).start()

    def gqz_add(o, acc):
        src = (z + Z - o) % Z
        return acc + qz[src]

    settle(qz.at[pl.ds(0, Z - 1)], recv=ms_r.at[4], dev=at_core)
    qsum = lax.fori_loop(1, Z, gqz_add, qs[...])
    lane = lax.broadcasted_iota(jnp.int32, (Z, Z * 16), 1)
    zrow = lax.broadcasted_iota(jnp.int32, (Z, Z * 16), 0)
    spread = jnp.where((lane >= zrow * 16) & (lane < zrow * 16 + 16), qsum, 0.0)
    src = lax.broadcasted_iota(jnp.int32, (Z * 16, 128), 0)
    to = lax.broadcasted_iota(jnp.int32, (Z * 16, 128), 1)
    place = jnp.where((src & 15) + (y * 2 + xhi) * 16 == to, 1.0, 0.0)
    qy[...] = jnp.dot(spread, place, precision=lax.Precision.HIGHEST, preferred_element_type=F32)
    qys = [copy(qy, qyr.at[o], ms_s.at[6], ms_r.at[6], at_y(o)) for o in (1, 2, 3)]
    for d in qys:
        d.start()

    get_yx.finish()
    hand_yx(2, c).start()
    get_xy.finish()
    hand_xy(2, c).start()

    settle(qyr.at[pl.ds(0, 3)], recv=ms_r.at[6], dev=at_core)
    qx[...] = qy[...] + qyr[1] + qyr[2] + qyr[3]
    qxs = [
        copy(qx, qxr.at[2 * o + r], ms_s.at[7], ms_r.at[7], at_x(o, sib if r else c))
        for o in range(4) for r in range(2) if o or r
    ]
    for d in qxs:
        d.start()

    def rsz_add(o, acc):
        src = (z + Z - o) % Z
        return acc + zr[src].astype(F32)

    settle(zr.at[pl.ds(0, Z - 1)], recv=ms_r.at[3], dev=at_core)
    s4 = lax.fori_loop(1, Z, rsz_add, S3[z].astype(F32))

    s4 = s4 * (g16 * inverse)
    S4[0] = s4[0:8]
    S4[1] = s4[8:16]
    gx = copy(S4.at[sib], wgr, ms_s.at[1], ms_r.at[5], at_core)
    gx.start()

    settle(W.at[sib], recv=ms_r.at[2], dev=at_core)
    span = D // 2

    def project(k, acc):
        t = tok[:, pl.ds(pl.multiple_of(k * span, span), span)]
        return tuple(
            acc[h] + jnp.dot(t, W[h, pl.ds(k * hz, hz)].reshape(span, HALF), preferred_element_type=F32)
            for h in range(2)
        )

    zero = jnp.zeros((rows, HALF), F32)
    prods = lax.fori_loop(0, 2, project, (zero, zero))
    mean = jnp.zeros((rows, 1), F32)
    for h in range(2):
        kf = jnp.where(live, prods[h] * rs, 0.0)
        keys[:, h * HALF:(h + 1) * HALF] = kf.astype(BF16)
        mean += jnp.sum(kf * kg[:, h * HALF:(h + 1) * HALF].astype(F32), axis=1, keepdims=True)
    coef = rs * rs * (mean / D)
    stores = [
        pltpu.make_async_copy(a, b, out_s.at[i])
        for i, (a, b) in enumerate(((keys, keys_hbm), (wg, wg_hbm), (gg, gg_hbm)))
    ]
    stores[0].start()

    def back(k, carry):
        cols = pl.ds(pl.multiple_of(k * TILE, TILE), TILE)
        d = -(tok[:, cols].astype(F32) * coef)
        for h in range(2):
            d += lax.dot_general(
                M[:, h * HALF:(h + 1) * HALF], W[h, pl.ds(k * zt, zt)].reshape(TILE, HALF),
                (((1,), (1,)), ((), ())), preferred_element_type=F32,
            )
        tig[:, cols] = d.astype(BF16)
        pltpu.make_async_copy(tig.at[:, cols], tig_hbm.at[:, cols], out_s.at[3]).start()
        return carry

    lax.fori_loop(0, tiles, back, 0)

    gx.wait_recv()
    own, other = S4[c], wgr[...]
    wg[:, 0:HALF] = jnp.where(c == 0, own, other)
    wg[:, HALF:2 * HALF] = jnp.where(c == 0, other, own)
    stores[1].start()
    settle(qxr.at[pl.ds(0, 7)], recv=ms_r.at[7], dev=at_core)
    same = qx[...] + qxr[1] + qxr[4] + qxr[5]
    next_x = (qxr[2] + qxr[3]) + (qxr[6] + qxr[7])
    row = lax.broadcasted_iota(jnp.int32, (2 * Z, Z), 0)
    zcol = lax.broadcasted_iota(jnp.int32, (2 * Z, Z), 1)
    total = sum(
        jnp.dot(
            jnp.where(row == 2 * zcol + p, 1.0, 0.0), v,
            precision=lax.Precision.HIGHEST, preferred_element_type=F32,
        )
        for p, v in ((xlo, same), (1 - xlo, next_x))
    )
    gg[...] = total * inverse / gain[...]
    stores[2].start()

    wx.wait_send()
    gx.wait_send()
    for ref, i in (
        (G.at[sib], 0), (W.at[c, pl.ds(0, Z - 1), xlo, y, xhi], 2), (W.at[c], 3), (S3.at[pl.ds(0, Z - 1)], 4),
        (qz.at[pl.ds(0, Z - 1)], 5), (qyr.at[pl.ds(0, 3)], 6), (qxr.at[pl.ds(0, 7)], 7),
    ):
        settle(ref, send=ms_s.at[i], dev=at_core)
    sum_y.sent(G.at[c, pl.ds(0, hz), :, pl.ds(0, 3)])
    sum_x.sent(G.at[c, pl.ds(0, hz), :, pl.ds(0, 3)])
    sum_yx.sent(Sx.at[:, pl.ds(0, 3)])
    sum_xy.sent(Sx.at[:, pl.ds(0, 3)])
    get_y.sent(W.at[c, pl.ds(0, hz), xlo, pl.ds(0, 3), xhi])
    get_x.sent(W.at[c, pl.ds(0, hz), xlo, pl.ds(0, 3), xhi])
    get_yx.sent(W.at[c, pl.ds(0, hz), :, pl.ds(0, 3)])
    get_xy.sent(W.at[c, pl.ds(0, hz), :, pl.ds(0, 3)])
    pltpu.make_async_copy(tig, tig_hbm, out_s.at[3]).wait()
    for d in stores:
        d.wait()


def keep(keys, tig, wg, gg, keys_out, tig_out, wg_out, gg_out, keys_v, tig_v, wg_v, gg_v, in_s, out_s):
    step = tig.shape[0] // 4
    moves = [(keys, keys_v, keys_out), (wg, wg_v, wg_out), (gg, gg_v, gg_out)]
    for i in range(4):
        part = pl.ds(i * step, step)
        moves.append((tig.at[part], tig_v.at[part], tig_out.at[part]))
    reads = [pltpu.make_async_copy(a, v, in_s.at[i]) for i, (a, v, _) in enumerate(moves)]
    writes = [pltpu.make_async_copy(v, b, out_s.at[i]) for i, (_, v, b) in enumerate(moves)]
    for d in reads:
        d.start()
    for r, w in zip(reads, writes):
        r.wait()
        w.start()
    for w in writes:
        w.wait()


def local(tokens, gain, w_codes, w_scales, seq_counts, key_grad):
    rows, D = tokens.shape
    node_count = lax.axis_size("node")
    local_count = lax.axis_size("local")
    Z = node_count // 2
    inverse = 1.0 / math.sqrt(rows * node_count * local_count)
    hbm = pl.BlockSpec(memory_space=pl.ANY)
    dma = pltpu.SemaphoreType.DMA
    hz = Z // 2

    def ring(n, *inner):
        return [pltpu.VMEM((*m, *inner, 16, HALF), BF16) for m in ((n // 2,), (n // 2,), (2, n))]

    outs = pl.pallas_call(
        functools.partial(kernel, Z, inverse),
        out_shape=(
            jax.ShapeDtypeStruct((rows, 2 * HALF), BF16),
            jax.ShapeDtypeStruct((rows, D), BF16),
            jax.ShapeDtypeStruct((8, 2 * HALF), F32),
            jax.ShapeDtypeStruct((2 * Z, 128), F32),
        ),
        in_specs=[pl.BlockSpec(memory_space=pltpu.SMEM)] + [hbm] * 5,
        out_specs=(hbm,) * 4,
        scratch_shapes=[
            pltpu.VMEM((rows, D), BF16),
            pltpu.VMEM((rows, 2 * HALF), BF16),
            pltpu.VMEM(w_codes.shape, BF16),
            pltpu.VMEM(w_scales.shape, BF16),
            pltpu.VMEM((D // 128, 128), F32),
            pltpu.VMEM((rows, 2 * HALF), BF16),
            pltpu.VMEM((rows, D), BF16),
            pltpu.VMEM((8, 2 * HALF), F32),
            pltpu.VMEM((2 * Z, 128), F32),
            pltpu.VMEM((2, 8, HALF), F32),
            pltpu.VMEM((2, Z, 2, 4, 2, 16, HALF), BF16),
            pltpu.VMEM((rows, 2 * HALF), BF16),
            pltpu.VMEM((2, Z, 2, 4, 2, 16, HALF), BF16),
            pltpu.VMEM((Z, 2, 4, 2, 16, HALF), BF16),
            pltpu.VMEM((16, HALF), F32),
            pltpu.VMEM((8, HALF), F32),
            *ring(hz, 2, 2),
            *ring(hz, 4),
            pltpu.VMEM((hz, 2, 2, 16, HALF), BF16),
            pltpu.VMEM((hz, 4, 16, HALF), BF16),
            *ring(hz),
            *ring(hz),
            pltpu.VMEM((Z, 16, HALF), BF16),
            pltpu.VMEM((Z, 16, HALF), BF16),
            pltpu.VMEM((2, 8, HALF), F32),
            pltpu.VMEM((8, HALF), F32),
            pltpu.VMEM((1, Z * 16), F32),
            pltpu.VMEM((Z, 1, Z * 16), F32),
            pltpu.VMEM((Z, 128), F32),
            pltpu.VMEM((4, Z, 128), F32),
            pltpu.VMEM((Z, 128), F32),
            pltpu.VMEM((8, Z, 128), F32),
            dma((6,)),
            dma((4,)),
            dma((12,)),
            dma((12,)),
            dma((D // WIDE,)),
            dma((16,)), dma((8,)),
        ],
        compiler_params=pltpu.CompilerParams(
            collective_id=0, has_side_effects=True, vmem_limit_bytes=VMEM_BYTES
        ),
    )(seq_counts, tokens, key_grad, w_codes, w_scales, gain.reshape(D // 128, 128))
    keys, tig, wg, gg = pl.pallas_call(
        keep,
        out_shape=tuple(jax.ShapeDtypeStruct(o.shape, o.dtype) for o in outs),
        in_specs=[hbm] * 4,
        out_specs=(hbm,) * 4,
        scratch_shapes=[pltpu.VMEM(o.shape, o.dtype) for o in outs] + [dma((7,)), dma((7,))],
        compiler_params=pltpu.CompilerParams(vmem_limit_bytes=VMEM_BYTES),
    )(*outs)
    return keys, tig, wg, gg.reshape(D)


def solution(mesh):
    return jax.shard_map(
        local,
        mesh=mesh,
        in_specs=(
            P(("node", "local"), None),
            P(),
            P(None, ("node", "local"), None),
            P(None, ("node", "local")),
            P(("node", "local")),
            P(("node", "local"), None),
        ),
        out_specs=(
            P(("node", "local"), None),
            P(("node", "local"), None),
            P(("node", "local"), None),
            P(),
        ),
        check_vma=False,
    )
```

```python
import functools
import math

import jax
import jax.numpy as jnp
from jax import lax
from jax.experimental import pallas as pl
from jax.experimental.pallas import tpu as pltpu
from jax.sharding import PartitionSpec as P

SEQ_LEN = 64
HALF = 256
WIDE = 1024
MESH = pl.DeviceIdType.MESH
F32 = jnp.float32
BF16 = jnp.bfloat16
ALL = slice(None)
VMEM_BYTES = 63 << 20


def copy(src, dst, send, recv, dev):
    return pltpu.make_async_remote_copy(
        src_ref=src, dst_ref=dst, send_sem=send, recv_sem=recv, device_id=dev, device_id_type=MESH
    )


def settle(ref, send=None, recv=None, dev=None):
    d = copy(ref, ref, send if recv is None else recv, recv if send is None else send, dev)
    if recv is None:
        d.wait_send()
    else:
        d.wait_recv()


class RingSum:
    def __init__(self, ref, at, first, n, bufs, sems, plus, minus):
        self.ref, self.at, self.first, self.n, self.h = ref, at, first, n, n // 2
        self.a, self.b, self.lr = bufs
        self.send, self.recv, self.dev = *sems, plus
        h = self.h
        near, far = pl.ds(0, h), pl.ds(h, h)

        def one(i, o, part, dst, dev):
            src = ref.at[at(o, pl.ds(first + part.start, h))]
            return copy(src, dst, self.send, self.recv.at[i], dev)

        self.to_a = one(0, 2, near, self.a, plus)
        self.to_b = one(1, 2, far, self.b, minus)
        self.l0 = one(2, 1, near, self.lr.at[0, near], plus)
        self.l1 = one(2, 1, far, self.lr.at[0, far], plus)
        self.r0 = one(2, 3, near, self.lr.at[1, near], minus)
        self.r1 = one(2, 3, far, self.lr.at[1, far], minus)

    def start(self):
        for d in (self.to_a, self.to_b, self.l1, self.r0):
            d.start()

    def add(self, o, base, buf):
        def body(k, carry):
            i = self.at(o, self.first + base + k)
            self.ref[i] = (self.ref[i].astype(F32) + buf[k].astype(F32)).astype(BF16)
            return carry

        lax.fori_loop(0, self.h, body, 0)

    def forward(self):
        self.to_a.wait_recv()
        self.add(1, 0, self.a)
        self.l0.start()
        self.to_b.wait_recv()
        self.add(3, self.h, self.b)
        self.r1.start()

    def finish(self, dst, dst_first):
        settle(self.lr, recv=self.recv.at[2], dev=self.dev)

        def body(k, carry):
            own = self.ref[self.at(0, self.first + k)].astype(F32)
            total = own + self.lr[0, k].astype(F32) + self.lr[1, k].astype(F32)
            dst[dst_first + k] = total.astype(BF16)
            return carry

        lax.fori_loop(0, self.n, body, 0)

    def sent(self, like):
        settle(like, send=self.send, dev=self.dev)


class RingGather:
    def __init__(self, ref, at, first, n, sems, plus, minus):
        h = n // 2
        whole, near, far = pl.ds(first, n), pl.ds(first, h), pl.ds(first + h, h)
        self.send, self.recv, self.dev = *sems, plus
        self.opposite = ref.at[at(2, whole)]

        def one(i, o, part, dev):
            block = ref.at[at(o, part)]
            return copy(block, block, self.send, self.recv.at[i], dev)

        self.first = (one(0, 0, near, plus), one(1, 0, far, minus), one(3, 0, far, plus), one(3, 0, near, minus))
        self.relay = (one(2, 3, near, plus), one(2, 1, far, minus))
        self.recvs = (one(0, 3, near, plus), one(1, 1, far, minus))

    def start(self):
        for d in self.first:
            d.start()

    def pass_on(self, i):
        self.recvs[i].wait_recv()
        self.relay[i].start()

    def neighbours(self):
        settle(self.opposite, recv=self.recv.at[3], dev=self.dev)

    def finish(self):
        settle(self.opposite, recv=self.recv.at[2], dev=self.dev)

    def sent(self, like):
        settle(like, send=self.send, dev=self.dev)


class Sum:
    def __init__(self, ref, at, n, got, sems, devs):
        self.ref, self.at, self.n, self.got = ref, at, n, got
        self.send, self.recv, self.dev = *sems, devs[1]
        self.copies = [
            copy(ref.at[at(o, pl.ds(0, n))], got.at[o - 1], self.send, self.recv, devs[o]) for o in (2, 1, 3)
        ]

    def start(self):
        for d in self.copies:
            d.start()

    def finish(self, dst, dst_first):
        settle(self.got, recv=self.recv, dev=self.dev)

        def body(k, carry):
            total = self.ref[self.at(0, k)].astype(F32)
            for o in range(3):
                total += self.got[o, k].astype(F32)
            dst[dst_first + k] = total.astype(BF16)
            return carry

        lax.fori_loop(0, self.n, body, 0)

    def sent(self):
        settle(self.got, send=self.send, dev=self.dev)


class Gather:
    def __init__(self, block, sems, devs):
        self.send, self.recv, self.dev = *sems, devs[1]
        self.copies = [copy(block, block, self.send, self.recv, devs[o]) for o in (2, 1, 3)]

    def start(self):
        for d in self.copies:
            d.start()

    def finish(self, like):
        settle(like, recv=self.recv, dev=self.dev)

    def sent(self, like):
        settle(like, send=self.send, dev=self.dev)


def kernel(
    Z, inverse,
    cnt_hbm, tok_hbm, kg_hbm, codes_hbm, scales_hbm, gain_hbm,
    keys_hbm, tig_hbm, wg_hbm, gg_hbm,
    cnt, tok, kg, codes, scales, gain, keys, tig, wg, gg, wsh, W, M, G, GR, W16, wrecv,
    ya, yb, ylr, xa, xb, xlr, Sy, Sx,
    y2, x2, S3, zr, S4, wgr,
    qs, qz, qy, qyr, qx, qxr,
    in_s, out_s, ag_r, rs_r, cr_r, ms_s, ms_r,
):
    rows, D = tok.shape
    gtiles = D // WIDE
    gt = Z // gtiles
    hz = Z // 2
    node = lax.axis_index("node")
    loc = lax.axis_index("local")
    z, xlo = node // 2, node % 2
    y, xhi, c = loc // 4, (loc // 2) % 2, loc % 2
    x = 2 * xhi + xlo
    sib = 1 - c

    def at_z(o):
        return (((z + o) % Z) * 2 + xlo, loc)

    def far_first(i):
        k = (i + 1) // 2
        return Z // 2 + k - 2 * k * (i % 2)

    def at_y(o):
        return (node, ((y + o) % 4) * 4 + xhi * 2 + c)

    def at_x(o, core):
        xx = (x + o) % 4
        return (z * 2 + xx % 2, y * 4 + (xx // 2) * 2 + core)

    at_core = (node, y * 4 + xhi * 2 + sib)
    ys = [(y + o) % 4 for o in range(4)]
    xs = [((x + o) % 4) % 2 for o in range(4)]
    xh = [((x + o) % 4) // 2 for o in range(4)]

    small = ((codes_hbm, codes), (scales_hbm, scales), (gain_hbm, gain), (cnt_hbm, cnt))
    loads = [pltpu.make_async_copy(a, b, in_s.at[i]) for i, (a, b) in enumerate(small)]
    quarter = D // 4
    for i in range(4):
        part = pl.ds(i * quarter, quarter)
        loads.append(pltpu.make_async_copy(tok_hbm.at[:, part], tok.at[:, part], in_s.at[4 + i]))
    loads.append(pltpu.make_async_copy(kg_hbm, kg, in_s.at[8]))
    for d in loads:
        d.start()

    barrier = pltpu.get_barrier_semaphore()

    def greet(dev):
        pl.semaphore_signal(barrier, inc=1, device_id=dev, device_id_type=MESH)

    def hello(o, carry):
        greet(at_z(o))
        return carry

    greet(at_core)
    for o in (1, 2, 3):
        greet(at_y(o))
        greet(at_x(o, c))
        greet(at_x(o, sib))
    lax.fori_loop(1, Z, hello, 0)

    for d in loads[:3]:
        d.wait()
    chip = (node * 16 + loc) // 2
    lane = lax.broadcasted_iota(jnp.int32, (16, 128), 1)
    sub = lax.broadcasted_iota(jnp.int32, (16, 128), 0)
    grow = gain[pl.ds(chip // 8, 1), :]
    g16 = jnp.sum(jnp.where(lane == (chip % 8) * 16 + sub, grow, 0.0), axis=1, keepdims=True)
    eye = lax.broadcasted_iota(jnp.int32, (8, 8), 0) == lax.broadcasted_iota(jnp.int32, (8, 8), 1)
    sc = scales[...].astype(F32)
    for b in range(4):
        col = jnp.sum(jnp.where(eye, sc[b:b + 1, :], 0.0), axis=1, keepdims=True)
        wsh[b // 2, :, (b % 2) * 128:(b % 2 + 1) * 128] = codes[b].astype(F32) * col

    total = jnp.zeros((rows, 128), F32)
    for i in range(4):
        loads[4 + i].wait()

        def square(k, acc):
            t = tok[:, pl.ds(pl.multiple_of(i * quarter + k * 128, 128), 128)].astype(F32)
            return acc + t * t

        total = lax.fori_loop(0, quarter // 128, square, total, unroll=True)
    rs = lax.rsqrt(jnp.sum(total, axis=1, keepdims=True) / D + 1e-05)
    loads[3].wait()
    loads[8].wait()
    live = lax.broadcasted_iota(jnp.int32, (rows, 1), 0) // SEQ_LEN < cnt[...]
    M[...] = (jnp.where(live, kg[...].astype(F32), 0.0) * rs).astype(BF16)

    def core_copy(k):
        part = pl.ds(k * gt, gt)
        return copy(G.at[sib, part], GR.at[part], ms_s.at[0], cr_r.at[k], at_core)

    def grad(k, carry):
        t = tok[:, pl.ds(pl.multiple_of(k * WIDE, WIDE), WIDE)]
        g = lax.dot_general(t, M[...], (((0,), (0,)), ((), ())), preferred_element_type=F32).astype(BF16)
        for h in range(2):
            G[h, pl.ds(k * gt, gt)] = g[:, h * HALF:(h + 1) * HALF].reshape(gt, 2, 4, 2, 16, HALF)
        return carry

    def core_start(k, carry):
        core_copy(k).start()
        return carry

    lax.fori_loop(0, gtiles // 2, grad, 0)
    pl.semaphore_wait(barrier, Z - 1 + 10)
    wx = copy(wsh.at[sib], wrecv, ms_s.at[1], ms_r.at[0], at_core)
    wx.start()
    lax.fori_loop(0, gtiles // 2, core_start, 0)
    lax.fori_loop(gtiles // 2, gtiles, grad, 0)
    lax.fori_loop(gtiles // 2, gtiles, core_start, 0)

    wx.wait_recv()
    own, other = wsh[c], wrecv[...]
    W16[0:8, :] = jnp.where(c == 0, own, other)
    W16[8:16, :] = jnp.where(c == 0, other, own)
    W[c, z, xlo, y, xhi] = (W16[...] * g16).astype(BF16)

    def agz(o, src_z):
        block = W.at[c, src_z, xlo, y, xhi]
        return copy(block, block, ms_s.at[2], ms_r.at[1], at_z(o))

    def agz_start(i, carry):
        agz(far_first(i), z).start()
        return carry

    lax.fori_loop(0, Z - 1, agz_start, 0)

    def core_add(k, carry):
        core_copy(k).wait_recv()
        part = pl.ds(k * gt, gt)
        G[c, part] = (G[c, part].astype(F32) + GR[part].astype(F32)).astype(BF16)
        return carry

    def sems(i, pair, j, n):
        return ms_s.at[i], pair.at[pl.ds(j, n)]

    devs_y = [at_y(o) for o in range(4)]
    devs_x = [at_x(o, c) for o in range(4)]
    low, high = pl.ds(0, hz), pl.ds(hz, hz)
    sum_y = RingSum(
        G, lambda o, p: (c, p, ALL, ys[o]), 0, hz, (ya, yb, ylr), sems(8, rs_r, 0, 3), devs_y[1], devs_y[3]
    )
    sum_x = RingSum(
        G, lambda o, p: (c, p, xs[o], ALL, xh[o]), hz, hz, (xa, xb, xlr), sems(9, rs_r, 3, 3), devs_x[1], devs_x[3]
    )
    sum_yx = Sum(Sy, lambda o, p: (p, xs[o], xh[o]), hz, x2, (ms_s.at[10], rs_r.at[6]), devs_x)
    sum_xy = Sum(Sx, lambda o, p: (p, ys[o]), hz, y2, (ms_s.at[11], rs_r.at[7]), devs_y)
    get_y = Gather(W.at[c, low, xlo, y, xhi], (ms_s.at[12], rs_r.at[8]), devs_y)
    get_x = Gather(W.at[c, high, xlo, y, xhi], (ms_s.at[13], rs_r.at[9]), devs_x)
    get_yx = RingGather(
        W, lambda o, p: (c, p, xs[o], ALL, xh[o]), 0, hz, sems(14, ag_r, 0, 4), devs_x[1], devs_x[3]
    )
    get_xy = RingGather(W, lambda o, p: (c, p, ALL, ys[o]), hz, hz, sems(15, ag_r, 4, 4), devs_y[1], devs_y[3])
    three = W.at[c, low, xlo, pl.ds(0, 3), xhi]

    near, far = pl.ds(0, hz // 2), pl.ds(hz // 2, hz // 2)
    near2, far2 = pl.ds(hz, hz // 2), pl.ds(hz + hz // 2, hz // 2)

    def hand_yx(o, part):
        block = W.at[c, part, xs[o], :, xh[o]]
        copy(block, block, ms_s.at[3], ms_r.at[2], at_core).start()

    def hand_xy(o, part):
        block = W.at[c, part, :, ys[o]]
        copy(block, block, ms_s.at[3], ms_r.at[2], at_core).start()

    lax.fori_loop(0, gtiles // 2, core_add, 0)
    sum_y.start()
    lax.fori_loop(gtiles // 2, gtiles, core_add, 0)
    sum_x.start()

    sum_y.forward()
    sum_x.forward()

    settle(W.at[c, pl.ds(0, Z - 1), xlo, y, xhi], recv=ms_r.at[1], dev=at_core)
    get_y.start()
    get_x.start()
    sum_y.finish(Sy, 0)
    sum_yx.start()
    sum_x.finish(Sx, 0)
    sum_xy.start()
    get_y.finish(three)
    get_yx.start()
    hand_yx(0, low)
    get_x.finish(three)
    get_xy.start()
    hand_xy(0, high)
    sum_yx.finish(S3, 0)
    sum_xy.finish(S3, hz)

    q = jnp.sum(W[c, :, xlo, y, xhi].astype(F32) * S3[...].astype(F32), axis=2, keepdims=True).reshape(Z * 16, 1)
    diag = lax.broadcasted_iota(jnp.int32, (Z * 16, Z * 16), 0) == lax.broadcasted_iota(jnp.int32, (Z * 16, Z * 16), 1)
    qs[...] = jnp.sum(jnp.where(diag, q, 0.0), axis=0, keepdims=True)

    def gqz(o, src_z):
        return copy(qs, qz.at[src_z], ms_s.at[5], ms_r.at[4], at_z(o))

    def gqz_start(i, carry):
        gqz(far_first(i), z).start()
        return carry

    lax.fori_loop(0, Z - 1, gqz_start, 0)

    def rsz(o, dst_z, src_z):
        return copy(S3.at[dst_z], zr.at[src_z], ms_s.at[4], ms_r.at[3], at_z(o))

    def rsz_start(i, carry):
        o = far_first(i)
        rsz(o, (z + o) % Z, z).start()
        return carry

    lax.fori_loop(0, Z - 1, rsz_start, 0)

    for i, o in ((0, 3), (1, 1)):
        get_yx.pass_on(i)
        hand_yx(o, (near, far)[i])
        get_xy.pass_on(i)
        hand_xy(o, (near2, far2)[i])

    def gqz_add(o, acc):
        src = (z + Z - o) % Z
        return acc + qz[src]

    settle(qz.at[pl.ds(0, Z - 1)], recv=ms_r.at[4], dev=at_core)
    qsum = lax.fori_loop(1, Z, gqz_add, qs[...])
    lane = lax.broadcasted_iota(jnp.int32, (Z, Z * 16), 1)
    zrow = lax.broadcasted_iota(jnp.int32, (Z, Z * 16), 0)
    spread = jnp.where((lane >= zrow * 16) & (lane < zrow * 16 + 16), qsum, 0.0)
    src = lax.broadcasted_iota(jnp.int32, (Z * 16, 128), 0)
    to = lax.broadcasted_iota(jnp.int32, (Z * 16, 128), 1)
    place = jnp.where((src & 15) + (y * 2 + xhi) * 16 == to, 1.0, 0.0)
    qy[...] = jnp.dot(spread, place, precision=lax.Precision.HIGHEST, preferred_element_type=F32)
    qys = [copy(qy, qyr.at[o], ms_s.at[6], ms_r.at[6], at_y(o)) for o in (1, 2, 3)]
    for d in qys:
        d.start()

    get_yx.neighbours()
    hand_yx(3, far)
    hand_yx(1, near)
    get_xy.neighbours()
    hand_xy(3, far2)
    hand_xy(1, near2)
    get_yx.finish()
    hand_yx(2, low)
    get_xy.finish()
    hand_xy(2, high)

    span = D // 2

    def project(h):
        def body(k, acc):
            t = tok[:, pl.ds(pl.multiple_of(k * span, span), span)]
            w = W[h, pl.ds(k * hz, hz)].reshape(span, HALF)
            return acc + jnp.dot(t, w, preferred_element_type=F32)

        prod = lax.fori_loop(0, 2, body, jnp.zeros((rows, HALF), F32))
        kf = jnp.where(live, prod * rs, 0.0)
        cols = pl.ds(pl.multiple_of(h * HALF, HALF), HALF)
        keys[:, cols] = kf.astype(BF16)
        return jnp.sum(kf * kg[:, cols].astype(F32), axis=1, keepdims=True)

    mean = project(c)

    settle(W.at[sib], recv=ms_r.at[2], dev=at_core)
    settle(qyr.at[pl.ds(0, 3)], recv=ms_r.at[6], dev=at_core)
    qx[...] = qy[...] + qyr[1] + qyr[2] + qyr[3]
    qxs = [
        copy(qx, qxr.at[2 * o + r], ms_s.at[7], ms_r.at[7], at_x(o, sib if r else c))
        for o in range(4) for r in range(2) if o or r
    ]
    for d in qxs:
        d.start()

    mean += project(sib)
    coef = rs * rs * (mean / D)
    stores = [
        pltpu.make_async_copy(a, b, out_s.at[i])
        for i, (a, b) in enumerate(((keys, keys_hbm), (wg, wg_hbm), (gg, gg_hbm)))
    ]
    stores[0].start()

    def rsz_add(o, acc):
        src = (z + Z - o) % Z
        return acc + zr[src].astype(F32)

    settle(zr.at[pl.ds(0, Z - 1)], recv=ms_r.at[3], dev=at_core)
    s4 = lax.fori_loop(1, Z, rsz_add, S3[z].astype(F32))

    s4 = s4 * (g16 * inverse)
    S4[0] = s4[0:8]
    S4[1] = s4[8:16]
    gx = copy(S4.at[sib], wgr, ms_s.at[1], ms_r.at[5], at_core)
    gx.start()

    def back(k, carry):
        cols = pl.ds(pl.multiple_of(k * WIDE, WIDE), WIDE)
        d = -(tok[:, cols].astype(F32) * coef)
        for h in range(2):
            d += lax.dot_general(
                M[:, h * HALF:(h + 1) * HALF], W[h, pl.ds(k * gt, gt)].reshape(WIDE, HALF),
                (((1,), (1,)), ((), ())), preferred_element_type=F32,
            )
        tig[:, cols] = d.astype(BF16)
        pltpu.make_async_copy(tig.at[:, cols], tig_hbm.at[:, cols], out_s.at[3]).start()
        return carry

    lax.fori_loop(0, gtiles, back, 0)

    gx.wait_recv()
    own, other = S4[c], wgr[...]
    wg[:, 0:HALF] = jnp.where(c == 0, own, other)
    wg[:, HALF:2 * HALF] = jnp.where(c == 0, other, own)
    stores[1].start()
    settle(qxr.at[pl.ds(0, 7)], recv=ms_r.at[7], dev=at_core)
    same = qx[...] + qxr[1] + qxr[4] + qxr[5]
    next_x = (qxr[2] + qxr[3]) + (qxr[6] + qxr[7])
    row = lax.broadcasted_iota(jnp.int32, (2 * Z, Z), 0)
    zcol = lax.broadcasted_iota(jnp.int32, (2 * Z, Z), 1)
    total = sum(
        jnp.dot(
            jnp.where(row == 2 * zcol + p, 1.0, 0.0), v,
            precision=lax.Precision.HIGHEST, preferred_element_type=F32,
        )
        for p, v in ((xlo, same), (1 - xlo, next_x))
    )
    gg[...] = total * inverse / gain[...]
    stores[2].start()

    wx.wait_send()
    gx.wait_send()
    for ref, i in (
        (G.at[sib], 0), (W.at[c, pl.ds(0, Z - 1), xlo, y, xhi], 2), (W.at[c], 3), (S3.at[pl.ds(0, Z - 1)], 4),
        (qz.at[pl.ds(0, Z - 1)], 5), (qyr.at[pl.ds(0, 3)], 6), (qxr.at[pl.ds(0, 7)], 7),
    ):
        settle(ref, send=ms_s.at[i], dev=at_core)
    sum_y.sent(G.at[c, pl.ds(0, hz), :, pl.ds(0, 3)])
    sum_x.sent(G.at[c, pl.ds(0, hz), :, pl.ds(0, 3)])
    sum_yx.sent()
    sum_xy.sent()
    get_y.sent(three)
    get_x.sent(three)
    get_yx.sent(W.at[c, pl.ds(0, hz), :, pl.ds(0, 3)])
    get_xy.sent(W.at[c, pl.ds(0, hz), :, pl.ds(0, 3)])
    pltpu.make_async_copy(tig, tig_hbm, out_s.at[3]).wait()
    for d in stores:
        d.wait()


def keep(keys, tig, wg, gg, keys_out, tig_out, wg_out, gg_out, keys_v, tig_v, wg_v, gg_v, in_s, out_s):
    step = tig.shape[0] // 4
    moves = [(keys, keys_v, keys_out), (wg, wg_v, wg_out), (gg, gg_v, gg_out)]
    for i in range(4):
        part = pl.ds(i * step, step)
        moves.append((tig.at[part], tig_v.at[part], tig_out.at[part]))
    reads = [pltpu.make_async_copy(a, v, in_s.at[i]) for i, (a, v, _) in enumerate(moves)]
    writes = [pltpu.make_async_copy(v, b, out_s.at[i]) for i, (_, v, b) in enumerate(moves)]
    for d in reads:
        d.start()
    for r, w in zip(reads, writes):
        r.wait()
        w.start()
    for w in writes:
        w.wait()


def local(tokens, gain, w_codes, w_scales, seq_counts, key_grad):
    rows, D = tokens.shape
    node_count = lax.axis_size("node")
    local_count = lax.axis_size("local")
    Z = node_count // 2
    inverse = 1.0 / math.sqrt(rows * node_count * local_count)
    hbm = pl.BlockSpec(memory_space=pl.ANY)
    dma = pltpu.SemaphoreType.DMA
    hz = Z // 2

    def ring(n, *inner):
        return [pltpu.VMEM((*m, *inner, 16, HALF), BF16) for m in ((n // 2,), (n // 2,), (2, n))]

    outs = pl.pallas_call(
        functools.partial(kernel, Z, inverse),
        out_shape=(
            jax.ShapeDtypeStruct((rows, 2 * HALF), BF16),
            jax.ShapeDtypeStruct((rows, D), BF16),
            jax.ShapeDtypeStruct((8, 2 * HALF), F32),
            jax.ShapeDtypeStruct((2 * Z, 128), F32),
        ),
        in_specs=[hbm] * 6,
        out_specs=(hbm,) * 4,
        scratch_shapes=[
            pltpu.VMEM((1, 1), jnp.int32),
            pltpu.VMEM((rows, D), BF16),
            pltpu.VMEM((rows, 2 * HALF), BF16),
            pltpu.VMEM(w_codes.shape, BF16),
            pltpu.VMEM(w_scales.shape, BF16),
            pltpu.VMEM((D // 128, 128), F32),
            pltpu.VMEM((rows, 2 * HALF), BF16),
            pltpu.VMEM((rows, D), BF16),
            pltpu.VMEM((8, 2 * HALF), F32),
            pltpu.VMEM((2 * Z, 128), F32),
            pltpu.VMEM((2, 8, HALF), F32),
            pltpu.VMEM((2, Z, 2, 4, 2, 16, HALF), BF16),
            pltpu.VMEM((rows, 2 * HALF), BF16),
            pltpu.VMEM((2, Z, 2, 4, 2, 16, HALF), BF16),
            pltpu.VMEM((Z, 2, 4, 2, 16, HALF), BF16),
            pltpu.VMEM((16, HALF), F32),
            pltpu.VMEM((8, HALF), F32),
            *ring(hz, 2, 2),
            *ring(hz, 4),
            pltpu.VMEM((hz, 2, 2, 16, HALF), BF16),
            pltpu.VMEM((hz, 4, 16, HALF), BF16),
            pltpu.VMEM((3, hz, 16, HALF), BF16),
            pltpu.VMEM((3, hz, 16, HALF), BF16),
            pltpu.VMEM((Z, 16, HALF), BF16),
            pltpu.VMEM((Z, 16, HALF), BF16),
            pltpu.VMEM((2, 8, HALF), F32),
            pltpu.VMEM((8, HALF), F32),
            pltpu.VMEM((1, Z * 16), F32),
            pltpu.VMEM((Z, 1, Z * 16), F32),
            pltpu.VMEM((Z, 128), F32),
            pltpu.VMEM((4, Z, 128), F32),
            pltpu.VMEM((Z, 128), F32),
            pltpu.VMEM((8, Z, 128), F32),
            dma((9,)),
            dma((4,)),
            dma((8,)),
            dma((10,)),
            dma((D // WIDE,)),
            dma((16,)), dma((8,)),
        ],
        compiler_params=pltpu.CompilerParams(
            collective_id=0, has_side_effects=True, vmem_limit_bytes=VMEM_BYTES
        ),
    )(seq_counts.reshape(1, 1), tokens, key_grad, w_codes, w_scales, gain.reshape(D // 128, 128))
    keys, tig, wg, gg = pl.pallas_call(
        keep,
        out_shape=tuple(jax.ShapeDtypeStruct(o.shape, o.dtype) for o in outs),
        in_specs=[hbm] * 4,
        out_specs=(hbm,) * 4,
        scratch_shapes=[pltpu.VMEM(o.shape, o.dtype) for o in outs] + [dma((7,)), dma((7,))],
        compiler_params=pltpu.CompilerParams(vmem_limit_bytes=VMEM_BYTES),
    )(*outs)
    return keys, tig, wg, gg.reshape(D)


def solution(mesh):
    return jax.shard_map(
        local,
        mesh=mesh,
        in_specs=(
            P(("node", "local"), None),
            P(),
            P(None, ("node", "local"), None),
            P(None, ("node", "local")),
            P(("node", "local")),
            P(("node", "local"), None),
        ),
        out_specs=(
            P(("node", "local"), None),
            P(("node", "local"), None),
            P(("node", "local"), None),
            P(),
        ),
        check_vma=False,
    )
```

```python
import functools
import math

import jax
import jax.numpy as jnp
from jax import lax
from jax.experimental import pallas as pl
from jax.experimental.pallas import tpu as pltpu
from jax.sharding import PartitionSpec as P

SEQ_LEN = 64
HALF = 256
WIDE = 1024
MESH = pl.DeviceIdType.MESH
F32 = jnp.float32
BF16 = jnp.bfloat16
ALL = slice(None)
VMEM_BYTES = 63 << 20


def copy(src, dst, send, recv, dev):
    return pltpu.make_async_remote_copy(
        src_ref=src, dst_ref=dst, send_sem=send, recv_sem=recv, device_id=dev, device_id_type=MESH
    )


def settle(ref, send=None, recv=None, dev=None):
    d = copy(ref, ref, send if recv is None else recv, recv if send is None else send, dev)
    if recv is None:
        d.wait_send()
    else:
        d.wait_recv()


class RingSum:
    def __init__(self, ref, at, first, n, bufs, sems, plus, minus):
        self.ref, self.at, self.first, self.n, self.h = ref, at, first, n, n // 2
        self.a, self.b, self.lr = bufs
        self.send, self.recv, self.dev = *sems, plus
        h = self.h
        near, far = pl.ds(0, h), pl.ds(h, h)

        def one(i, o, part, dst, dev):
            src = ref.at[at(o, pl.ds(first + part.start, h))]
            return copy(src, dst, self.send, self.recv.at[i], dev)

        self.to_a = one(0, 2, near, self.a, plus)
        self.to_b = one(1, 2, far, self.b, minus)
        self.l0 = one(2, 1, near, self.lr.at[0, near], plus)
        self.l1 = one(2, 1, far, self.lr.at[0, far], plus)
        self.r0 = one(2, 3, near, self.lr.at[1, near], minus)
        self.r1 = one(2, 3, far, self.lr.at[1, far], minus)

    def start(self):
        for d in (self.to_a, self.to_b, self.l1, self.r0):
            d.start()

    def add(self, o, base, buf):
        def body(k, carry):
            i = self.at(o, self.first + base + k)
            self.ref[i] = (self.ref[i].astype(F32) + buf[k].astype(F32)).astype(BF16)
            return carry

        lax.fori_loop(0, self.h, body, 0)

    def forward(self):
        self.to_a.wait_recv()
        self.add(1, 0, self.a)
        self.l0.start()
        self.to_b.wait_recv()
        self.add(3, self.h, self.b)
        self.r1.start()

    def finish(self, dst, dst_first):
        settle(self.lr, recv=self.recv.at[2], dev=self.dev)

        def body(k, carry):
            own = self.ref[self.at(0, self.first + k)].astype(F32)
            total = own + self.lr[0, k].astype(F32) + self.lr[1, k].astype(F32)
            dst[dst_first + k] = total.astype(BF16)
            return carry

        lax.fori_loop(0, self.n, body, 0)

    def sent(self, like):
        settle(like, send=self.send, dev=self.dev)


class RingGather:
    def __init__(self, ref, at, first, n, sems, plus, minus):
        h = n // 2
        whole, near, far = pl.ds(first, n), pl.ds(first, h), pl.ds(first + h, h)
        self.send, self.recv, self.dev = *sems, plus
        self.opposite = ref.at[at(2, whole)]

        def one(i, o, part, dev):
            block = ref.at[at(o, part)]
            return copy(block, block, self.send, self.recv.at[i], dev)

        self.first = (one(0, 0, near, plus), one(1, 0, far, minus), one(3, 0, far, plus), one(3, 0, near, minus))
        self.relay = (one(2, 3, near, plus), one(2, 1, far, minus))
        self.recvs = (one(0, 3, near, plus), one(1, 1, far, minus))

    def start(self):
        for d in self.first:
            d.start()

    def pass_on(self, i):
        self.recvs[i].wait_recv()
        self.relay[i].start()

    def neighbours(self):
        settle(self.opposite, recv=self.recv.at[3], dev=self.dev)

    def finish(self):
        settle(self.opposite, recv=self.recv.at[2], dev=self.dev)

    def sent(self, like):
        settle(like, send=self.send, dev=self.dev)


class Sum:
    def __init__(self, ref, at, n, got, sems, devs):
        self.ref, self.at, self.n, self.got = ref, at, n, got
        self.send, self.recv, self.dev = *sems, devs[1]
        self.copies = [
            copy(ref.at[at(o, pl.ds(0, n))], got.at[o - 1], self.send, self.recv, devs[o]) for o in (2, 1, 3)
        ]

    def start(self):
        for d in self.copies:
            d.start()

    def finish(self, dst, dst_first):
        settle(self.got, recv=self.recv, dev=self.dev)

        def body(k, carry):
            total = self.ref[self.at(0, k)].astype(F32)
            for o in range(3):
                total += self.got[o, k].astype(F32)
            dst[dst_first + k] = total.astype(BF16)
            return carry

        lax.fori_loop(0, self.n, body, 0)

    def sent(self):
        settle(self.got, send=self.send, dev=self.dev)


class Gather:
    def __init__(self, block, sems, devs):
        self.send, self.recv, self.dev = *sems, devs[1]
        self.copies = [copy(block, block, self.send, self.recv, devs[o]) for o in (2, 1, 3)]

    def start(self):
        for d in self.copies:
            d.start()

    def finish(self, like):
        settle(like, recv=self.recv, dev=self.dev)

    def sent(self, like):
        settle(like, send=self.send, dev=self.dev)


def kernel(
    Z, inverse,
    cnt_hbm, tok_hbm, kg_hbm, codes_hbm, scales_hbm, gain_hbm,
    keys_hbm, tig_hbm, wg_hbm, gg_hbm,
    cnt, tok, kg, codes, scales, gain, keys, tig, wg, gg, wsh, W, M, G, GR, W16, wrecv, wother,
    ya, yb, ylr, xa, xb, xlr, Sy, Sx,
    y2, x2, S3, zr, S4, wgr,
    qs, qz, qy, qyr, qx, qxr,
    met, in_s, out_s, ag_r, rs_r, cr_r, ms_s, ms_r,
):
    rows, D = tok.shape
    gtiles = D // WIDE
    gt = Z // gtiles
    hz = Z // 2
    node = lax.axis_index("node")
    loc = lax.axis_index("local")
    z, xlo = node // 2, node % 2
    y, xhi, c = loc // 4, (loc // 2) % 2, loc % 2
    x = 2 * xhi + xlo
    sib = 1 - c

    def at_z(o):
        return (((z + o) % Z) * 2 + xlo, loc)

    def far_first(i):
        k = (i + 1) // 2
        return Z // 2 + k - 2 * k * (i % 2)

    def at_y(o):
        return (node, ((y + o) % 4) * 4 + xhi * 2 + c)

    def at_x(o, core):
        xx = (x + o) % 4
        return (z * 2 + xx % 2, y * 4 + (xx // 2) * 2 + core)

    at_core = (node, y * 4 + xhi * 2 + sib)
    ys = [(y + o) % 4 for o in range(4)]
    xs = [((x + o) % 4) % 2 for o in range(4)]
    xh = [((x + o) % 4) // 2 for o in range(4)]

    small = ((codes_hbm, codes), (scales_hbm, scales), (gain_hbm, gain), (cnt_hbm, cnt))
    loads = [pltpu.make_async_copy(a, b, in_s.at[i]) for i, (a, b) in enumerate(small)]
    quarter = D // 4
    for i in range(4):
        part = pl.ds(i * quarter, quarter)
        loads.append(pltpu.make_async_copy(tok_hbm.at[:, part], tok.at[:, part], in_s.at[4 + i]))
    loads.append(pltpu.make_async_copy(kg_hbm, kg, in_s.at[8]))
    for d in loads:
        d.start()

    barrier = pltpu.get_barrier_semaphore()

    def greet(dev):
        pl.semaphore_signal(barrier, inc=1, device_id=dev, device_id_type=MESH)

    def hello(i, carry):
        greet((((z + far_first(i)) % Z) * 2 + xlo, y * 4 + xhi * 2 + 1))
        return carry

    lax.fori_loop(0, Z - 1, hello, 0)
    for o in (1, 2, 3):
        greet((node, ((y + o) % 4) * 4 + xhi * 2))
        greet(at_x(o, 0))

    @pl.when(c == 1)
    def _():
        greet(at_core)

    for d in loads[:3]:
        d.wait()
    chip = (node * 16 + loc) // 2
    lane = lax.broadcasted_iota(jnp.int32, (16, 128), 1)
    sub = lax.broadcasted_iota(jnp.int32, (16, 128), 0)
    grow = gain[pl.ds(chip // 8, 1), :]
    g16 = jnp.sum(jnp.where(lane == (chip % 8) * 16 + sub, grow, 0.0), axis=1, keepdims=True)
    eye = lax.broadcasted_iota(jnp.int32, (8, 8), 0) == lax.broadcasted_iota(jnp.int32, (8, 8), 1)
    sc = scales[...].astype(F32)
    for b in range(4):
        col = jnp.sum(jnp.where(eye, sc[b:b + 1, :], 0.0), axis=1, keepdims=True)
        wsh[b // 2, :, (b % 2) * 128:(b % 2 + 1) * 128] = codes[b].astype(F32) * col

    total = jnp.zeros((rows, 128), F32)
    for i in range(4):
        loads[4 + i].wait()

        def square(k, acc):
            t = tok[:, pl.ds(pl.multiple_of(i * quarter + k * 128, 128), 128)].astype(F32)
            return acc + t * t

        total = lax.fori_loop(0, quarter // 128, square, total, unroll=True)
    rs = lax.rsqrt(jnp.sum(total, axis=1, keepdims=True) / D + 1e-05)
    loads[3].wait()
    loads[8].wait()
    live = lax.broadcasted_iota(jnp.int32, (rows, 1), 0) // SEQ_LEN < cnt[...]
    M[...] = (jnp.where(live, kg[...].astype(F32), 0.0) * rs).astype(BF16)

    def core_copy(k):
        part = pl.ds(k * gt, gt)
        return copy(G.at[sib, part], GR.at[part], ms_s.at[0], cr_r.at[k], at_core)

    def grad(k, carry):
        t = tok[:, pl.ds(pl.multiple_of(k * WIDE, WIDE), WIDE)]
        g = lax.dot_general(t, M[...], (((0,), (0,)), ((), ())), preferred_element_type=F32).astype(BF16)
        for h in range(2):
            G[h, pl.ds(k * gt, gt)] = g[:, h * HALF:(h + 1) * HALF].reshape(gt, 2, 4, 2, 16, HALF)
        return carry

    def core_start(k, carry):
        core_copy(k).start()
        return carry

    lax.fori_loop(0, gtiles // 2, grad, 0)

    @pl.when(c == 0)
    def _():
        pl.semaphore_wait(barrier, 13)
        pl.semaphore_signal(met.at[0], inc=1, device_id=at_core, device_id_type=MESH)

    @pl.when(c == 1)
    def _():
        pl.semaphore_wait(met.at[0], 1)

    wx = copy(wsh, wrecv, ms_s.at[1], ms_r.at[0], at_core)
    wx.start()
    lax.fori_loop(0, gtiles // 2, core_start, 0)
    lax.fori_loop(gtiles // 2, gtiles, grad, 0)
    lax.fori_loop(gtiles // 2, gtiles, core_start, 0)

    wx.wait_recv()

    def rows16(h):
        own, other = wsh[h], wrecv[h]
        W16[0:8, :] = jnp.where(c == 0, own, other)
        W16[8:16, :] = jnp.where(c == 0, other, own)
        return (W16[...] * g16).astype(BF16)

    W[c, z, xlo, y, xhi] = rows16(c)

    def agz(o):
        zz = (z + o) % Z
        place = (z, xlo, y, xhi)
        return tuple(
            copy(src, W.at[h, *place], ms_s.at[2], ms_r.at[1], (zz * 2 + xlo, y * 4 + xhi * 2 + h))
            for h, src in ((1, W.at[1, *place]), (0, wother))
        )

    @pl.when(c == 1)
    def _():
        wother[...] = rows16(0)
        pl.semaphore_wait(barrier, 2 * (Z - 1))
        pl.semaphore_signal(met.at[1], inc=1, device_id=at_core, device_id_type=MESH)

        def agz_start(i, carry):
            for d in agz(far_first(i)):
                d.start()
            return carry

        lax.fori_loop(0, Z - 1, agz_start, 0)

    def core_add(k, carry):
        core_copy(k).wait_recv()
        part = pl.ds(k * gt, gt)
        G[c, part] = (G[c, part].astype(F32) + GR[part].astype(F32)).astype(BF16)
        return carry

    def sems(i, pair, j, n):
        return ms_s.at[i], pair.at[pl.ds(j, n)]

    devs_y = [at_y(o) for o in range(4)]
    devs_x = [at_x(o, c) for o in range(4)]
    low, high = pl.ds(0, hz), pl.ds(hz, hz)
    sum_y = RingSum(
        G, lambda o, p: (c, p, ALL, ys[o]), 0, hz, (ya, yb, ylr), sems(8, rs_r, 0, 3), devs_y[1], devs_y[3]
    )
    sum_x = RingSum(
        G, lambda o, p: (c, p, xs[o], ALL, xh[o]), hz, hz, (xa, xb, xlr), sems(9, rs_r, 3, 3), devs_x[1], devs_x[3]
    )
    sum_yx = Sum(Sy, lambda o, p: (p, xs[o], xh[o]), hz, x2, (ms_s.at[10], rs_r.at[6]), devs_x)
    sum_xy = Sum(Sx, lambda o, p: (p, ys[o]), hz, y2, (ms_s.at[11], rs_r.at[7]), devs_y)
    get_y = Gather(W.at[c, low, xlo, y, xhi], (ms_s.at[12], rs_r.at[8]), devs_y)
    get_x = Gather(W.at[c, high, xlo, y, xhi], (ms_s.at[13], rs_r.at[9]), devs_x)
    get_yx = RingGather(
        W, lambda o, p: (c, p, xs[o], ALL, xh[o]), 0, hz, sems(14, ag_r, 0, 4), devs_x[1], devs_x[3]
    )
    get_xy = RingGather(W, lambda o, p: (c, p, ALL, ys[o]), hz, hz, sems(15, ag_r, 4, 4), devs_y[1], devs_y[3])
    three = W.at[c, low, xlo, pl.ds(0, 3), xhi]

    near, far = pl.ds(0, hz // 2), pl.ds(hz // 2, hz // 2)
    near2, far2 = pl.ds(hz, hz // 2), pl.ds(hz + hz // 2, hz // 2)

    def hand_yx(o, part):
        block = W.at[c, part, xs[o], :, xh[o]]
        copy(block, block, ms_s.at[3], ms_r.at[2], at_core).start()

    def hand_xy(o, part):
        block = W.at[c, part, :, ys[o]]
        copy(block, block, ms_s.at[3], ms_r.at[2], at_core).start()

    lax.fori_loop(0, gtiles // 2, core_add, 0)
    sum_y.start()
    lax.fori_loop(gtiles // 2, gtiles, core_add, 0)
    sum_x.start()

    sum_y.forward()
    sum_x.forward()

    sum_y.finish(Sy, 0)
    sum_yx.start()
    sum_x.finish(Sx, 0)
    sum_xy.start()
    settle(W.at[c, pl.ds(0, Z - 1), xlo, y, xhi], recv=ms_r.at[1], dev=at_core)
    get_y.start()
    get_x.start()
    sum_yx.finish(S3, 0)
    sum_xy.finish(S3, hz)

    q = jnp.sum(W[c, :, xlo, y, xhi].astype(F32) * S3[...].astype(F32), axis=2, keepdims=True).reshape(Z * 16, 1)
    diag = lax.broadcasted_iota(jnp.int32, (Z * 16, Z * 16), 0) == lax.broadcasted_iota(jnp.int32, (Z * 16, Z * 16), 1)
    qs[...] = jnp.sum(jnp.where(diag, q, 0.0), axis=0, keepdims=True)

    def gqz(o, src_z):
        return copy(qs, qz.at[src_z], ms_s.at[5], ms_r.at[4], at_z(o))

    def gqz_start(i, carry):
        gqz(far_first(i), z).start()
        return carry

    @pl.when(c == 0)
    def _():
        pl.semaphore_wait(met.at[1], 1)

    lax.fori_loop(0, Z - 1, gqz_start, 0)

    get_y.finish(three)
    get_yx.start()
    hand_yx(0, low)
    get_x.finish(three)
    get_xy.start()
    hand_xy(0, high)
    def rsz(o, dst_z, src_z):
        return copy(S3.at[dst_z], zr.at[src_z], ms_s.at[4], ms_r.at[3], at_z(o))

    def rsz_start(i, carry):
        o = far_first(i)
        rsz(o, (z + o) % Z, z).start()
        return carry

    lax.fori_loop(0, Z - 1, rsz_start, 0)

    for i, o in ((0, 3), (1, 1)):
        get_yx.pass_on(i)
        hand_yx(o, (near, far)[i])
        get_xy.pass_on(i)
        hand_xy(o, (near2, far2)[i])

    get_yx.neighbours()
    hand_yx(3, far)
    hand_yx(1, near)
    get_xy.neighbours()
    hand_xy(3, far2)
    hand_xy(1, near2)

    def gqz_add(o, acc):
        src = (z + Z - o) % Z
        return acc + qz[src]

    settle(qz.at[pl.ds(0, Z - 1)], recv=ms_r.at[4], dev=at_core)
    qsum = lax.fori_loop(1, Z, gqz_add, qs[...])
    lane = lax.broadcasted_iota(jnp.int32, (Z, Z * 16), 1)
    zrow = lax.broadcasted_iota(jnp.int32, (Z, Z * 16), 0)
    spread = jnp.where((lane >= zrow * 16) & (lane < zrow * 16 + 16), qsum, 0.0)
    src = lax.broadcasted_iota(jnp.int32, (Z * 16, 128), 0)
    to = lax.broadcasted_iota(jnp.int32, (Z * 16, 128), 1)
    place = jnp.where((src & 15) + (y * 2 + xhi) * 16 == to, 1.0, 0.0)
    qy[...] = jnp.dot(spread, place, precision=lax.Precision.HIGHEST, preferred_element_type=F32)
    qys = [copy(qy, qyr.at[o], ms_s.at[6], ms_r.at[6], at_y(o)) for o in (1, 2, 3)]
    for d in qys:
        d.start()

    get_yx.finish()
    hand_yx(2, low)
    get_xy.finish()
    hand_xy(2, high)

    span = D // 2

    def project(h):
        def body(k, acc):
            t = tok[:, pl.ds(pl.multiple_of(k * span, span), span)]
            w = W[h, pl.ds(k * hz, hz)].reshape(span, HALF)
            return acc + jnp.dot(t, w, preferred_element_type=F32)

        prod = lax.fori_loop(0, 2, body, jnp.zeros((rows, HALF), F32))
        kf = jnp.where(live, prod * rs, 0.0)
        cols = pl.ds(pl.multiple_of(h * HALF, HALF), HALF)
        keys[:, cols] = kf.astype(BF16)
        return jnp.sum(kf * kg[:, cols].astype(F32), axis=1, keepdims=True)

    mean = project(c)

    settle(qyr.at[pl.ds(0, 3)], recv=ms_r.at[6], dev=at_core)
    qx[...] = qy[...] + qyr[1] + qyr[2] + qyr[3]
    qxs = [
        copy(qx, qxr.at[2 * o + r], ms_s.at[7], ms_r.at[7], at_x(o, sib if r else c))
        for o in range(4) for r in range(2) if o or r
    ]
    for d in qxs:
        d.start()

    def rsz_add(o, acc):
        src = (z + Z - o) % Z
        return acc + zr[src].astype(F32)

    settle(zr.at[pl.ds(0, Z - 1)], recv=ms_r.at[3], dev=at_core)
    s4 = lax.fori_loop(1, Z, rsz_add, S3[z].astype(F32))

    s4 = s4 * (g16 * inverse)
    S4[0] = s4[0:8]
    S4[1] = s4[8:16]
    gx = copy(S4.at[sib], wgr, ms_s.at[1], ms_r.at[5], at_core)
    gx.start()

    settle(W.at[sib], recv=ms_r.at[2], dev=at_core)
    mean += project(sib)
    coef = rs * rs * (mean / D)
    stores = [
        pltpu.make_async_copy(a, b, out_s.at[i])
        for i, (a, b) in enumerate(((keys, keys_hbm), (wg, wg_hbm), (gg, gg_hbm)))
    ]
    stores[0].start()

    def back(k, carry):
        cols = pl.ds(pl.multiple_of(k * WIDE, WIDE), WIDE)
        d = -(tok[:, cols].astype(F32) * coef)
        for h in range(2):
            d += lax.dot_general(
                M[:, h * HALF:(h + 1) * HALF], W[h, pl.ds(k * gt, gt)].reshape(WIDE, HALF),
                (((1,), (1,)), ((), ())), preferred_element_type=F32,
            )
        tig[:, cols] = d.astype(BF16)
        pltpu.make_async_copy(tig.at[:, cols], tig_hbm.at[:, cols], out_s.at[3]).start()
        return carry

    lax.fori_loop(0, gtiles, back, 0)

    gx.wait_recv()
    own, other = S4[c], wgr[...]
    wg[:, 0:HALF] = jnp.where(c == 0, own, other)
    wg[:, HALF:2 * HALF] = jnp.where(c == 0, other, own)
    stores[1].start()
    settle(qxr.at[pl.ds(0, 7)], recv=ms_r.at[7], dev=at_core)
    same = qx[...] + qxr[1] + qxr[4] + qxr[5]
    next_x = (qxr[2] + qxr[3]) + (qxr[6] + qxr[7])
    row = lax.broadcasted_iota(jnp.int32, (2 * Z, Z), 0)
    zcol = lax.broadcasted_iota(jnp.int32, (2 * Z, Z), 1)
    total = sum(
        jnp.dot(
            jnp.where(row == 2 * zcol + p, 1.0, 0.0), v,
            precision=lax.Precision.HIGHEST, preferred_element_type=F32,
        )
        for p, v in ((xlo, same), (1 - xlo, next_x))
    )
    gg[...] = total * inverse / gain[...]
    stores[2].start()

    wx.wait_send()
    gx.wait_send()
    for ref, i in (
        (G.at[sib], 0), (W.at[c], 3), (S3.at[pl.ds(0, Z - 1)], 4),
        (qz.at[pl.ds(0, Z - 1)], 5), (qyr.at[pl.ds(0, 3)], 6), (qxr.at[pl.ds(0, 7)], 7),
    ):
        settle(ref, send=ms_s.at[i], dev=at_core)

    @pl.when(c == 1)
    def _():
        settle(W.at[:, pl.ds(0, Z - 1), xlo, y, xhi], send=ms_s.at[2], dev=at_core)

    sum_y.sent(G.at[c, pl.ds(0, hz), :, pl.ds(0, 3)])
    sum_x.sent(G.at[c, pl.ds(0, hz), :, pl.ds(0, 3)])
    sum_yx.sent()
    sum_xy.sent()
    get_y.sent(three)
    get_x.sent(three)
    get_yx.sent(W.at[c, pl.ds(0, hz), :, pl.ds(0, 3)])
    get_xy.sent(W.at[c, pl.ds(0, hz), :, pl.ds(0, 3)])
    pltpu.make_async_copy(tig, tig_hbm, out_s.at[3]).wait()
    for d in stores:
        d.wait()


def keep(keys, tig, wg, gg, keys_out, tig_out, wg_out, gg_out, keys_v, tig_v, wg_v, gg_v, in_s, out_s):
    step = tig.shape[0] // 4
    moves = [(keys, keys_v, keys_out), (wg, wg_v, wg_out), (gg, gg_v, gg_out)]
    for i in range(4):
        part = pl.ds(i * step, step)
        moves.append((tig.at[part], tig_v.at[part], tig_out.at[part]))
    reads = [pltpu.make_async_copy(a, v, in_s.at[i]) for i, (a, v, _) in enumerate(moves)]
    writes = [pltpu.make_async_copy(v, b, out_s.at[i]) for i, (_, v, b) in enumerate(moves)]
    for d in reads:
        d.start()
    for r, w in zip(reads, writes):
        r.wait()
        w.start()
    for w in writes:
        w.wait()


def local(tokens, gain, w_codes, w_scales, seq_counts, key_grad):
    rows, D = tokens.shape
    node_count = lax.axis_size("node")
    local_count = lax.axis_size("local")
    Z = node_count // 2
    inverse = 1.0 / math.sqrt(rows * node_count * local_count)
    hbm = pl.BlockSpec(memory_space=pl.ANY)
    dma = pltpu.SemaphoreType.DMA
    hz = Z // 2

    def ring(n, *inner):
        return [pltpu.VMEM((*m, *inner, 16, HALF), BF16) for m in ((n // 2,), (n // 2,), (2, n))]

    outs = pl.pallas_call(
        functools.partial(kernel, Z, inverse),
        out_shape=(
            jax.ShapeDtypeStruct((rows, 2 * HALF), BF16),
            jax.ShapeDtypeStruct((rows, D), BF16),
            jax.ShapeDtypeStruct((8, 2 * HALF), F32),
            jax.ShapeDtypeStruct((2 * Z, 128), F32),
        ),
        in_specs=[hbm] * 6,
        out_specs=(hbm,) * 4,
        scratch_shapes=[
            pltpu.VMEM((1, 1), jnp.int32),
            pltpu.VMEM((rows, D), BF16),
            pltpu.VMEM((rows, 2 * HALF), BF16),
            pltpu.VMEM(w_codes.shape, BF16),
            pltpu.VMEM(w_scales.shape, BF16),
            pltpu.VMEM((D // 128, 128), F32),
            pltpu.VMEM((rows, 2 * HALF), BF16),
            pltpu.VMEM((rows, D), BF16),
            pltpu.VMEM((8, 2 * HALF), F32),
            pltpu.VMEM((2 * Z, 128), F32),
            pltpu.VMEM((2, 8, HALF), F32),
            pltpu.VMEM((2, Z, 2, 4, 2, 16, HALF), BF16),
            pltpu.VMEM((rows, 2 * HALF), BF16),
            pltpu.VMEM((2, Z, 2, 4, 2, 16, HALF), BF16),
            pltpu.VMEM((Z, 2, 4, 2, 16, HALF), BF16),
            pltpu.VMEM((16, HALF), F32),
            pltpu.VMEM((2, 8, HALF), F32),
            pltpu.VMEM((16, HALF), BF16),
            *ring(hz, 2, 2),
            *ring(hz, 4),
            pltpu.VMEM((hz, 2, 2, 16, HALF), BF16),
            pltpu.VMEM((hz, 4, 16, HALF), BF16),
            pltpu.VMEM((3, hz, 16, HALF), BF16),
            pltpu.VMEM((3, hz, 16, HALF), BF16),
            pltpu.VMEM((Z, 16, HALF), BF16),
            pltpu.VMEM((Z, 16, HALF), BF16),
            pltpu.VMEM((2, 8, HALF), F32),
            pltpu.VMEM((8, HALF), F32),
            pltpu.VMEM((1, Z * 16), F32),
            pltpu.VMEM((Z, 1, Z * 16), F32),
            pltpu.VMEM((Z, 128), F32),
            pltpu.VMEM((4, Z, 128), F32),
            pltpu.VMEM((Z, 128), F32),
            pltpu.VMEM((8, Z, 128), F32),
            pltpu.SemaphoreType.REGULAR((2,)),
            dma((9,)),
            dma((4,)),
            dma((8,)),
            dma((10,)),
            dma((D // WIDE,)),
            dma((16,)), dma((8,)),
        ],
        compiler_params=pltpu.CompilerParams(
            collective_id=0, has_side_effects=True, vmem_limit_bytes=VMEM_BYTES
        ),
    )(seq_counts.reshape(1, 1), tokens, key_grad, w_codes, w_scales, gain.reshape(D // 128, 128))
    keys, tig, wg, gg = pl.pallas_call(
        keep,
        out_shape=tuple(jax.ShapeDtypeStruct(o.shape, o.dtype) for o in outs),
        in_specs=[hbm] * 4,
        out_specs=(hbm,) * 4,
        scratch_shapes=[pltpu.VMEM(o.shape, o.dtype) for o in outs] + [dma((7,)), dma((7,))],
        compiler_params=pltpu.CompilerParams(vmem_limit_bytes=VMEM_BYTES),
    )(*outs)
    return keys, tig, wg, gg.reshape(D)


def solution(mesh):
    return jax.shard_map(
        local,
        mesh=mesh,
        in_specs=(
            P(("node", "local"), None),
            P(),
            P(None, ("node", "local"), None),
            P(None, ("node", "local")),
            P(("node", "local")),
            P(("node", "local"), None),
        ),
        out_specs=(
            P(("node", "local"), None),
            P(("node", "local"), None),
            P(("node", "local"), None),
            P(),
        ),
        check_vma=False,
    )
```

```python
import functools
import math

import jax
import jax.numpy as jnp
from jax import lax
from jax.experimental import pallas as pl
from jax.experimental.pallas import tpu as pltpu
from jax.sharding import PartitionSpec as P

SEQ_LEN = 64
HALF = 256
WIDE = 1024
MESH = pl.DeviceIdType.MESH
F32 = jnp.float32
BF16 = jnp.bfloat16
ALL = slice(None)
VMEM_BYTES = 63 << 20


def copy(src, dst, send, recv, dev):
    return pltpu.make_async_remote_copy(
        src_ref=src, dst_ref=dst, send_sem=send, recv_sem=recv, device_id=dev, device_id_type=MESH
    )


def settle(ref, send=None, recv=None, dev=None):
    d = copy(ref, ref, send if recv is None else recv, recv if send is None else send, dev)
    if recv is None:
        d.wait_send()
    else:
        d.wait_recv()


class RingSum:
    def __init__(self, ref, at, first, n, bufs, sems, plus, minus):
        self.ref, self.at, self.first, self.n, self.h = ref, at, first, n, n // 2
        self.a, self.b, self.lr = bufs
        self.send, self.recv, self.dev = *sems, plus
        h = self.h
        near, far = pl.ds(0, h), pl.ds(h, h)

        def one(i, o, part, dst, dev):
            src = ref.at[at(o, pl.ds(first + part.start, h))]
            return copy(src, dst, self.send, self.recv.at[i], dev)

        self.to_a = one(0, 2, near, self.a, plus)
        self.to_b = one(1, 2, far, self.b, minus)
        self.l0 = one(2, 1, near, self.lr.at[0, near], plus)
        self.l1 = one(2, 1, far, self.lr.at[0, far], plus)
        self.r0 = one(2, 3, near, self.lr.at[1, near], minus)
        self.r1 = one(2, 3, far, self.lr.at[1, far], minus)

    def start(self):
        for d in (self.to_a, self.to_b, self.l1, self.r0):
            d.start()

    def add(self, o, base, buf):
        def body(k, carry):
            i = self.at(o, self.first + base + k)
            self.ref[i] = (self.ref[i].astype(F32) + buf[k].astype(F32)).astype(BF16)
            return carry

        lax.fori_loop(0, self.h, body, 0)

    def forward(self):
        self.to_a.wait_recv()
        self.add(1, 0, self.a)
        self.l0.start()
        self.to_b.wait_recv()
        self.add(3, self.h, self.b)
        self.r1.start()

    def finish(self, dst, dst_first):
        settle(self.lr, recv=self.recv.at[2], dev=self.dev)

        def body(k, carry):
            own = self.ref[self.at(0, self.first + k)].astype(F32)
            total = own + self.lr[0, k].astype(F32) + self.lr[1, k].astype(F32)
            dst[dst_first + k] = total.astype(BF16)
            return carry

        lax.fori_loop(0, self.n, body, 0)

    def sent(self, like):
        settle(like, send=self.send, dev=self.dev)


class RingGather:
    def __init__(self, ref, at, first, n, sems, plus, minus):
        h = n // 2
        whole, near, far = pl.ds(first, n), pl.ds(first, h), pl.ds(first + h, h)
        self.send, self.recv, self.dev = *sems, plus
        self.opposite = ref.at[at(2, whole)]

        def one(i, o, part, dev):
            block = ref.at[at(o, part)]
            return copy(block, block, self.send, self.recv.at[i], dev)

        self.first = (one(0, 0, near, plus), one(1, 0, far, minus), one(3, 0, far, plus), one(3, 0, near, minus))
        self.relay = (one(2, 3, near, plus), one(2, 1, far, minus))
        self.recvs = (one(0, 3, near, plus), one(1, 1, far, minus))

    def start(self):
        for d in self.first:
            d.start()

    def pass_on(self, i):
        self.recvs[i].wait_recv()
        self.relay[i].start()

    def neighbours(self):
        settle(self.opposite, recv=self.recv.at[3], dev=self.dev)

    def finish(self):
        settle(self.opposite, recv=self.recv.at[2], dev=self.dev)

    def sent(self, like):
        settle(like, send=self.send, dev=self.dev)


class Sum:
    def __init__(self, ref, at, n, got, sems, devs):
        self.ref, self.at, self.n, self.got = ref, at, n, got
        self.send, self.recv, self.dev = *sems, devs[1]
        self.copies = [
            copy(ref.at[at(o, pl.ds(0, n))], got.at[o - 1], self.send, self.recv, devs[o]) for o in (2, 1, 3)
        ]

    def start(self):
        for d in self.copies:
            d.start()

    def finish(self, dst, dst_first):
        settle(self.got, recv=self.recv, dev=self.dev)

        def body(k, carry):
            total = self.ref[self.at(0, k)].astype(F32)
            for o in range(3):
                total += self.got[o, k].astype(F32)
            dst[dst_first + k] = total.astype(BF16)
            return carry

        lax.fori_loop(0, self.n, body, 0)

    def sent(self):
        settle(self.got, send=self.send, dev=self.dev)


class Gather:
    def __init__(self, block, sems, devs):
        self.send, self.recv, self.dev = *sems, devs[1]
        self.copies = [copy(block, block, self.send, self.recv, devs[o]) for o in (2, 1, 3)]

    def start(self):
        for d in self.copies:
            d.start()

    def finish(self, like):
        settle(like, recv=self.recv, dev=self.dev)

    def sent(self, like):
        settle(like, send=self.send, dev=self.dev)


def kernel(
    Z, inverse,
    cnt_hbm, tok_hbm, kg_hbm, codes_hbm, scales_hbm, gain_hbm,
    keys_hbm, tig_hbm, wg_hbm, qxr,
    cnt, tok, kg, codes, scales, gain, keys, tig, wsh, W, M, G, GR, W16, wrecv, wother,
    ya, yb, ylr, xa, xb, xlr, Sy, Sx,
    y2, x2, S3, zr, S4,
    qs, qz, qy, qyr, qx,
    met, in_s, out_s, ag_r, rs_r, cr_r, ms_s, ms_r,
):
    rows, D = tok.shape
    gtiles = D // WIDE
    gt = Z // gtiles
    hz = Z // 2
    node = lax.axis_index("node")
    loc = lax.axis_index("local")
    z, xlo = node // 2, node % 2
    y, xhi, c = loc // 4, (loc // 2) % 2, loc % 2
    x = 2 * xhi + xlo
    sib = 1 - c

    def at_z(o):
        return (((z + o) % Z) * 2 + xlo, loc)

    def far_first(i):
        k = (i + 1) // 2
        return Z // 2 + k - 2 * k * (i % 2)

    def at_y(o):
        return (node, ((y + o) % 4) * 4 + xhi * 2 + c)

    def at_x(o, core):
        xx = (x + o) % 4
        return (z * 2 + xx % 2, y * 4 + (xx // 2) * 2 + core)

    at_core = (node, y * 4 + xhi * 2 + sib)
    ys = [(y + o) % 4 for o in range(4)]
    xs = [((x + o) % 4) % 2 for o in range(4)]
    xh = [((x + o) % 4) // 2 for o in range(4)]

    small = ((codes_hbm, codes), (scales_hbm, scales), (gain_hbm, gain), (cnt_hbm, cnt))
    loads = [pltpu.make_async_copy(a, b, in_s.at[i]) for i, (a, b) in enumerate(small)]
    quarter = D // 4
    for i in range(4):
        part = pl.ds(i * quarter, quarter)
        loads.append(pltpu.make_async_copy(tok_hbm.at[:, part], tok.at[:, part], in_s.at[4 + i]))
    loads.append(pltpu.make_async_copy(kg_hbm, kg, in_s.at[8]))
    for d in loads:
        d.start()

    barrier = pltpu.get_barrier_semaphore()

    def greet(dev):
        pl.semaphore_signal(barrier, inc=1, device_id=dev, device_id_type=MESH)

    def hello(i, carry):
        greet((((z + far_first(i)) % Z) * 2 + xlo, y * 4 + xhi * 2 + 1))
        return carry

    lax.fori_loop(0, Z - 1, hello, 0)
    for o in (1, 2, 3):
        greet((node, ((y + o) % 4) * 4 + xhi * 2))
        greet(at_x(o, 0))

    @pl.when(c == 1)
    def _():
        greet(at_core)

    for d in loads[:3]:
        d.wait()
    chip = (node * 16 + loc) // 2
    lane = lax.broadcasted_iota(jnp.int32, (16, 128), 1)
    sub = lax.broadcasted_iota(jnp.int32, (16, 128), 0)
    grow = gain[pl.ds(chip // 8, 1), :]
    g16 = jnp.sum(jnp.where(lane == (chip % 8) * 16 + sub, grow, 0.0), axis=1, keepdims=True)
    eye = lax.broadcasted_iota(jnp.int32, (8, 8), 0) == lax.broadcasted_iota(jnp.int32, (8, 8), 1)
    sc = scales[...].astype(F32)
    for b in range(4):
        col = jnp.sum(jnp.where(eye, sc[b:b + 1, :], 0.0), axis=1, keepdims=True)
        wsh[b // 2, :, (b % 2) * 128:(b % 2 + 1) * 128] = codes[b].astype(F32) * col

    total = jnp.zeros((rows, 128), F32)
    for i in range(4):
        loads[4 + i].wait()

        def square(k, acc):
            t = tok[:, pl.ds(pl.multiple_of(i * quarter + k * 128, 128), 128)].astype(F32)
            return acc + t * t

        total = lax.fori_loop(0, quarter // 128, square, total, unroll=True)
    rs = lax.rsqrt(jnp.sum(total, axis=1, keepdims=True) / D + 1e-05)
    loads[3].wait()
    loads[8].wait()
    live = lax.broadcasted_iota(jnp.int32, (rows, 1), 0) // SEQ_LEN < cnt[0]
    M[...] = (jnp.where(live, kg[...].astype(F32), 0.0) * rs).astype(BF16)

    def core_copy(k):
        part = pl.ds(k * gt, gt)
        return copy(G.at[sib, part], GR.at[part], ms_s.at[0], cr_r.at[k], at_core)

    def grad(k, carry):
        t = tok[:, pl.ds(pl.multiple_of(k * WIDE, WIDE), WIDE)]
        g = lax.dot_general(t, M[...], (((0,), (0,)), ((), ())), preferred_element_type=F32).astype(BF16)
        for h in range(2):
            G[h, pl.ds(k * gt, gt)] = g[:, h * HALF:(h + 1) * HALF].reshape(gt, 2, 4, 2, 16, HALF)
        return carry

    def core_start(k, carry):
        core_copy(k).start()
        return carry

    lax.fori_loop(0, gtiles // 2, grad, 0)

    @pl.when(c == 0)
    def _():
        pl.semaphore_wait(barrier, 13)
        pl.semaphore_signal(met.at[0], inc=1, device_id=at_core, device_id_type=MESH)

    @pl.when(c == 1)
    def _():
        pl.semaphore_wait(met.at[0], 1)

    wx = copy(wsh, wrecv, ms_s.at[1], ms_r.at[0], at_core)
    wx.start()
    lax.fori_loop(0, gtiles // 2, core_start, 0)
    lax.fori_loop(gtiles // 2, gtiles, grad, 0)
    lax.fori_loop(gtiles // 2, gtiles, core_start, 0)

    wx.wait_recv()

    def rows16(h):
        own, other = wsh[h], wrecv[h]
        W16[0:8, :] = jnp.where(c == 0, own, other)
        W16[8:16, :] = jnp.where(c == 0, other, own)
        return (W16[...] * g16).astype(BF16)

    W[c, z, xlo, y, xhi] = rows16(c)

    def agz(o):
        zz = (z + o) % Z
        place = (z, xlo, y, xhi)
        return tuple(
            copy(src, W.at[h, *place], ms_s.at[2], ms_r.at[1], (zz * 2 + xlo, y * 4 + xhi * 2 + h))
            for h, src in ((1, W.at[1, *place]), (0, wother))
        )

    @pl.when(c == 1)
    def _():
        wother[...] = rows16(0)
        pl.semaphore_wait(barrier, 2 * (Z - 1))
        pl.semaphore_signal(met.at[1], inc=1, device_id=at_core, device_id_type=MESH)

        def agz_start(i, carry):
            for d in agz(far_first(i)):
                d.start()
            return carry

        lax.fori_loop(0, Z - 1, agz_start, 0)

    def core_add(k, carry):
        core_copy(k).wait_recv()
        part = pl.ds(k * gt, gt)
        G[c, part] = (G[c, part].astype(F32) + GR[part].astype(F32)).astype(BF16)
        return carry

    def sems(i, pair, j, n):
        return ms_s.at[i], pair.at[pl.ds(j, n)]

    devs_y = [at_y(o) for o in range(4)]
    devs_x = [at_x(o, c) for o in range(4)]
    low, high = pl.ds(0, hz), pl.ds(hz, hz)
    sum_y = RingSum(
        G, lambda o, p: (c, p, ALL, ys[o]), 0, hz, (ya, yb, ylr), sems(8, rs_r, 0, 3), devs_y[1], devs_y[3]
    )
    sum_x = RingSum(
        G, lambda o, p: (c, p, xs[o], ALL, xh[o]), hz, hz, (xa, xb, xlr), sems(9, rs_r, 3, 3), devs_x[1], devs_x[3]
    )
    sum_yx = Sum(Sy, lambda o, p: (p, xs[o], xh[o]), hz, x2, (ms_s.at[10], rs_r.at[6]), devs_x)
    sum_xy = Sum(Sx, lambda o, p: (p, ys[o]), hz, y2, (ms_s.at[11], rs_r.at[7]), devs_y)
    get_y = Gather(W.at[c, low, xlo, y, xhi], (ms_s.at[12], rs_r.at[8]), devs_y)
    get_x = Gather(W.at[c, high, xlo, y, xhi], (ms_s.at[13], rs_r.at[9]), devs_x)
    get_yx = RingGather(
        W, lambda o, p: (c, p, xs[o], ALL, xh[o]), 0, hz, sems(14, ag_r, 0, 4), devs_x[1], devs_x[3]
    )
    get_xy = RingGather(W, lambda o, p: (c, p, ALL, ys[o]), hz, hz, sems(15, ag_r, 4, 4), devs_y[1], devs_y[3])
    three = W.at[c, low, xlo, pl.ds(0, 3), xhi]

    near, far = pl.ds(0, hz // 2), pl.ds(hz // 2, hz // 2)
    near2, far2 = pl.ds(hz, hz // 2), pl.ds(hz + hz // 2, hz // 2)

    def hand_yx(o, part):
        block = W.at[c, part, xs[o], :, xh[o]]
        copy(block, block, ms_s.at[3], ms_r.at[2], at_core).start()

    def hand_xy(o, part):
        block = W.at[c, part, :, ys[o]]
        copy(block, block, ms_s.at[3], ms_r.at[2], at_core).start()

    lax.fori_loop(0, gtiles // 2, core_add, 0)
    sum_y.start()
    lax.fori_loop(gtiles // 2, gtiles, core_add, 0)
    sum_x.start()

    sum_y.forward()
    sum_x.forward()

    sum_y.finish(Sy, 0)
    sum_yx.start()
    sum_x.finish(Sx, 0)
    sum_xy.start()
    settle(W.at[c, pl.ds(0, Z - 1), xlo, y, xhi], recv=ms_r.at[1], dev=at_core)
    get_y.start()
    get_x.start()
    sum_yx.finish(S3, 0)
    sum_xy.finish(S3, hz)

    q = jnp.sum(W[c, :, xlo, y, xhi].astype(F32) * S3[...].astype(F32), axis=2, keepdims=True).reshape(Z * 16, 1)
    diag = lax.broadcasted_iota(jnp.int32, (Z * 16, Z * 16), 0) == lax.broadcasted_iota(jnp.int32, (Z * 16, Z * 16), 1)
    qs[...] = jnp.sum(jnp.where(diag, q, 0.0), axis=0, keepdims=True)

    def gqz(o, src_z):
        return copy(qs, qz.at[src_z], ms_s.at[5], ms_r.at[4], at_z(o))

    def gqz_start(i, carry):
        gqz(far_first(i), z).start()
        return carry

    @pl.when(c == 0)
    def _():
        pl.semaphore_wait(met.at[1], 1)

    lax.fori_loop(0, Z - 1, gqz_start, 0)

    get_y.finish(three)
    get_yx.start()
    hand_yx(0, low)
    get_x.finish(three)
    get_xy.start()
    hand_xy(0, high)
    def rsz(o, dst_z, src_z):
        return copy(S3.at[dst_z], zr.at[src_z], ms_s.at[4], ms_r.at[3], at_z(o))

    def rsz_start(i, carry):
        o = far_first(i)
        rsz(o, (z + o) % Z, z).start()
        return carry

    lax.fori_loop(0, Z - 1, rsz_start, 0)

    for i, o in ((0, 3), (1, 1)):
        get_yx.pass_on(i)
        hand_yx(o, (near, far)[i])
        get_xy.pass_on(i)
        hand_xy(o, (near2, far2)[i])

    get_yx.neighbours()
    hand_yx(3, far)
    hand_yx(1, near)
    get_xy.neighbours()
    hand_xy(3, far2)
    hand_xy(1, near2)

    def gqz_add(o, acc):
        src = (z + Z - o) % Z
        return acc + qz[src]

    settle(qz.at[pl.ds(0, Z - 1)], recv=ms_r.at[4], dev=at_core)
    qsum = lax.fori_loop(1, Z, gqz_add, qs[...])
    lane = lax.broadcasted_iota(jnp.int32, (Z, Z * 16), 1)
    zrow = lax.broadcasted_iota(jnp.int32, (Z, Z * 16), 0)
    spread = jnp.where((lane >= zrow * 16) & (lane < zrow * 16 + 16), qsum, 0.0)
    src = lax.broadcasted_iota(jnp.int32, (Z * 16, 128), 0)
    to = lax.broadcasted_iota(jnp.int32, (Z * 16, 128), 1)
    place = jnp.where((src & 15) + (y * 2 + xhi) * 16 == to, 1.0, 0.0)
    qy[...] = jnp.dot(spread, place, precision=lax.Precision.HIGHEST, preferred_element_type=F32)
    qys = [copy(qy, qyr.at[o], ms_s.at[6], ms_r.at[6], at_y(o)) for o in (1, 2, 3)]
    for d in qys:
        d.start()

    get_yx.finish()
    hand_yx(2, low)
    get_xy.finish()
    hand_xy(2, high)

    span = D // 2

    def project(h):
        def body(k, acc):
            t = tok[:, pl.ds(pl.multiple_of(k * span, span), span)]
            w = W[h, pl.ds(k * hz, hz)].reshape(span, HALF)
            return acc + jnp.dot(t, w, preferred_element_type=F32)

        prod = lax.fori_loop(0, 2, body, jnp.zeros((rows, HALF), F32))
        kf = jnp.where(live, prod * rs, 0.0)
        cols = pl.ds(pl.multiple_of(h * HALF, HALF), HALF)
        keys[:, cols] = kf.astype(BF16)
        return jnp.sum(kf * kg[:, cols].astype(F32), axis=1, keepdims=True)

    mean = project(c)

    settle(W.at[sib], recv=ms_r.at[2], dev=at_core)
    settle(qyr.at[pl.ds(0, 3)], recv=ms_r.at[6], dev=at_core)
    qx[...] = qy[...] + qyr[1] + qyr[2] + qyr[3]
    qxs = [
        copy(qx, qxr.at[2 * o + r], ms_s.at[7], ms_r.at[7], at_x(o, sib if r else c))
        for o in range(4) for r in range(2) if o or r
    ]
    for d in qxs:
        d.start()
    qx_out = pltpu.make_async_copy(qx, qxr.at[0], out_s.at[0])
    qx_out.start()

    mean += project(sib)
    coef = rs * rs * (mean / D)
    keys_out = pltpu.make_async_copy(keys, keys_hbm, out_s.at[2])
    keys_out.start()

    def rsz_add(o, acc):
        src = (z + Z - o) % Z
        return acc + zr[src].astype(F32)

    settle(zr.at[pl.ds(0, Z - 1)], recv=ms_r.at[3], dev=at_core)
    s4 = lax.fori_loop(1, Z, rsz_add, S3[z].astype(F32))

    s4 = s4 * (g16 * inverse)
    S4[0] = s4[0:8]
    S4[1] = s4[8:16]
    columns = wg_hbm.at[:, pl.ds(pl.multiple_of(c * HALF, HALF), HALF)]
    gx = copy(S4.at[sib], columns, ms_s.at[1], ms_r.at[5], at_core)
    gx.start()
    wg_out = pltpu.make_async_copy(S4.at[c], columns, out_s.at[1])
    wg_out.start()

    def back(k, carry):
        cols = pl.ds(pl.multiple_of(k * WIDE, WIDE), WIDE)
        d = -(tok[:, cols].astype(F32) * coef)
        for h in range(2):
            d += lax.dot_general(
                M[:, h * HALF:(h + 1) * HALF], W[h, pl.ds(k * gt, gt)].reshape(WIDE, HALF),
                (((1,), (1,)), ((), ())), preferred_element_type=F32,
            )
        tig[:, cols] = d.astype(BF16)
        pltpu.make_async_copy(tig.at[:, cols], tig_hbm.at[:, cols], out_s.at[3]).start()
        return carry

    lax.fori_loop(0, gtiles, back, 0)

    wx.wait_send()
    for ref, i in (
        (G.at[sib], 0), (W.at[c], 3), (S3.at[pl.ds(0, Z - 1)], 4),
        (qz.at[pl.ds(0, Z - 1)], 5), (qyr.at[pl.ds(0, 3)], 6),
    ):
        settle(ref, send=ms_s.at[i], dev=at_core)

    @pl.when(c == 1)
    def _():
        settle(W.at[:, pl.ds(0, Z - 1), xlo, y, xhi], send=ms_s.at[2], dev=at_core)

    sum_y.sent(G.at[c, pl.ds(0, hz), :, pl.ds(0, 3)])
    sum_x.sent(G.at[c, pl.ds(0, hz), :, pl.ds(0, 3)])
    sum_yx.sent()
    sum_xy.sent()
    get_y.sent(three)
    get_x.sent(three)
    get_yx.sent(W.at[c, pl.ds(0, hz), :, pl.ds(0, 3)])
    get_xy.sent(W.at[c, pl.ds(0, hz), :, pl.ds(0, 3)])

    gx.wait_recv()
    settle(qxr.at[pl.ds(1, 7)], recv=ms_r.at[7], dev=at_core)
    gx.wait_send()
    settle(qxr.at[pl.ds(1, 7)], send=ms_s.at[7], dev=at_core)
    pltpu.make_async_copy(tig, tig_hbm, out_s.at[3]).wait()
    for d in (keys_out, wg_out, qx_out):
        d.wait()


def keep(
    inverse, keys, tig, wg, qxr, gain, keys_out, tig_out, wg_out, gg_out,
    keys_v, tig_v, wg_v, qxr_v, gain_v, gg_v, in_s, out_s,
):
    loads = [pltpu.make_async_copy(a, v, in_s.at[i]) for i, (a, v) in enumerate(((qxr, qxr_v), (gain, gain_v)))]
    step = tig.shape[0] // 8
    moves = []
    for i in range(8):
        part = pl.ds(i * step, step)
        moves.append((tig.at[part], tig_v.at[part], tig_out.at[part]))
    moves += [(keys, keys_v, keys_out), (wg, wg_v, wg_out)]
    reads = [pltpu.make_async_copy(a, v, in_s.at[2 + i]) for i, (a, v, _) in enumerate(moves)]
    writes = [pltpu.make_async_copy(v, b, out_s.at[i]) for i, (_, v, b) in enumerate(moves)]
    for d in loads + reads:
        d.start()
    for r, w in zip(reads[:4], writes[:4]):
        r.wait()
        w.start()
    for d in loads:
        d.wait()
    Z = qxr_v.shape[1]
    xlo = lax.axis_index("node") % 2
    same = qxr_v[0] + qxr_v[1] + qxr_v[4] + qxr_v[5]
    next_x = (qxr_v[2] + qxr_v[3]) + (qxr_v[6] + qxr_v[7])
    row = lax.broadcasted_iota(jnp.int32, (2 * Z, 2 * Z), 0)
    col = lax.broadcasted_iota(jnp.int32, (2 * Z, 2 * Z), 1)
    order = jnp.where(row == jnp.where(col < Z, 2 * col + xlo, 2 * (col - Z) + 1 - xlo), 1.0, 0.0)
    total = jnp.dot(
        order, jnp.concatenate([same, next_x], axis=0),
        precision=lax.Precision.HIGHEST, preferred_element_type=F32,
    )
    gg_v[...] = total * inverse / gain_v[...]
    gg_write = pltpu.make_async_copy(gg_v, gg_out, out_s.at[len(moves)])
    gg_write.start()
    for r, w in zip(reads[4:], writes[4:]):
        r.wait()
        w.start()
    for w in writes:
        w.wait()
    gg_write.wait()


def local(tokens, gain, w_codes, w_scales, seq_counts, key_grad):
    rows, D = tokens.shape
    node_count = lax.axis_size("node")
    local_count = lax.axis_size("local")
    Z = node_count // 2
    inverse = 1.0 / math.sqrt(rows * node_count * local_count)
    hbm = pl.BlockSpec(memory_space=pl.ANY)
    dma = pltpu.SemaphoreType.DMA
    hz = Z // 2

    def ring(n, *inner):
        return [pltpu.VMEM((*m, *inner, 16, HALF), BF16) for m in ((n // 2,), (n // 2,), (2, n))]

    outs = pl.pallas_call(
        functools.partial(kernel, Z, inverse),
        out_shape=(
            jax.ShapeDtypeStruct((rows, 2 * HALF), BF16),
            jax.ShapeDtypeStruct((rows, D), BF16),
            jax.ShapeDtypeStruct((8, 2 * HALF), F32),
            jax.ShapeDtypeStruct((8, Z, 128), F32),
        ),
        in_specs=[pl.BlockSpec(memory_space=pltpu.HBM)] + [hbm] * 5,
        out_specs=(hbm,) * 4,
        scratch_shapes=[
            pltpu.SMEM((1,), jnp.int32),
            pltpu.VMEM((rows, D), BF16),
            pltpu.VMEM((rows, 2 * HALF), BF16),
            pltpu.VMEM(w_codes.shape, BF16),
            pltpu.VMEM(w_scales.shape, BF16),
            pltpu.VMEM((D // 128, 128), F32),
            pltpu.VMEM((rows, 2 * HALF), BF16),
            pltpu.VMEM((rows, D), BF16),
            pltpu.VMEM((2, 8, HALF), F32),
            pltpu.VMEM((2, Z, 2, 4, 2, 16, HALF), BF16),
            pltpu.VMEM((rows, 2 * HALF), BF16),
            pltpu.VMEM((2, Z, 2, 4, 2, 16, HALF), BF16),
            pltpu.VMEM((Z, 2, 4, 2, 16, HALF), BF16),
            pltpu.VMEM((16, HALF), F32),
            pltpu.VMEM((2, 8, HALF), F32),
            pltpu.VMEM((16, HALF), BF16),
            *ring(hz, 2, 2),
            *ring(hz, 4),
            pltpu.VMEM((hz, 2, 2, 16, HALF), BF16),
            pltpu.VMEM((hz, 4, 16, HALF), BF16),
            pltpu.VMEM((3, hz, 16, HALF), BF16),
            pltpu.VMEM((3, hz, 16, HALF), BF16),
            pltpu.VMEM((Z, 16, HALF), BF16),
            pltpu.VMEM((Z, 16, HALF), BF16),
            pltpu.VMEM((2, 8, HALF), F32),
            pltpu.VMEM((1, Z * 16), F32),
            pltpu.VMEM((Z, 1, Z * 16), F32),
            pltpu.VMEM((Z, 128), F32),
            pltpu.VMEM((4, Z, 128), F32),
            pltpu.VMEM((Z, 128), F32),
            pltpu.SemaphoreType.REGULAR((2,)),
            dma((9,)),
            dma((4,)),
            dma((8,)),
            dma((10,)),
            dma((D // WIDE,)),
            dma((16,)), dma((8,)),
        ],
        compiler_params=pltpu.CompilerParams(
            collective_id=0, has_side_effects=True, vmem_limit_bytes=VMEM_BYTES
        ),
    )(seq_counts, tokens, key_grad, w_codes, w_scales, gain.reshape(D // 128, 128))
    gains = jax.ShapeDtypeStruct((D // 128, 128), F32)
    kept = [jax.ShapeDtypeStruct(o.shape, o.dtype) for o in outs]
    keys, tig, wg, gg = pl.pallas_call(
        functools.partial(keep, inverse),
        out_shape=(*kept[:3], gains),
        in_specs=[hbm] * 5,
        out_specs=(hbm,) * 4,
        scratch_shapes=[pltpu.VMEM(o.shape, o.dtype) for o in (*kept, gains, gains)] + [dma((12,)), dma((11,))],
        compiler_params=pltpu.CompilerParams(vmem_limit_bytes=VMEM_BYTES),
    )(*outs, gain.reshape(D // 128, 128))
    return keys, tig, wg, gg.reshape(D)


def solution(mesh):
    return jax.shard_map(
        local,
        mesh=mesh,
        in_specs=(
            P(("node", "local"), None),
            P(),
            P(None, ("node", "local"), None),
            P(None, ("node", "local")),
            P(("node", "local")),
            P(("node", "local"), None),
        ),
        out_specs=(
            P(("node", "local"), None),
            P(("node", "local"), None),
            P(("node", "local"), None),
            P(),
        ),
        check_vma=False,
    )
```

```python
import functools
import math

import jax
import jax.numpy as jnp
from jax import lax
from jax.experimental import pallas as pl
from jax.experimental.pallas import tpu as pltpu
from jax.sharding import PartitionSpec as P

SEQ_LEN = 64
HALF = 256
WIDE = 1024
MESH = pl.DeviceIdType.MESH
F32 = jnp.float32
BF16 = jnp.bfloat16
ALL = slice(None)
VMEM_BYTES = 63 << 20


def copy(src, dst, send, recv, dev):
    return pltpu.make_async_remote_copy(
        src_ref=src, dst_ref=dst, send_sem=send, recv_sem=recv, device_id=dev, device_id_type=MESH
    )


def settle(ref, send=None, recv=None, dev=None):
    d = copy(ref, ref, send if recv is None else recv, recv if send is None else send, dev)
    if recv is None:
        d.wait_send()
    else:
        d.wait_recv()


class RingSum:
    def __init__(self, ref, at, first, n, bufs, sems, plus, minus):
        self.ref, self.at, self.first, self.n, self.h = ref, at, first, n, n // 2
        self.a, self.b, self.lr = bufs
        self.send, self.recv, self.dev = *sems, plus
        h = self.h
        near, far = pl.ds(0, h), pl.ds(h, h)

        def one(i, o, part, dst, dev):
            src = ref.at[at(o, pl.ds(first + part.start, h))]
            return copy(src, dst, self.send, self.recv.at[i], dev)

        self.to_a = one(0, 2, near, self.a, plus)
        self.to_b = one(1, 2, far, self.b, minus)
        self.l0 = one(2, 1, near, self.lr.at[0, near], plus)
        self.l1 = one(2, 1, far, self.lr.at[0, far], plus)
        self.r0 = one(2, 3, near, self.lr.at[1, near], minus)
        self.r1 = one(2, 3, far, self.lr.at[1, far], minus)

    def start(self):
        for d in (self.to_a, self.to_b, self.l1, self.r0):
            d.start()

    def add(self, o, base, buf):
        def body(k, carry):
            i = self.at(o, self.first + base + k)
            self.ref[i] = (self.ref[i].astype(F32) + buf[k].astype(F32)).astype(BF16)
            return carry

        lax.fori_loop(0, self.h, body, 0)

    def forward(self):
        self.to_a.wait_recv()
        self.add(1, 0, self.a)
        self.l0.start()
        self.to_b.wait_recv()
        self.add(3, self.h, self.b)
        self.r1.start()

    def finish(self, dst, dst_first):
        settle(self.lr, recv=self.recv.at[2], dev=self.dev)

        def body(k, carry):
            own = self.ref[self.at(0, self.first + k)].astype(F32)
            total = own + self.lr[0, k].astype(F32) + self.lr[1, k].astype(F32)
            dst[dst_first + k] = total.astype(BF16)
            return carry

        lax.fori_loop(0, self.n, body, 0)

    def sent(self, like):
        settle(like, send=self.send, dev=self.dev)


class RingGather:
    def __init__(self, ref, at, first, n, sems, plus, minus):
        h = n // 2
        whole, near, far = pl.ds(first, n), pl.ds(first, h), pl.ds(first + h, h)
        self.send, self.recv, self.dev = *sems, plus
        self.opposite = ref.at[at(2, whole)]

        def one(i, o, part, dev):
            block = ref.at[at(o, part)]
            return copy(block, block, self.send, self.recv.at[i], dev)

        self.first = (one(0, 0, near, plus), one(1, 0, far, minus), one(3, 0, far, plus), one(3, 0, near, minus))
        self.relay = (one(2, 3, near, plus), one(2, 1, far, minus))
        self.recvs = (one(0, 3, near, plus), one(1, 1, far, minus))

    def start(self):
        for d in self.first:
            d.start()

    def pass_on(self, i):
        self.recvs[i].wait_recv()
        self.relay[i].start()

    def neighbours(self):
        settle(self.opposite, recv=self.recv.at[3], dev=self.dev)

    def finish(self):
        settle(self.opposite, recv=self.recv.at[2], dev=self.dev)

    def sent(self, like):
        settle(like, send=self.send, dev=self.dev)


class Sum:
    def __init__(self, ref, at, n, got, sems, devs):
        self.ref, self.at, self.n, self.got = ref, at, n, got
        self.send, self.recv, self.dev = *sems, devs[1]
        self.copies = [
            copy(ref.at[at(o, pl.ds(0, n))], got.at[o - 1], self.send, self.recv, devs[o]) for o in (2, 1, 3)
        ]

    def start(self):
        for d in self.copies:
            d.start()

    def finish(self, dst, dst_first):
        settle(self.got, recv=self.recv, dev=self.dev)

        def body(k, carry):
            total = self.ref[self.at(0, k)].astype(F32)
            for o in range(3):
                total += self.got[o, k].astype(F32)
            dst[dst_first + k] = total.astype(BF16)
            return carry

        lax.fori_loop(0, self.n, body, 0)

    def sent(self):
        settle(self.got, send=self.send, dev=self.dev)


class Gather:
    def __init__(self, block, sems, devs):
        self.send, self.recv, self.dev = *sems, devs[1]
        self.copies = [copy(block, block, self.send, self.recv, devs[o]) for o in (2, 1, 3)]

    def start(self):
        for d in self.copies:
            d.start()

    def finish(self, like):
        settle(like, recv=self.recv, dev=self.dev)

    def sent(self, like):
        settle(like, send=self.send, dev=self.dev)


def kernel(
    Z, inverse,
    cnt_hbm, tok_hbm, kg_hbm, codes_hbm, scales_hbm, gain_hbm,
    keys_hbm, tig_hbm, wg_hbm, qxr,
    cnt, tok, kg, codes, scales, gain, keys, tig, wsh, W, M, G, GR, W16, wrecv, wother,
    ya, yb, ylr, xa, xb, xlr, Sy, Sx,
    y2, x2, S3, zr, S4,
    qs, qz, qy, qyr, qx,
    met, in_s, out_s, ag_r, rs_r, cr_r, ms_s, ms_r,
):
    rows, D = tok.shape
    gtiles = D // WIDE
    gt = Z // gtiles
    hz = Z // 2
    node = lax.axis_index("node")
    loc = lax.axis_index("local")
    z, xlo = node // 2, node % 2
    y, xhi, c = loc // 4, (loc // 2) % 2, loc % 2
    x = 2 * xhi + xlo
    sib = 1 - c

    def at_z(o):
        return (((z + o) % Z) * 2 + xlo, loc)

    def far_first(i):
        k = (i + 1) // 2
        return Z // 2 + k - 2 * k * (i % 2)

    def at_y(o, core):
        return (node, ((y + o) % 4) * 4 + xhi * 2 + core)

    def at_x(o, core):
        xx = (x + o) % 4
        return (z * 2 + xx % 2, y * 4 + (xx // 2) * 2 + core)

    at_core = (node, y * 4 + xhi * 2 + sib)
    ys = [(y + o) % 4 for o in range(4)]
    xs = [((x + o) % 4) % 2 for o in range(4)]
    xh = [((x + o) % 4) // 2 for o in range(4)]

    small = ((codes_hbm, codes), (scales_hbm, scales), (gain_hbm, gain), (cnt_hbm, cnt))
    loads = [pltpu.make_async_copy(a, b, in_s.at[i]) for i, (a, b) in enumerate(small)]
    quarter = D // 4
    for i in range(4):
        part = pl.ds(i * quarter, quarter)
        loads.append(pltpu.make_async_copy(tok_hbm.at[:, part], tok.at[:, part], in_s.at[4 + i]))
    loads.append(pltpu.make_async_copy(kg_hbm, kg, in_s.at[8]))
    for d in loads:
        d.start()

    barrier = pltpu.get_barrier_semaphore()

    def greet(dev):
        pl.semaphore_signal(barrier, inc=1, device_id=dev, device_id_type=MESH)

    def hello(i, carry):
        greet((((z + far_first(i)) % Z) * 2 + xlo, y * 4 + xhi * 2 + 1))
        return carry

    lax.fori_loop(0, Z - 1, hello, 0)
    for o in (1, 2, 3):
        greet((node, ((y + o) % 4) * 4 + xhi * 2))
        greet(at_x(o, 0))

    @pl.when(c == 1)
    def _():
        greet(at_core)

    for d in loads[:3]:
        d.wait()
    chip = (node * 16 + loc) // 2
    lane = lax.broadcasted_iota(jnp.int32, (16, 128), 1)
    sub = lax.broadcasted_iota(jnp.int32, (16, 128), 0)
    grow = gain[pl.ds(chip // 8, 1), :]
    g16 = jnp.sum(jnp.where(lane == (chip % 8) * 16 + sub, grow, 0.0), axis=1, keepdims=True)
    eye = lax.broadcasted_iota(jnp.int32, (8, 8), 0) == lax.broadcasted_iota(jnp.int32, (8, 8), 1)
    sc = scales[...].astype(F32)
    for b in range(4):
        col = jnp.sum(jnp.where(eye, sc[b:b + 1, :], 0.0), axis=1, keepdims=True)
        wsh[b // 2, :, (b % 2) * 128:(b % 2 + 1) * 128] = codes[b].astype(F32) * col

    total = jnp.zeros((rows, 128), F32)
    for i in range(4):
        loads[4 + i].wait()

        def square(k, acc):
            t = tok[:, pl.ds(pl.multiple_of(i * quarter + k * 128, 128), 128)].astype(F32)
            return acc + t * t

        total = lax.fori_loop(0, quarter // 128, square, total, unroll=True)
    rs = lax.rsqrt(jnp.sum(total, axis=1, keepdims=True) / D + 1e-05)
    loads[3].wait()
    loads[8].wait()
    live = lax.broadcasted_iota(jnp.int32, (rows, 1), 0) // SEQ_LEN < cnt[0]
    M[...] = (jnp.where(live, kg[...].astype(F32), 0.0) * rs).astype(BF16)

    def core_copy(k):
        part = pl.ds(k * gt, gt)
        return copy(G.at[sib, part], GR.at[part], ms_s.at[0], cr_r.at[k], at_core)

    def grad(k, carry):
        t = tok[:, pl.ds(pl.multiple_of(k * WIDE, WIDE), WIDE)]
        g = lax.dot_general(t, M[...], (((0,), (0,)), ((), ())), preferred_element_type=F32).astype(BF16)
        for h in range(2):
            G[h, pl.ds(k * gt, gt)] = g[:, h * HALF:(h + 1) * HALF].reshape(gt, 2, 4, 2, 16, HALF)
        return carry

    def core_start(k, carry):
        core_copy(k).start()
        return carry

    lax.fori_loop(0, gtiles // 2, grad, 0)

    @pl.when(c == 0)
    def _():
        pl.semaphore_wait(barrier, 13)
        pl.semaphore_signal(met.at[0], inc=1, device_id=at_core, device_id_type=MESH)

    @pl.when(c == 1)
    def _():
        pl.semaphore_wait(met.at[0], 1)

    wx = copy(wsh, wrecv, ms_s.at[1], ms_r.at[0], at_core)
    wx.start()
    lax.fori_loop(0, gtiles // 2, core_start, 0)
    lax.fori_loop(gtiles // 2, gtiles, grad, 0)
    lax.fori_loop(gtiles // 2, gtiles, core_start, 0)

    wx.wait_recv()

    def rows16(h):
        own, other = wsh[h], wrecv[h]
        W16[0:8, :] = jnp.where(c == 0, own, other)
        W16[8:16, :] = jnp.where(c == 0, other, own)
        return (W16[...] * g16).astype(BF16)

    W[c, z, xlo, y, xhi] = rows16(c)

    def agz(o):
        zz = (z + o) % Z
        place = (z, xlo, y, xhi)
        return tuple(
            copy(src, W.at[h, *place], ms_s.at[2], ms_r.at[1], (zz * 2 + xlo, y * 4 + xhi * 2 + h))
            for h, src in ((1, W.at[1, *place]), (0, wother))
        )

    @pl.when(c == 1)
    def _():
        wother[...] = rows16(0)
        pl.semaphore_wait(barrier, 2 * (Z - 1))
        pl.semaphore_signal(met.at[1], inc=1, device_id=at_core, device_id_type=MESH)

        def agz_start(i, carry):
            for d in agz(far_first(i)):
                d.start()
            return carry

        lax.fori_loop(0, Z - 1, agz_start, 0)

    def core_add(k, carry):
        core_copy(k).wait_recv()
        part = pl.ds(k * gt, gt)
        G[c, part] = (G[c, part].astype(F32) + GR[part].astype(F32)).astype(BF16)
        return carry

    def sems(i, pair, j, n):
        return ms_s.at[i], pair.at[pl.ds(j, n)]

    devs_y = [at_y(o, c) for o in range(4)]
    devs_x = [at_x(o, c) for o in range(4)]
    low, high = pl.ds(0, hz), pl.ds(hz, hz)
    sum_y = RingSum(
        G, lambda o, p: (c, p, ALL, ys[o]), 0, hz, (ya, yb, ylr), sems(8, rs_r, 0, 3), devs_y[1], devs_y[3]
    )
    sum_x = RingSum(
        G, lambda o, p: (c, p, xs[o], ALL, xh[o]), hz, hz, (xa, xb, xlr), sems(9, rs_r, 3, 3), devs_x[1], devs_x[3]
    )
    sum_yx = Sum(Sy, lambda o, p: (p, xs[o], xh[o]), hz, x2, (ms_s.at[10], rs_r.at[6]), devs_x)
    sum_xy = Sum(Sx, lambda o, p: (p, ys[o]), hz, y2, (ms_s.at[11], rs_r.at[7]), devs_y)
    get_y = Gather(W.at[c, low, xlo, y, xhi], (ms_s.at[12], rs_r.at[8]), devs_y)
    get_x = Gather(W.at[c, high, xlo, y, xhi], (ms_s.at[13], rs_r.at[9]), devs_x)
    get_yx = RingGather(
        W, lambda o, p: (c, p, xs[o], ALL, xh[o]), 0, hz, sems(14, ag_r, 0, 4), devs_x[1], devs_x[3]
    )
    get_xy = RingGather(W, lambda o, p: (c, p, ALL, ys[o]), hz, hz, sems(15, ag_r, 4, 4), devs_y[1], devs_y[3])
    three = W.at[c, low, xlo, pl.ds(0, 3), xhi]

    near, far = pl.ds(0, hz // 2), pl.ds(hz // 2, hz // 2)
    near2, far2 = pl.ds(hz, hz // 2), pl.ds(hz + hz // 2, hz // 2)

    def hand_yx(o, part):
        block = W.at[c, part, xs[o], :, xh[o]]
        copy(block, block, ms_s.at[3], ms_r.at[2], at_core).start()

    def hand_xy(o, part):
        block = W.at[c, part, :, ys[o]]
        copy(block, block, ms_s.at[3], ms_r.at[2], at_core).start()

    lax.fori_loop(0, gtiles // 2, core_add, 0)
    sum_y.start()
    lax.fori_loop(gtiles // 2, gtiles, core_add, 0)
    sum_x.start()

    sum_y.forward()
    sum_x.forward()

    sum_y.finish(Sy, 0)
    sum_yx.start()
    sum_x.finish(Sx, 0)
    sum_xy.start()
    settle(W.at[c, pl.ds(0, Z - 1), xlo, y, xhi], recv=ms_r.at[1], dev=at_core)
    get_y.start()
    get_x.start()
    def terms(first):
        part = pl.ds(first, hz)
        wide, lanes = hz * 16, Z * 16
        q = jnp.sum(W[c, part, xlo, y, xhi].astype(F32) * S3[part].astype(F32), axis=2, keepdims=True)
        row = lax.broadcasted_iota(jnp.int32, (wide, lanes), 0) + first * 16
        diag = row == lax.broadcasted_iota(jnp.int32, (wide, lanes), 1)
        return jnp.sum(jnp.where(diag, q.reshape(wide, 1), 0.0), axis=0, keepdims=True)

    sum_yx.finish(S3, 0)
    low_terms = terms(0)
    sum_xy.finish(S3, hz)
    qs[...] = low_terms + terms(hz)

    def gqz(o, src_z):
        return copy(qs, qz.at[src_z], ms_s.at[5], ms_r.at[4], at_z(o))

    def gqz_start(i, carry):
        gqz(far_first(i), z).start()
        return carry

    @pl.when(c == 0)
    def _():
        pl.semaphore_wait(met.at[1], 1)

    lax.fori_loop(0, Z - 1, gqz_start, 0)

    get_y.finish(three)
    get_yx.start()
    hand_yx(0, low)
    get_x.finish(three)
    get_xy.start()
    hand_xy(0, high)
    def rsz(o, dst_z, src_z):
        return copy(S3.at[dst_z], zr.at[src_z], ms_s.at[4], ms_r.at[3], at_z(o))

    def rsz_start(i, carry):
        o = far_first(i)
        rsz(o, (z + o) % Z, z).start()
        return carry

    lax.fori_loop(0, Z - 1, rsz_start, 0)

    for i, o in ((0, 3), (1, 1)):
        get_yx.pass_on(i)
        hand_yx(o, (near, far)[i])
        get_xy.pass_on(i)
        hand_xy(o, (near2, far2)[i])

    get_yx.neighbours()
    hand_yx(3, far)
    hand_yx(1, near)
    get_xy.neighbours()
    hand_xy(3, far2)
    hand_xy(1, near2)

    def gqz_add(o, acc):
        src = (z + Z - o) % Z
        return acc + qz[src]

    lane = lax.broadcasted_iota(jnp.int32, (Z, Z * 16), 1)
    zrow = lax.broadcasted_iota(jnp.int32, (Z, Z * 16), 0)
    src = lax.broadcasted_iota(jnp.int32, (Z * 16, 128), 0)
    to = lax.broadcasted_iota(jnp.int32, (Z * 16, 128), 1)
    place = jnp.where((src & 15) + (y * 2 + xhi) * 16 == to, 1.0, 0.0)
    settle(qz.at[pl.ds(0, Z - 1)], recv=ms_r.at[4], dev=at_core)
    qsum = lax.fori_loop(1, Z, gqz_add, qs[...])
    spread = jnp.where((lane >= zrow * 16) & (lane < zrow * 16 + 16), qsum, 0.0)
    qy[...] = jnp.dot(spread, place, precision=lax.Precision.HIGHEST, preferred_element_type=F32)
    qys = [
        copy(qy, qyr.at[2 * o + r], ms_s.at[6], ms_r.at[6], at_y(o, sib if r else c))
        for o in range(4) for r in range(2) if o or r
    ]
    for d in qys:
        d.start()

    get_yx.finish()
    hand_yx(2, low)
    get_xy.finish()
    hand_xy(2, high)

    span = D // 2

    def project(h):
        def body(k, acc):
            t = tok[:, pl.ds(pl.multiple_of(k * span, span), span)]
            w = W[h, pl.ds(k * hz, hz)].reshape(span, HALF)
            return acc + jnp.dot(t, w, preferred_element_type=F32)

        prod = lax.fori_loop(0, 2, body, jnp.zeros((rows, HALF), F32))
        kf = jnp.where(live, prod * rs, 0.0)
        cols = pl.ds(pl.multiple_of(h * HALF, HALF), HALF)
        keys[:, cols] = kf.astype(BF16)
        return jnp.sum(kf * kg[:, cols].astype(F32), axis=1, keepdims=True)

    mean = project(c)

    def rsz_add(o, acc):
        src = (z + Z - o) % Z
        return acc + zr[src].astype(F32)

    settle(zr.at[pl.ds(0, Z - 1)], recv=ms_r.at[3], dev=at_core)
    s4 = lax.fori_loop(1, Z, rsz_add, S3[z].astype(F32))

    s4 = s4 * (g16 * inverse)
    S4[0] = s4[0:8]
    S4[1] = s4[8:16]
    columns = wg_hbm.at[:, pl.ds(pl.multiple_of(c * HALF, HALF), HALF)]
    gx = copy(S4.at[sib], columns, ms_s.at[1], ms_r.at[5], at_core)
    gx.start()
    wg_out = pltpu.make_async_copy(S4.at[c], columns, out_s.at[1])
    wg_out.start()

    settle(W.at[sib], recv=ms_r.at[2], dev=at_core)
    mean += project(sib)
    coef = rs * rs * (mean / D)
    keys_out = pltpu.make_async_copy(keys, keys_hbm, out_s.at[2])
    keys_out.start()

    settle(qyr.at[pl.ds(1, 7)], recv=ms_r.at[6], dev=at_core)
    qx[...] = sum((qyr[i] for i in range(1, 8)), qy[...])
    qxs = [copy(qx, qxr.at[o], ms_s.at[7], ms_r.at[7], at_x(o, c)) for o in (1, 2, 3)]
    for d in qxs:
        d.start()
    qx_out = pltpu.make_async_copy(qx, qxr.at[0], out_s.at[0])
    qx_out.start()

    def back(k, carry):
        cols = pl.ds(pl.multiple_of(k * span, span), span)
        d = -(tok[:, cols].astype(F32) * coef)
        for h in range(2):
            d += lax.dot_general(
                M[:, h * HALF:(h + 1) * HALF], W[h, pl.ds(k * hz, hz)].reshape(span, HALF),
                (((1,), (1,)), ((), ())), preferred_element_type=F32,
            )
        tig[:, cols] = d.astype(BF16)
        pltpu.make_async_copy(tig.at[:, cols], tig_hbm.at[:, cols], out_s.at[3]).start()
        return carry

    lax.fori_loop(0, 2, back, 0)

    wx.wait_send()
    for ref, i in (
        (G.at[sib], 0), (W.at[c], 3), (S3.at[pl.ds(0, Z - 1)], 4),
        (qz.at[pl.ds(0, Z - 1)], 5), (qyr.at[pl.ds(1, 7)], 6),
    ):
        settle(ref, send=ms_s.at[i], dev=at_core)

    @pl.when(c == 1)
    def _():
        settle(W.at[:, pl.ds(0, Z - 1), xlo, y, xhi], send=ms_s.at[2], dev=at_core)

    sum_y.sent(G.at[c, pl.ds(0, hz), :, pl.ds(0, 3)])
    sum_x.sent(G.at[c, pl.ds(0, hz), :, pl.ds(0, 3)])
    sum_yx.sent()
    sum_xy.sent()
    get_y.sent(three)
    get_x.sent(three)
    get_yx.sent(W.at[c, pl.ds(0, hz), :, pl.ds(0, 3)])
    get_xy.sent(W.at[c, pl.ds(0, hz), :, pl.ds(0, 3)])

    gx.wait_recv()
    settle(qxr.at[pl.ds(1, 3)], recv=ms_r.at[7], dev=at_core)
    gx.wait_send()
    settle(qxr.at[pl.ds(1, 3)], send=ms_s.at[7], dev=at_core)
    pltpu.make_async_copy(tig, tig_hbm, out_s.at[3]).wait()
    for d in (keys_out, wg_out, qx_out):
        d.wait()


def keep(
    inverse, keys, tig, wg, qxr, gain, keys_out, tig_out, wg_out, gg_out,
    keys_v, tig_v, wg_v, qxr_v, gain_v, gg_v, in_s, out_s,
):
    loads = [pltpu.make_async_copy(a, v, in_s.at[i]) for i, (a, v) in enumerate(((qxr, qxr_v), (gain, gain_v)))]
    step = tig.shape[0] // 8
    moves = []
    for i in range(8):
        part = pl.ds(i * step, step)
        moves.append((tig.at[part], tig_v.at[part], tig_out.at[part]))
    moves += [(keys, keys_v, keys_out), (wg, wg_v, wg_out)]
    reads = [pltpu.make_async_copy(a, v, in_s.at[2 + i]) for i, (a, v, _) in enumerate(moves)]
    writes = [pltpu.make_async_copy(v, b, out_s.at[i]) for i, (_, v, b) in enumerate(moves)]
    for d in loads + reads:
        d.start()
    for r, w in zip(reads[:4], writes[:4]):
        r.wait()
        w.start()
    for d in loads:
        d.wait()
    Z = qxr_v.shape[1]
    xlo = lax.axis_index("node") % 2
    same = qxr_v[0] + qxr_v[2]
    next_x = qxr_v[1] + qxr_v[3]
    row = lax.broadcasted_iota(jnp.int32, (2 * Z, 2 * Z), 0)
    col = lax.broadcasted_iota(jnp.int32, (2 * Z, 2 * Z), 1)
    order = jnp.where(row == jnp.where(col < Z, 2 * col + xlo, 2 * (col - Z) + 1 - xlo), 1.0, 0.0)
    total = jnp.dot(
        order, jnp.concatenate([same, next_x], axis=0),
        precision=lax.Precision.HIGHEST, preferred_element_type=F32,
    )
    gg_v[...] = total * inverse / gain_v[...]
    gg_write = pltpu.make_async_copy(gg_v, gg_out, out_s.at[len(moves)])
    gg_write.start()
    for r, w in zip(reads[4:], writes[4:]):
        r.wait()
        w.start()
    for w in writes:
        w.wait()
    gg_write.wait()


def local(tokens, gain, w_codes, w_scales, seq_counts, key_grad):
    rows, D = tokens.shape
    node_count = lax.axis_size("node")
    local_count = lax.axis_size("local")
    Z = node_count // 2
    inverse = 1.0 / math.sqrt(rows * node_count * local_count)
    hbm = pl.BlockSpec(memory_space=pl.ANY)
    dma = pltpu.SemaphoreType.DMA
    hz = Z // 2

    def ring(n, *inner):
        return [pltpu.VMEM((*m, *inner, 16, HALF), BF16) for m in ((n // 2,), (n // 2,), (2, n))]

    outs = pl.pallas_call(
        functools.partial(kernel, Z, inverse),
        out_shape=(
            jax.ShapeDtypeStruct((rows, 2 * HALF), BF16),
            jax.ShapeDtypeStruct((rows, D), BF16),
            jax.ShapeDtypeStruct((8, 2 * HALF), F32),
            jax.ShapeDtypeStruct((4, Z, 128), F32),
        ),
        in_specs=[pl.BlockSpec(memory_space=pltpu.HBM)] + [hbm] * 5,
        out_specs=(hbm,) * 4,
        scratch_shapes=[
            pltpu.SMEM((1,), jnp.int32),
            pltpu.VMEM((rows, D), BF16),
            pltpu.VMEM((rows, 2 * HALF), BF16),
            pltpu.VMEM(w_codes.shape, BF16),
            pltpu.VMEM(w_scales.shape, BF16),
            pltpu.VMEM((D // 128, 128), F32),
            pltpu.VMEM((rows, 2 * HALF), BF16),
            pltpu.VMEM((rows, D), BF16),
            pltpu.VMEM((2, 8, HALF), F32),
            pltpu.VMEM((2, Z, 2, 4, 2, 16, HALF), BF16),
            pltpu.VMEM((rows, 2 * HALF), BF16),
            pltpu.VMEM((2, Z, 2, 4, 2, 16, HALF), BF16),
            pltpu.VMEM((Z, 2, 4, 2, 16, HALF), BF16),
            pltpu.VMEM((16, HALF), F32),
            pltpu.VMEM((2, 8, HALF), F32),
            pltpu.VMEM((16, HALF), BF16),
            *ring(hz, 2, 2),
            *ring(hz, 4),
            pltpu.VMEM((hz, 2, 2, 16, HALF), BF16),
            pltpu.VMEM((hz, 4, 16, HALF), BF16),
            pltpu.VMEM((3, hz, 16, HALF), BF16),
            pltpu.VMEM((3, hz, 16, HALF), BF16),
            pltpu.VMEM((Z, 16, HALF), BF16),
            pltpu.VMEM((Z, 16, HALF), BF16),
            pltpu.VMEM((2, 8, HALF), F32),
            pltpu.VMEM((1, Z * 16), F32),
            pltpu.VMEM((Z, 1, Z * 16), F32),
            pltpu.VMEM((Z, 128), F32),
            pltpu.VMEM((8, Z, 128), F32),
            pltpu.VMEM((Z, 128), F32),
            pltpu.SemaphoreType.REGULAR((2,)),
            dma((9,)),
            dma((4,)),
            dma((8,)),
            dma((10,)),
            dma((D // WIDE,)),
            dma((16,)), dma((8,)),
        ],
        compiler_params=pltpu.CompilerParams(
            collective_id=0, has_side_effects=True, vmem_limit_bytes=VMEM_BYTES
        ),
    )(seq_counts, tokens, key_grad, w_codes, w_scales, gain.reshape(D // 128, 128))
    gains = jax.ShapeDtypeStruct((D // 128, 128), F32)
    kept = [jax.ShapeDtypeStruct(o.shape, o.dtype) for o in outs]
    keys, tig, wg, gg = pl.pallas_call(
        functools.partial(keep, inverse),
        out_shape=(*kept[:3], gains),
        in_specs=[hbm] * 5,
        out_specs=(hbm,) * 4,
        scratch_shapes=[pltpu.VMEM(o.shape, o.dtype) for o in (*kept, gains, gains)] + [dma((12,)), dma((11,))],
        compiler_params=pltpu.CompilerParams(vmem_limit_bytes=VMEM_BYTES),
    )(*outs, gain.reshape(D // 128, 128))
    return keys, tig, wg, gg.reshape(D)


def solution(mesh):
    return jax.shard_map(
        local,
        mesh=mesh,
        in_specs=(
            P(("node", "local"), None),
            P(),
            P(None, ("node", "local"), None),
            P(None, ("node", "local")),
            P(("node", "local")),
            P(("node", "local"), None),
        ),
        out_specs=(
            P(("node", "local"), None),
            P(("node", "local"), None),
            P(("node", "local"), None),
            P(),
        ),
        check_vma=False,
    )
```

```python
import functools
import math

import jax
import jax.numpy as jnp
from jax import lax
from jax.experimental import pallas as pl
from jax.experimental.pallas import tpu as pltpu
from jax.sharding import PartitionSpec as P

SEQ_LEN = 64
HALF = 256
WIDE = 1024
MESH = pl.DeviceIdType.MESH
F32 = jnp.float32
BF16 = jnp.bfloat16
ALL = slice(None)
VMEM_BYTES = 63 << 20


def copy(src, dst, send, recv, dev):
    return pltpu.make_async_remote_copy(
        src_ref=src, dst_ref=dst, send_sem=send, recv_sem=recv, device_id=dev, device_id_type=MESH
    )


def settle(ref, send=None, recv=None, dev=None):
    d = copy(ref, ref, send if recv is None else recv, recv if send is None else send, dev)
    if recv is None:
        d.wait_send()
    else:
        d.wait_recv()


class RingSum:
    def __init__(self, ref, at, first, n, bufs, sems, plus, minus):
        self.ref, self.at, self.first, self.n, self.h = ref, at, first, n, n // 2
        self.a, self.b, self.lr = bufs
        self.send, self.recv, self.dev = *sems, plus
        h = self.h
        near, far = pl.ds(0, h), pl.ds(h, h)

        def one(i, o, part, dst, dev):
            src = ref.at[at(o, pl.ds(first + part.start, h))]
            return copy(src, dst, self.send, self.recv.at[i], dev)

        self.to_a = one(0, 2, near, self.a, plus)
        self.to_b = one(1, 2, far, self.b, minus)
        self.l0 = one(2, 1, near, self.lr.at[0, near], plus)
        self.l1 = one(2, 1, far, self.lr.at[0, far], plus)
        self.r0 = one(2, 3, near, self.lr.at[1, near], minus)
        self.r1 = one(2, 3, far, self.lr.at[1, far], minus)

    def start_near(self):
        self.to_a.start()
        self.r0.start()

    def start_far(self):
        self.to_b.start()
        self.l1.start()

    def add(self, o, base, buf):
        def body(k, carry):
            i = self.at(o, self.first + base + k)
            self.ref[i] = (self.ref[i].astype(F32) + buf[k].astype(F32)).astype(BF16)
            return carry

        lax.fori_loop(0, self.h, body, 0)

    def forward(self):
        self.to_a.wait_recv()
        self.add(1, 0, self.a)
        self.l0.start()
        self.to_b.wait_recv()
        self.add(3, self.h, self.b)
        self.r1.start()

    def finish(self, dst, dst_first):
        settle(self.lr, recv=self.recv.at[2], dev=self.dev)

        def body(k, carry):
            own = self.ref[self.at(0, self.first + k)].astype(F32)
            total = own + self.lr[0, k].astype(F32) + self.lr[1, k].astype(F32)
            dst[dst_first + k] = total.astype(BF16)
            return carry

        lax.fori_loop(0, self.n, body, 0)

    def sent(self, like):
        settle(like, send=self.send, dev=self.dev)


class RingGather:
    def __init__(self, ref, at, first, n, sems, plus, minus):
        h = n // 2
        whole, near, far = pl.ds(first, n), pl.ds(first, h), pl.ds(first + h, h)
        self.send, self.recv, self.dev = *sems, plus
        self.opposite = ref.at[at(2, whole)]

        def one(i, o, part, dev):
            block = ref.at[at(o, part)]
            return copy(block, block, self.send, self.recv.at[i], dev)

        self.first = (one(0, 0, near, plus), one(1, 0, far, minus), one(3, 0, far, plus), one(3, 0, near, minus))
        self.relay = (one(2, 3, near, plus), one(2, 1, far, minus))
        self.recvs = (one(0, 3, near, plus), one(1, 1, far, minus))

    def start(self):
        for d in self.first:
            d.start()

    def pass_on(self, i):
        self.recvs[i].wait_recv()
        self.relay[i].start()

    def neighbours(self):
        settle(self.opposite, recv=self.recv.at[3], dev=self.dev)

    def finish(self):
        settle(self.opposite, recv=self.recv.at[2], dev=self.dev)

    def sent(self, like):
        settle(like, send=self.send, dev=self.dev)


class Sum:
    def __init__(self, ref, at, n, got, sems, devs):
        self.ref, self.at, self.n, self.got = ref, at, n, got
        self.send, self.recv, self.dev = *sems, devs[1]
        self.copies = [
            copy(ref.at[at(o, pl.ds(0, n))], got.at[o - 1], self.send, self.recv, devs[o]) for o in (2, 1, 3)
        ]

    def start(self):
        for d in self.copies:
            d.start()

    def finish(self, dst, dst_first):
        settle(self.got, recv=self.recv, dev=self.dev)

        def body(k, carry):
            total = self.ref[self.at(0, k)].astype(F32)
            for o in range(3):
                total += self.got[o, k].astype(F32)
            dst[dst_first + k] = total.astype(BF16)
            return carry

        lax.fori_loop(0, self.n, body, 0)

    def sent(self):
        settle(self.got, send=self.send, dev=self.dev)


class Gather:
    def __init__(self, block, sems, devs):
        self.send, self.recv, self.dev = *sems, devs[1]
        self.copies = [copy(block, block, self.send, self.recv, devs[o]) for o in (2, 1, 3)]

    def start(self):
        for d in self.copies:
            d.start()

    def finish(self, like):
        settle(like, recv=self.recv, dev=self.dev)

    def sent(self, like):
        settle(like, send=self.send, dev=self.dev)


def kernel(
    Z, inverse,
    cnt_hbm, tok_hbm, kg_hbm, codes_hbm, scales_hbm, gain_hbm,
    keys_hbm, tig_hbm, wg_hbm, qxr,
    cnt, tok, kg, codes, scales, gain, keys, tig, wsh, W, M, G, GR, W16, wrecv, wother,
    ya, yb, ylr, xa, xb, xlr, Sy, Sx,
    y2, x2, S3, zr, S4,
    qs, qz, qy, qyr, qx,
    met, in_s, out_s, ag_r, rs_r, cr_r, ms_s, ms_r,
):
    rows, D = tok.shape
    gtiles = D // WIDE
    gt = Z // gtiles
    hz = Z // 2
    node = lax.axis_index("node")
    loc = lax.axis_index("local")
    z, xlo = node // 2, node % 2
    y, xhi, c = loc // 4, (loc // 2) % 2, loc % 2
    x = 2 * xhi + xlo
    sib = 1 - c

    def at_z(o):
        return (((z + o) % Z) * 2 + xlo, loc)

    def far_first(i):
        k = (i + 1) // 2
        return Z // 2 + k - 2 * k * (i % 2)

    def at_y(o, core):
        return (node, ((y + o) % 4) * 4 + xhi * 2 + core)

    def at_x(o, core):
        xx = (x + o) % 4
        return (z * 2 + xx % 2, y * 4 + (xx // 2) * 2 + core)

    at_core = (node, y * 4 + xhi * 2 + sib)
    ys = [(y + o) % 4 for o in range(4)]
    xs = [((x + o) % 4) % 2 for o in range(4)]
    xh = [((x + o) % 4) // 2 for o in range(4)]

    small = ((codes_hbm, codes), (scales_hbm, scales), (gain_hbm, gain), (cnt_hbm, cnt))
    loads = [pltpu.make_async_copy(a, b, in_s.at[i]) for i, (a, b) in enumerate(small)]
    quarter = D // 4
    for i in range(4):
        part = pl.ds(i * quarter, quarter)
        loads.append(pltpu.make_async_copy(tok_hbm.at[:, part], tok.at[:, part], in_s.at[4 + i]))
    loads.append(pltpu.make_async_copy(kg_hbm, kg, in_s.at[8]))
    for d in loads:
        d.start()

    barrier = pltpu.get_barrier_semaphore()

    def greet(dev):
        pl.semaphore_signal(barrier, inc=1, device_id=dev, device_id_type=MESH)

    def hello(i, carry):
        greet((((z + far_first(i)) % Z) * 2 + xlo, y * 4 + xhi * 2 + 1))
        return carry

    lax.fori_loop(0, Z - 1, hello, 0)
    for o in (1, 2, 3):
        greet((node, ((y + o) % 4) * 4 + xhi * 2))
        greet(at_x(o, 0))

    @pl.when(c == 1)
    def _():
        greet(at_core)

    for d in loads[:3]:
        d.wait()
    chip = (node * 16 + loc) // 2
    lane = lax.broadcasted_iota(jnp.int32, (16, 128), 1)
    sub = lax.broadcasted_iota(jnp.int32, (16, 128), 0)
    grow = gain[pl.ds(chip // 8, 1), :]
    g16 = jnp.sum(jnp.where(lane == (chip % 8) * 16 + sub, grow, 0.0), axis=1, keepdims=True)
    eye = lax.broadcasted_iota(jnp.int32, (8, 8), 0) == lax.broadcasted_iota(jnp.int32, (8, 8), 1)
    sc = scales[...].astype(F32)
    for b in range(4):
        col = jnp.sum(jnp.where(eye, sc[b:b + 1, :], 0.0), axis=1, keepdims=True)
        wsh[b // 2, :, (b % 2) * 128:(b % 2 + 1) * 128] = codes[b].astype(F32) * col

    total = jnp.zeros((rows, 128), F32)
    for i in range(4):
        loads[4 + i].wait()

        def square(k, acc):
            t = tok[:, pl.ds(pl.multiple_of(i * quarter + k * 128, 128), 128)].astype(F32)
            return acc + t * t

        total = lax.fori_loop(0, quarter // 128, square, total, unroll=True)
    rs = lax.rsqrt(jnp.sum(total, axis=1, keepdims=True) / D + 1e-05)
    loads[3].wait()
    loads[8].wait()
    live = lax.broadcasted_iota(jnp.int32, (rows, 1), 0) // SEQ_LEN < cnt[0]
    M[...] = (jnp.where(live, kg[...].astype(F32), 0.0) * rs).astype(BF16)

    def core_copy(k):
        part = pl.ds(k * gt, gt)
        return copy(G.at[sib, part], GR.at[part], ms_s.at[0], cr_r.at[k], at_core)

    def grad(k, carry):
        t = tok[:, pl.ds(pl.multiple_of(k * WIDE, WIDE), WIDE)]
        g = lax.dot_general(t, M[...], (((0,), (0,)), ((), ())), preferred_element_type=F32).astype(BF16)
        for h in range(2):
            G[h, pl.ds(k * gt, gt)] = g[:, h * HALF:(h + 1) * HALF].reshape(gt, 2, 4, 2, 16, HALF)
        return carry

    def core_start(k, carry):
        core_copy(k).start()
        return carry

    lax.fori_loop(0, gtiles // 2, grad, 0)

    @pl.when(c == 0)
    def _():
        pl.semaphore_wait(barrier, 13)
        pl.semaphore_signal(met.at[0], inc=1, device_id=at_core, device_id_type=MESH)

    @pl.when(c == 1)
    def _():
        pl.semaphore_wait(met.at[0], 1)

    wx = copy(wsh, wrecv, ms_s.at[1], ms_r.at[0], at_core)
    wx.start()
    lax.fori_loop(0, gtiles // 2, core_start, 0)
    lax.fori_loop(gtiles // 2, gtiles, grad, 0)
    lax.fori_loop(gtiles // 2, gtiles, core_start, 0)

    wx.wait_recv()

    def rows16(h):
        own, other = wsh[h], wrecv[h]
        W16[0:8, :] = jnp.where(c == 0, own, other)
        W16[8:16, :] = jnp.where(c == 0, other, own)
        return (W16[...] * g16).astype(BF16)

    W[c, z, xlo, y, xhi] = rows16(c)

    def agz(o):
        zz = (z + o) % Z
        place = (z, xlo, y, xhi)
        return tuple(
            copy(src, W.at[h, *place], ms_s.at[2], ms_r.at[1], (zz * 2 + xlo, y * 4 + xhi * 2 + h))
            for h, src in ((1, W.at[1, *place]), (0, wother))
        )

    @pl.when(c == 1)
    def _():
        wother[...] = rows16(0)
        pl.semaphore_wait(barrier, 2 * (Z - 1))
        pl.semaphore_signal(met.at[1], inc=1, device_id=at_core, device_id_type=MESH)

        def agz_start(i, carry):
            for d in agz(far_first(i)):
                d.start()
            return carry

        lax.fori_loop(0, Z - 1, agz_start, 0)

    def core_add(k, carry):
        core_copy(k).wait_recv()
        part = pl.ds(k * gt, gt)
        G[c, part] = (G[c, part].astype(F32) + GR[part].astype(F32)).astype(BF16)
        return carry

    def sems(i, pair, j, n):
        return ms_s.at[i], pair.at[pl.ds(j, n)]

    devs_y = [at_y(o, c) for o in range(4)]
    devs_x = [at_x(o, c) for o in range(4)]
    low, high = pl.ds(0, hz), pl.ds(hz, hz)
    sum_y = RingSum(
        G, lambda o, p: (c, p, ALL, ys[o]), 0, hz, (ya, yb, ylr), sems(8, rs_r, 0, 3), devs_y[1], devs_y[3]
    )
    sum_x = RingSum(
        G, lambda o, p: (c, p, xs[o], ALL, xh[o]), hz, hz, (xa, xb, xlr), sems(9, rs_r, 3, 3), devs_x[1], devs_x[3]
    )
    sum_yx = Sum(Sy, lambda o, p: (p, xs[o], xh[o]), hz, x2, (ms_s.at[10], rs_r.at[6]), devs_x)
    sum_xy = Sum(Sx, lambda o, p: (p, ys[o]), hz, y2, (ms_s.at[11], rs_r.at[7]), devs_y)
    get_y = Gather(W.at[c, low, xlo, y, xhi], (ms_s.at[12], rs_r.at[8]), devs_y)
    get_x = Gather(W.at[c, high, xlo, y, xhi], (ms_s.at[13], rs_r.at[9]), devs_x)
    get_yx = RingGather(
        W, lambda o, p: (c, p, xs[o], ALL, xh[o]), 0, hz, sems(14, ag_r, 0, 4), devs_x[1], devs_x[3]
    )
    get_xy = RingGather(W, lambda o, p: (c, p, ALL, ys[o]), hz, hz, sems(15, ag_r, 4, 4), devs_y[1], devs_y[3])
    three = W.at[c, low, xlo, pl.ds(0, 3), xhi]

    near, far = pl.ds(0, hz // 2), pl.ds(hz // 2, hz // 2)
    near2, far2 = pl.ds(hz, hz // 2), pl.ds(hz + hz // 2, hz // 2)

    def hand_yx(o, part):
        block = W.at[c, part, xs[o], :, xh[o]]
        copy(block, block, ms_s.at[3], ms_r.at[2], at_core).start()

    def hand_xy(o, part):
        block = W.at[c, part, :, ys[o]]
        copy(block, block, ms_s.at[3], ms_r.at[2], at_core).start()

    core_add(0, 0)
    sum_y.start_near()
    core_add(1, 0)
    sum_y.start_far()
    core_add(2, 0)
    sum_x.start_near()
    core_add(3, 0)
    sum_x.start_far()

    sum_y.forward()
    sum_x.forward()

    sum_y.finish(Sy, 0)
    sum_yx.start()
    sum_x.finish(Sx, 0)
    sum_xy.start()
    settle(W.at[c, pl.ds(0, Z - 1), xlo, y, xhi], recv=ms_r.at[1], dev=at_core)
    get_y.start()
    get_x.start()
    def terms(first):
        part = pl.ds(first, hz)
        wide, lanes = hz * 16, Z * 16
        q = jnp.sum(W[c, part, xlo, y, xhi].astype(F32) * S3[part].astype(F32), axis=2, keepdims=True)
        row = lax.broadcasted_iota(jnp.int32, (wide, lanes), 0) + first * 16
        diag = row == lax.broadcasted_iota(jnp.int32, (wide, lanes), 1)
        return jnp.sum(jnp.where(diag, q.reshape(wide, 1), 0.0), axis=0, keepdims=True)

    sum_yx.finish(S3, 0)
    low_terms = terms(0)
    sum_xy.finish(S3, hz)
    qs[...] = low_terms + terms(hz)

    def gqz(o, src_z):
        return copy(qs, qz.at[src_z], ms_s.at[5], ms_r.at[4], at_z(o))

    def gqz_start(i, carry):
        gqz(far_first(i), z).start()
        return carry

    @pl.when(c == 0)
    def _():
        pl.semaphore_wait(met.at[1], 1)

    lax.fori_loop(0, Z - 1, gqz_start, 0)

    get_y.finish(three)
    get_yx.start()
    hand_yx(0, low)
    get_x.finish(three)
    get_xy.start()
    hand_xy(0, high)
    def rsz(o, dst_z, src_z):
        return copy(S3.at[dst_z], zr.at[src_z], ms_s.at[4], ms_r.at[3], at_z(o))

    def rsz_start(i, carry):
        o = far_first(i)
        rsz(o, (z + o) % Z, z).start()
        return carry

    lax.fori_loop(0, Z - 1, rsz_start, 0)

    for i, o in ((0, 3), (1, 1)):
        get_yx.pass_on(i)
        hand_yx(o, (near, far)[i])
        get_xy.pass_on(i)
        hand_xy(o, (near2, far2)[i])

    get_yx.neighbours()
    hand_yx(3, far)
    hand_yx(1, near)
    get_xy.neighbours()
    hand_xy(3, far2)
    hand_xy(1, near2)

    def gqz_add(o, acc):
        src = (z + Z - o) % Z
        return acc + qz[src]

    lane = lax.broadcasted_iota(jnp.int32, (Z, Z * 16), 1)
    zrow = lax.broadcasted_iota(jnp.int32, (Z, Z * 16), 0)
    src = lax.broadcasted_iota(jnp.int32, (Z * 16, 128), 0)
    to = lax.broadcasted_iota(jnp.int32, (Z * 16, 128), 1)
    place = jnp.where((src & 15) + (y * 2 + xhi) * 16 == to, 1.0, 0.0)
    settle(qz.at[pl.ds(0, Z - 1)], recv=ms_r.at[4], dev=at_core)
    qsum = lax.fori_loop(1, Z, gqz_add, qs[...])
    spread = jnp.where((lane >= zrow * 16) & (lane < zrow * 16 + 16), qsum, 0.0)
    qy[...] = jnp.dot(spread, place, precision=lax.Precision.HIGHEST, preferred_element_type=F32)
    qys = [
        copy(qy, qyr.at[2 * o + r], ms_s.at[6], ms_r.at[6], at_y(o, sib if r else c))
        for o in range(4) for r in range(2) if o or r
    ]
    for d in qys:
        d.start()

    get_yx.finish()
    hand_yx(2, low)
    get_xy.finish()
    hand_xy(2, high)

    span = D // 2

    def project(h):
        def body(k, acc):
            t = tok[:, pl.ds(pl.multiple_of(k * span, span), span)]
            w = W[h, pl.ds(k * hz, hz)].reshape(span, HALF)
            return acc + jnp.dot(t, w, preferred_element_type=F32)

        prod = lax.fori_loop(0, 2, body, jnp.zeros((rows, HALF), F32))
        kf = jnp.where(live, prod * rs, 0.0)
        cols = pl.ds(pl.multiple_of(h * HALF, HALF), HALF)
        keys[:, cols] = kf.astype(BF16)
        return jnp.sum(kf * kg[:, cols].astype(F32), axis=1, keepdims=True)

    mean = project(c)

    def rsz_add(o, acc):
        src = (z + Z - o) % Z
        return acc + zr[src].astype(F32)

    settle(zr.at[pl.ds(0, Z - 1)], recv=ms_r.at[3], dev=at_core)
    s4 = lax.fori_loop(1, Z, rsz_add, S3[z].astype(F32))

    s4 = s4 * (g16 * inverse)
    S4[0] = s4[0:8]
    S4[1] = s4[8:16]
    columns = wg_hbm.at[:, pl.ds(pl.multiple_of(c * HALF, HALF), HALF)]
    gx = copy(S4.at[sib], columns, ms_s.at[1], ms_r.at[5], at_core)
    gx.start()
    wg_out = pltpu.make_async_copy(S4.at[c], columns, out_s.at[1])
    wg_out.start()

    settle(W.at[sib], recv=ms_r.at[2], dev=at_core)
    mean += project(sib)
    coef = rs * rs * (mean / D)
    keys_out = pltpu.make_async_copy(keys, keys_hbm, out_s.at[2])
    keys_out.start()

    settle(qyr.at[pl.ds(1, 7)], recv=ms_r.at[6], dev=at_core)
    qx[...] = sum((qyr[i] for i in range(1, 8)), qy[...])
    qxs = [copy(qx, qxr.at[o], ms_s.at[7], ms_r.at[7], at_x(o, c)) for o in (1, 2, 3)]
    for d in qxs:
        d.start()
    qx_out = pltpu.make_async_copy(qx, qxr.at[0], out_s.at[0])
    qx_out.start()

    def back(k, carry):
        cols = pl.ds(pl.multiple_of(k * span, span), span)
        d = -(tok[:, cols].astype(F32) * coef)
        for h in range(2):
            d += lax.dot_general(
                M[:, h * HALF:(h + 1) * HALF], W[h, pl.ds(k * hz, hz)].reshape(span, HALF),
                (((1,), (1,)), ((), ())), preferred_element_type=F32,
            )
        tig[:, cols] = d.astype(BF16)
        pltpu.make_async_copy(tig.at[:, cols], tig_hbm.at[:, cols], out_s.at[3]).start()
        return carry

    lax.fori_loop(0, 2, back, 0)

    wx.wait_send()
    for ref, i in (
        (G.at[sib], 0), (W.at[c], 3), (S3.at[pl.ds(0, Z - 1)], 4),
        (qz.at[pl.ds(0, Z - 1)], 5), (qyr.at[pl.ds(1, 7)], 6),
    ):
        settle(ref, send=ms_s.at[i], dev=at_core)

    @pl.when(c == 1)
    def _():
        settle(W.at[:, pl.ds(0, Z - 1), xlo, y, xhi], send=ms_s.at[2], dev=at_core)

    sum_y.sent(G.at[c, pl.ds(0, hz), :, pl.ds(0, 3)])
    sum_x.sent(G.at[c, pl.ds(0, hz), :, pl.ds(0, 3)])
    sum_yx.sent()
    sum_xy.sent()
    get_y.sent(three)
    get_x.sent(three)
    get_yx.sent(W.at[c, pl.ds(0, hz), :, pl.ds(0, 3)])
    get_xy.sent(W.at[c, pl.ds(0, hz), :, pl.ds(0, 3)])

    gx.wait_recv()
    settle(qxr.at[pl.ds(1, 3)], recv=ms_r.at[7], dev=at_core)
    gx.wait_send()
    settle(qxr.at[pl.ds(1, 3)], send=ms_s.at[7], dev=at_core)
    pltpu.make_async_copy(tig, tig_hbm, out_s.at[3]).wait()
    for d in (keys_out, wg_out, qx_out):
        d.wait()


def keep(
    inverse, keys, tig, wg, qxr, gain, keys_out, tig_out, wg_out, gg_out,
    keys_v, tig_v, wg_v, qxr_v, gain_v, gg_v, in_s, out_s,
):
    loads = [pltpu.make_async_copy(a, v, in_s.at[i]) for i, (a, v) in enumerate(((qxr, qxr_v), (gain, gain_v)))]
    step = tig.shape[0] // 8
    moves = []
    for i in range(8):
        part = pl.ds(i * step, step)
        moves.append((tig.at[part], tig_v.at[part], tig_out.at[part]))
    moves += [(keys, keys_v, keys_out), (wg, wg_v, wg_out)]
    reads = [pltpu.make_async_copy(a, v, in_s.at[2 + i]) for i, (a, v, _) in enumerate(moves)]
    writes = [pltpu.make_async_copy(v, b, out_s.at[i]) for i, (_, v, b) in enumerate(moves)]
    for d in loads + reads:
        d.start()
    for r, w in zip(reads[:4], writes[:4]):
        r.wait()
        w.start()
    for d in loads:
        d.wait()
    Z = qxr_v.shape[1]
    xlo = lax.axis_index("node") % 2
    same = qxr_v[0] + qxr_v[2]
    next_x = qxr_v[1] + qxr_v[3]
    row = lax.broadcasted_iota(jnp.int32, (2 * Z, 2 * Z), 0)
    col = lax.broadcasted_iota(jnp.int32, (2 * Z, 2 * Z), 1)
    order = jnp.where(row == jnp.where(col < Z, 2 * col + xlo, 2 * (col - Z) + 1 - xlo), 1.0, 0.0)
    total = jnp.dot(
        order, jnp.concatenate([same, next_x], axis=0),
        precision=lax.Precision.HIGHEST, preferred_element_type=F32,
    )
    gg_v[...] = total * inverse / gain_v[...]
    gg_write = pltpu.make_async_copy(gg_v, gg_out, out_s.at[len(moves)])
    gg_write.start()
    for r, w in zip(reads[4:], writes[4:]):
        r.wait()
        w.start()
    for w in writes:
        w.wait()
    gg_write.wait()


def local(tokens, gain, w_codes, w_scales, seq_counts, key_grad):
    rows, D = tokens.shape
    node_count = lax.axis_size("node")
    local_count = lax.axis_size("local")
    Z = node_count // 2
    inverse = 1.0 / math.sqrt(rows * node_count * local_count)
    hbm = pl.BlockSpec(memory_space=pl.ANY)
    dma = pltpu.SemaphoreType.DMA
    hz = Z // 2

    def ring(n, *inner):
        return [pltpu.VMEM((*m, *inner, 16, HALF), BF16) for m in ((n // 2,), (n // 2,), (2, n))]

    outs = pl.pallas_call(
        functools.partial(kernel, Z, inverse),
        out_shape=(
            jax.ShapeDtypeStruct((rows, 2 * HALF), BF16),
            jax.ShapeDtypeStruct((rows, D), BF16),
            jax.ShapeDtypeStruct((8, 2 * HALF), F32),
            jax.ShapeDtypeStruct((4, Z, 128), F32),
        ),
        in_specs=[pl.BlockSpec(memory_space=pltpu.HBM)] + [hbm] * 5,
        out_specs=(hbm,) * 4,
        scratch_shapes=[
            pltpu.SMEM((1,), jnp.int32),
            pltpu.VMEM((rows, D), BF16),
            pltpu.VMEM((rows, 2 * HALF), BF16),
            pltpu.VMEM(w_codes.shape, BF16),
            pltpu.VMEM(w_scales.shape, BF16),
            pltpu.VMEM((D // 128, 128), F32),
            pltpu.VMEM((rows, 2 * HALF), BF16),
            pltpu.VMEM((rows, D), BF16),
            pltpu.VMEM((2, 8, HALF), F32),
            pltpu.VMEM((2, Z, 2, 4, 2, 16, HALF), BF16),
            pltpu.VMEM((rows, 2 * HALF), BF16),
            pltpu.VMEM((2, Z, 2, 4, 2, 16, HALF), BF16),
            pltpu.VMEM((Z, 2, 4, 2, 16, HALF), BF16),
            pltpu.VMEM((16, HALF), F32),
            pltpu.VMEM((2, 8, HALF), F32),
            pltpu.VMEM((16, HALF), BF16),
            *ring(hz, 2, 2),
            *ring(hz, 4),
            pltpu.VMEM((hz, 2, 2, 16, HALF), BF16),
            pltpu.VMEM((hz, 4, 16, HALF), BF16),
            pltpu.VMEM((3, hz, 16, HALF), BF16),
            pltpu.VMEM((3, hz, 16, HALF), BF16),
            pltpu.VMEM((Z, 16, HALF), BF16),
            pltpu.VMEM((Z, 16, HALF), BF16),
            pltpu.VMEM((2, 8, HALF), F32),
            pltpu.VMEM((1, Z * 16), F32),
            pltpu.VMEM((Z, 1, Z * 16), F32),
            pltpu.VMEM((Z, 128), F32),
            pltpu.VMEM((8, Z, 128), F32),
            pltpu.VMEM((Z, 128), F32),
            pltpu.SemaphoreType.REGULAR((2,)),
            dma((9,)),
            dma((4,)),
            dma((8,)),
            dma((10,)),
            dma((D // WIDE,)),
            dma((16,)), dma((8,)),
        ],
        compiler_params=pltpu.CompilerParams(
            collective_id=0, has_side_effects=True, vmem_limit_bytes=VMEM_BYTES
        ),
    )(seq_counts, tokens, key_grad, w_codes, w_scales, gain.reshape(D // 128, 128))
    gains = jax.ShapeDtypeStruct((D // 128, 128), F32)
    kept = [jax.ShapeDtypeStruct(o.shape, o.dtype) for o in outs]
    keys, tig, wg, gg = pl.pallas_call(
        functools.partial(keep, inverse),
        out_shape=(*kept[:3], gains),
        in_specs=[hbm] * 5,
        out_specs=(hbm,) * 4,
        scratch_shapes=[pltpu.VMEM(o.shape, o.dtype) for o in (*kept, gains, gains)] + [dma((12,)), dma((11,))],
        compiler_params=pltpu.CompilerParams(vmem_limit_bytes=VMEM_BYTES),
    )(*outs, gain.reshape(D // 128, 128))
    return keys, tig, wg, gg.reshape(D)


def solution(mesh):
    return jax.shard_map(
        local,
        mesh=mesh,
        in_specs=(
            P(("node", "local"), None),
            P(),
            P(None, ("node", "local"), None),
            P(None, ("node", "local")),
            P(("node", "local")),
            P(("node", "local"), None),
        ),
        out_specs=(
            P(("node", "local"), None),
            P(("node", "local"), None),
            P(("node", "local"), None),
            P(),
        ),
        check_vma=False,
    )
```
